32 devices in a mesh: section: 2 (over x), dp: 4 (over z), tensor: 4 (over y, core).
Axes of the slice: x: 2, y: 2, z: 4, core: 2. Of those that a mesh axis runs over, the one named last changes fastest.
Arguments:
- embedded: bfloat16 [8192, 768], P('dp'), may hold values from -6 to 6
- segment: int32 [16, 512], P('dp'), may hold values from 0 to 5, never falling along the last dimension, each value on 1 to 256 neighbouring positions
- query_key_value_weight: bfloat16 [2, 3, 768, 768], P('section', None, None, 'tensor'), may hold values from -0.21875 to 0.21875
- attention_output_weight: bfloat16 [2, 768, 768], P('section', 'tensor'), may hold values from -1.75 to 1.75
- feedforward_up_weight: bfloat16 [2, 768, 3072], P('section', None, 'tensor'), may hold values from -0.21875 to 0.21875
- feedforward_down_weight: bfloat16 [2, 3072, 768], P('section', 'tensor'), may hold values from -0.109375 to 0.109375
- adapter_down_weight: bfloat16 [2, 2, 768, 8], P('section'), may hold values from -0.21875 to 0.21875
- adapter_up_weight: bfloat16 [2, 2, 8, 768], P('section', None, None, 'tensor'), may hold values from -0.625 to 0.625
- layer_norm_gain: float32 [2, 2, 768], P('section'), may hold values from 0.5 to 1.5
- layer_norm_bias: float32 [2, 2, 768], P('section'), may hold values from -1.75 to 1.75
- cotangent: bfloat16 [8192, 768], P('dp'), may hold values from -6 to 6
Outputs:
- layer_outs: bfloat16 [2, 8192, 768], P('section', 'dp')
- in_grads: bfloat16 [2, 8192, 768], P('section', 'dp')
- grad_a: float32 [2, 2, 768, 8], P('section')
- grad_b: float32 [2, 2, 8, 768], P('section', None, None, 'tensor')
The draws below stay inside these ranges and needn't reach their ends.
Inputs may be any that keep to these rules, and one draw needn't show every extreme that they name: `segment`: within each pack the ids never fall, every id of the range occurs, each covers at most 256 rows and one covers exactly that many.
All inputs are finite; a program needn't handle non-finite values.
Results may differ from the reference program's by a relative error of at most 0.025.
Values may be sent and summed in bfloat16 or wider, within the bound.
A program may use at most 192 MiB of HBM per device.

```python
import math
import jax
import jax.numpy as jnp
import numpy as np
from jax import lax

MODEL_WIDTH = 768
HEADS = 12
HEAD_DIM = 64
FF = 3072
ADAPTER_RANK = 8
PACK_LEN = 512
LAYER_COUNT = 2
PACKS = 16
TOKENS = 8192


def shard_levels(rng, dims, cuts, low, top_value):
    def one(axis_at, parts):
        steps = jax.random.uniform(jax.random.fold_in(jax.random.fold_in(rng, 6), axis_at), (parts,), jnp.float32, low / len(cuts), top_value / len(cuts))
        return jnp.repeat(jnp.exp(steps), dims[axis_at] // parts).reshape((-1,) + (1,) * (len(dims) - axis_at - 1))

    level = one(*cuts[0])
    for cut in cuts[1:]:
        level = level * one(*cut)
    return level


def length_profile(number_of, total, most, skew):
    weights = [(1 << 20) // math.isqrt(grade ** skew) + 1 for grade in range(2, number_of + 1)]
    surplus, holding = total - most - (number_of - 1), [1] * (number_of - 1)
    while surplus > 0:
        candidates = [i for i in range(number_of - 1) if holding[i] < most]
        whole, remaining = sum([weights[i] for i in candidates]), surplus
        for i in candidates:
            more = min(most - holding[i], max(1, remaining * weights[i] // whole), surplus)
            holding[i] = holding[i] + more
            surplus = surplus - more
    return np.array([most] + holding)


def ragged_sizes(rng, amount, total, limit, lean):
    if amount == 2:
        one = jax.random.randint(rng, (), max(1, total - limit), min(limit, total - 1) + 1)
        return jnp.stack([one, total - one])
    sizes = jnp.asarray(length_profile(amount, total, limit, lean), jnp.int32)
    pairs = (amount - 1) // 2
    source_of, sink = sizes[1:1 + 2 * pairs:2], sizes[2:2 + 2 * pairs:2]
    slack = jnp.minimum(source_of - 1, limit - sink)
    moved = jax.random.randint(jax.random.fold_in(rng, 1), (pairs,), 0, 1 << 20) % (slack + 1)
    sizes = sizes.at[1:1 + 2 * pairs:2].set(source_of - moved).at[2:2 + 2 * pairs:2].set(sink + moved)
    return sizes[jax.random.permutation(jax.random.fold_in(rng, 2), amount)]


def bell_draw(rng, shape, deviation, limit, shards=(), dtype=jnp.bfloat16):
    entries = deviation * jax.random.normal(rng, shape, jnp.float32)
    if shards:
        entries = entries * shard_levels(rng, shape, shards, -0.22, 0.18)
    return jnp.clip(entries, -limit, limit).astype(dtype)


def setup_inputs(seed: int = 0) -> dict:
    seeds = jax.random.split(jax.random.key(seed), 12)
    embedded = bell_draw(seeds[0], (TOKENS, MODEL_WIDTH), 1.0, 6.0, ((0, 4),))
    segment = jax.vmap(lambda own: jnp.searchsorted(jnp.cumsum(ragged_sizes(own, 6, PACK_LEN, PACK_LEN // 2, 2)), jnp.arange(PACK_LEN), side="right"))(jax.random.split(seeds[1], PACKS)).reshape((PACKS, PACK_LEN)).astype(jnp.int32)
    query_key_value_weight = bell_draw(seeds[2], (LAYER_COUNT, 3, MODEL_WIDTH, MODEL_WIDTH), MODEL_WIDTH ** -0.5, 0.21875, ((0, 2), (3, 4)))
    attention_output_weight = bell_draw(seeds[3], (LAYER_COUNT, MODEL_WIDTH, MODEL_WIDTH), (max(MODEL_WIDTH // 64, 4)) ** -0.5, 1.75, ((0, 2), (1, 4)))
    feedforward_up_weight = bell_draw(seeds[4], (LAYER_COUNT, MODEL_WIDTH, FF), MODEL_WIDTH ** -0.5, 0.21875, ((0, 2), (2, 4)))
    feedforward_down_weight = bell_draw(seeds[5], (LAYER_COUNT, FF, MODEL_WIDTH), FF ** -0.5, 0.109375, ((0, 2), (1, 4)))
    adapter_down_weight = bell_draw(seeds[6], (LAYER_COUNT, 2, MODEL_WIDTH, ADAPTER_RANK), MODEL_WIDTH ** -0.5, 0.21875, ((0, 2),))
    adapter_up_weight = bell_draw(seeds[7], (LAYER_COUNT, 2, ADAPTER_RANK, MODEL_WIDTH), 0.1, 0.625, ((0, 2), (3, 4)))
    layer_norm_gain = jnp.clip(1.0 + 0.1 * jax.random.normal(seeds[8], (LAYER_COUNT, 2, MODEL_WIDTH), jnp.float32), 0.5, 1.5)
    layer_norm_bias = bell_draw(seeds[9], (LAYER_COUNT, 2, MODEL_WIDTH), 0.3, 1.75, ((0, 2),), jnp.float32)
    cotangent = bell_draw(seeds[10], (TOKENS, MODEL_WIDTH), 1.0, 6.0, ((0, 4),))
    return {"embedded": embedded, "segment": segment, "query_key_value_weight": query_key_value_weight, "attention_output_weight": attention_output_weight, "feedforward_up_weight": feedforward_up_weight, "feedforward_down_weight": feedforward_down_weight, "adapter_down_weight": adapter_down_weight, "adapter_up_weight": adapter_up_weight, "layer_norm_gain": layer_norm_gain, "layer_norm_bias": layer_norm_bias, "cotangent": cotangent}


@jax.custom_vjp
def low_rank_rows(v):
    return lax.optimization_barrier(v.astype(jnp.bfloat16)).astype(jnp.float32)

@jax.custom_vjp
def low_back(v):
    return v

def low_keep(v):
    return (low_rank_rows(v), None)

def low_pass(kept, grad):
    return (grad,)

def back_keep(v):
    return (v, None)

def back_low(kept, grad):
    return (low_rank_rows(grad),)
low_rank_rows.defvjp(low_keep, low_pass)
low_back.defvjp(back_keep, back_low)
highest_precision = lax.Precision.HIGHEST

def layer_norm(total, norm_gains, norm_biases):
    average = lax.optimization_barrier(jnp.mean(total, -1, keepdims=True))
    centred = total - average
    spread = lax.optimization_barrier(jnp.mean(centred * centred, -1, keepdims=True))
    return centred * lax.rsqrt(spread + 1e-05) * norm_gains + norm_biases

def attend_pack(pieces):
    queries, keys_all, values_all, segs = pieces
    same_doc = segs[:, None] == segs[None, :]
    scores = jnp.einsum('qhe,khe->hqk', queries, keys_all, precision=highest_precision) * HEAD_DIM ** (-0.5)
    scores = low_back(jnp.where(same_doc[None], scores, -1000000000.0))
    weights_soft = jax.nn.softmax(scores, axis=-1)
    return low_back(low_rank_rows(jnp.einsum('hqk,khe->qhe', low_rank_rows(weights_soft), values_all, precision=highest_precision)))

def run_layer(hidden_state, segs, parameter_tree):
    query_key_value_weight, attention_output_weight, feedforward_up_weight, feedforward_down_weight, adapter_down_weight, adapter_up_weight, norm_gains, norm_biases = parameter_tree
    row_count = hidden_state.shape[0]
    projected = jnp.einsum('td,sde->ste', hidden_state, query_key_value_weight, precision=highest_precision)
    middle_rows = low_rank_rows(jnp.einsum('qg,nga->nqa', hidden_state, adapter_down_weight, precision=highest_precision))
    adapted_rows = 2.0 * jnp.einsum('xwz,xzy->xwy', middle_rows, adapter_up_weight, precision=highest_precision)
    queries = low_back(low_rank_rows(projected[0] + adapted_rows[0]))
    keys_all = low_back(low_rank_rows(projected[1]))
    values_all = low_back(low_rank_rows(projected[2] + adapted_rows[1]))
    shaped = (segs.shape[0], segs.shape[1], HEADS, HEAD_DIM)
    context = lax.map(jax.checkpoint(attend_pack), (queries.reshape(shaped), keys_all.reshape(shaped), values_all.reshape(shaped), segs))
    context = context.reshape(row_count, MODEL_WIDTH)
    attn_out = low_back(jnp.dot(context, attention_output_weight, precision=highest_precision))
    first_out = layer_norm(hidden_state + attn_out, norm_gains[0], norm_biases[0])
    pre_act = low_back(jnp.dot(low_rank_rows(first_out), feedforward_up_weight, precision=highest_precision))
    ffn_out = low_back(jnp.dot(low_rank_rows(jax.nn.gelu(pre_act, approximate=False)), feedforward_down_weight, precision=highest_precision))
    return layer_norm(first_out + ffn_out, norm_gains[1], norm_biases[1])

def reference(embedded, segment, query_key_value_weight, attention_output_weight, feedforward_up_weight, feedforward_down_weight, adapter_down_weight, adapter_up_weight, layer_norm_gain, layer_norm_bias, cotangent):
    group_packs = 8
    group_count = PACKS // group_packs
    group_rows = group_packs * PACK_LEN
    inputs = embedded.astype(jnp.float32).reshape(group_count, group_rows, MODEL_WIDTH)
    segs_all = segment.reshape(group_count, group_packs, PACK_LEN)
    cots = cotangent.astype(jnp.float32).reshape(group_count, group_rows, MODEL_WIDTH)
    qkv_full = query_key_value_weight.astype(jnp.float32)
    out_full = attention_output_weight.astype(jnp.float32)
    up_full = feedforward_up_weight.astype(jnp.float32)
    down_full = feedforward_down_weight.astype(jnp.float32)
    adapter_down_list = adapter_down_weight.astype(jnp.float32)
    adapter_up_list = adapter_up_weight.astype(jnp.float32)
    gains_all = layer_norm_gain.astype(jnp.float32)
    biases_all = layer_norm_bias.astype(jnp.float32)

    def layer_params(level, down_now, up_now):
        return (qkv_full[level], out_full[level], up_full[level], down_full[level], down_now[level], up_now[level], gains_all[level], biases_all[level])

    def group_step(totals, pieces):
        inputs_group, segs_group, cots_group = pieces

        def forward(first_in, down_now, up_now, probe):
            out_zero = low_rank_rows(run_layer(first_in, segs_group, layer_params(0, down_now, up_now)))
            out_one = run_layer(low_back(out_zero + probe), segs_group, layer_params(1, down_now, up_now))
            return (out_zero, out_one)
        outputs, pullback = jax.vjp(forward, inputs_group, adapter_down_list, adapter_up_list, jnp.zeros_like(inputs_group))
        dfirst, ddown, dup, dprobe = pullback((jnp.zeros_like(outputs[0]), cots_group))
        return ((totals[0] + ddown, totals[1] + dup), (outputs[0], outputs[1], dfirst, dprobe))
    totals, stacked = lax.scan(group_step, (jnp.zeros_like(adapter_down_list), jnp.zeros_like(adapter_up_list)), (inputs, segs_all, cots))
    out_zero, out_one, dfirst, dprobe = stacked
    layer_outs = jnp.stack((out_zero.reshape(TOKENS, MODEL_WIDTH), out_one.reshape(TOKENS, MODEL_WIDTH))).astype(jnp.bfloat16)
    in_grads = jnp.stack((dfirst.reshape(TOKENS, MODEL_WIDTH), dprobe.reshape(TOKENS, MODEL_WIDTH))).astype(jnp.bfloat16)
    return (layer_outs, in_grads, totals[0], totals[1])
```

```python
from functools import partial

import jax
import jax.numpy as jnp
from jax import lax
from jax.experimental import pallas as pl
from jax.experimental.pallas import tpu as pltpu
from jax.sharding import PartitionSpec as P

HEAD_DIM = 64
EPS = 1e-05
VMEM_LIMIT = 60 * 2**20
F32 = jnp.float32
BF16 = jnp.bfloat16
ANY = pl.BlockSpec(memory_space=pl.ANY)
VMEM = pl.BlockSpec(memory_space=pltpu.VMEM)
SMEM = pl.BlockSpec(memory_space=pltpu.SMEM)


def nn(a, b):
    return jnp.dot(a, b, preferred_element_type=F32)


def nt(a, b):
    return lax.dot_general(a, b, (((1,), (1,)), ((), ())), preferred_element_type=F32)


def lane_mask(shape, low, high):
    lanes = lax.broadcasted_iota(jnp.int32, shape, len(shape) - 1)
    return (lanes >= low) & (lanes < high)


def normalize(total):
    average = jnp.mean(total, -1, keepdims=True)
    centred = total - average
    spread = jnp.mean(centred * centred, -1, keepdims=True)
    scaled = lax.rsqrt(spread + EPS)
    return centred * scaled, scaled


def normalize_back(normed, scaled, gains, incoming):
    weighted = incoming * gains
    return scaled * (
        weighted
        - jnp.mean(weighted, -1, keepdims=True)
        - normed * jnp.mean(weighted * normed, -1, keepdims=True)
    )


def split_copies(refs, slot, half_of, parity, sems):
    own, sib, near, far, sib_near, sib_far = refs
    pairs = [
        (own, slot(0)),
        (sib, slot(1)),
        (near, half_of(2, parity)),
        (far, half_of(2, 1 - parity)),
        (sib_near, half_of(3, parity)),
        (sib_far, half_of(3, 1 - parity)),
    ]
    return [pltpu.make_async_copy(a, b, sems.at[i]) for i, (a, b) in enumerate(pairs)]


def qkv_copies(refs, scr, parity, sems):
    half = scr.shape[2] // 2
    return split_copies(
        refs,
        lambda s: scr.at[s],
        lambda s, p: scr.at[s, :, pl.ds(p * half, half), :],
        parity,
        sems,
    )


def out_copies(refs, scr, parity, sems):
    rows = scr.shape[0] // 4
    half = rows // 2
    return split_copies(
        refs,
        lambda s: scr.at[pl.ds(s * rows, rows)],
        lambda s, p: scr.at[pl.ds(s * rows + p * half, half)],
        parity,
        sems,
    )


def up_copies(refs, scr, sems):
    wide = scr.shape[1] // 4
    half = wide // 2
    offsets = [(0, wide), (wide, wide)] + [(2 * wide + i * half, half) for i in range(4)]
    return [
        pltpu.make_async_copy(r, scr.at[:, pl.ds(o, n)], sems.at[i])
        for i, (r, (o, n)) in enumerate(zip(refs, offsets))
    ]


def down_copies(refs, scr, sems):
    rows = scr.shape[0] // 4
    half = rows // 2
    offsets = [(0, rows), (rows, rows)] + [(2 * rows + i * half, half) for i in range(4)]
    return [
        pltpu.make_async_copy(r, scr.at[pl.ds(o, n)], sems.at[i])
        for i, (r, (o, n)) in enumerate(zip(refs, offsets))
    ]


def pack_copy(meta, whole, received, dst, sem, use_received):
    rows = dst.shape[0]
    own = pltpu.make_async_copy(whole.at[pl.ds(meta[0] * rows, rows)], dst, sem)
    if received is None:
        own.start()
    else:
        got = pltpu.make_async_copy(received, dst, sem)

        @pl.when(use_received)
        def _():
            got.start()

        @pl.when(jnp.logical_not(use_received))
        def _():
            own.start()

    return own


def attention_kernel(keep, *refs):
    refs = list(refs)
    meta, whole = refs[:2]
    del refs[:2]
    received = refs.pop(0) if keep else None
    bias, adapt_down, adapt_up, gains, biases = refs[:5]
    qkv_refs, out_refs = refs[5:11], refs[11:17]
    del refs[:17]
    if keep:
        normed_out, scale_out, q_out, k_out, v_out, p_out, mid_out = refs[:7]
        del refs[:7]
    else:
        normed_out = refs.pop(0)
    h_v, qkv_v, out_v, acc, q_v, k_v, v_v, p_v, sems, p_sems = refs
    parity = meta[1]
    rows = h_v.shape[0]
    h_copy = pack_copy(meta, whole, received, h_v, sems.at[12], meta[2] == 0)
    weight_copies = qkv_copies(qkv_refs, qkv_v, parity, sems)
    for c in weight_copies:
        c.start()
    out_w_copies = out_copies(out_refs, out_v, parity, sems.at[pl.ds(6, 6)])
    for c in out_w_copies:
        c.start()
    h_copy.wait()
    h = h_v[...]
    mid = nn(h, adapt_down[...]).astype(BF16)
    if keep:
        small = (mid.shape[1], mid.shape[1])
        eye = lax.broadcasted_iota(jnp.int32, small, 0) == lax.broadcasted_iota(jnp.int32, small, 1)
        mid_out[...] = nt(eye.astype(BF16), mid).astype(BF16)
    for c in weight_copies:
        c.wait()
    for c in out_w_copies:
        c.wait()
    acc[...] = h.astype(F32)
    width = qkv_v.shape[3]
    chunk = 256

    def p_copy(slot, head):
        return pltpu.make_async_copy(p_v.at[slot], p_out.at[head], p_sems.at[slot])

    def piece(j, carry):
        h = h_v[...]
        q = nn(h, qkv_v[j, 0]) + 2.0 * nn(mid, adapt_up[j, 0])
        q_v[j] = q.astype(BF16)
        k = nn(h, qkv_v[j, 1]).astype(BF16)
        k_v[j] = k
        v = (nn(h, qkv_v[j, 2]) + 2.0 * nn(mid, adapt_up[j, 1])).astype(BF16)
        v_v[j] = v
        zero = jnp.zeros((), BF16)
        for c in range(rows // chunk):
            part = pl.ds(c * chunk, chunk)
            q_c = q_v[j, part] * jnp.asarray(HEAD_DIM**-0.5, BF16)
            ctx = jnp.zeros((chunk, width), F32)
            for e in range(width // HEAD_DIM):
                low = e * HEAD_DIM
                q_e = jnp.where(lane_mask(q_c.shape, low, low + HEAD_DIM), q_c, zero)
                v_e = jnp.where(lane_mask(v.shape, low, low + HEAD_DIM), v, zero)
                s = nt(q_e, k) + bias[part]
                top = jnp.max(s, -1, keepdims=True)
                w = jnp.exp(s - top)
                p = (w * (1.0 / jnp.sum(w, -1, keepdims=True))).astype(BF16)
                if keep:
                    slot = e
                    if c == 0:

                        @pl.when(j > 0)
                        def _():
                            p_copy(slot, 0).wait()

                    p_v[slot, part] = p
                    if c == rows // chunk - 1:
                        p_copy(slot, j * (width // HEAD_DIM) + e).start()
                ctx = ctx + nn(p, v_e)
            acc[part] += nn(ctx.astype(BF16), out_v[pl.ds(j * width, width)])
        return carry

    lax.fori_loop(0, 4, piece, 0)
    for r in range(0, rows, 128):
        part = pl.ds(r, 128)
        normed, scaled = normalize(acc[part])
        normed_out[part] = normed
        if keep:
            scale_out[part] = scaled
    if keep:
        q_out[...] = q_v[...]
        k_out[...] = k_v[...]
        v_out[...] = v_v[...]
        for e in range(width // HEAD_DIM):
            p_copy(e, 0).wait()


def feedforward_kernel(keep, *refs):
    refs = list(refs)
    normed, gains, biases = refs[:3]
    up_refs, down_refs = refs[3:9], refs[9:15]
    del refs[:15]
    if keep:
        out, normed_out, scale_out, slope_out = refs[:4]
        del refs[:4]
    else:
        out = refs.pop(0)
    up_v, down_v, low_v, act_v, sems = refs
    rows = normed.shape[0]
    ups = up_copies(up_refs, up_v, sems)
    downs = down_copies(down_refs, down_v, sems.at[pl.ds(6, 6)])
    for c in ups + downs:
        c.start()
    for r in range(0, rows, 128):
        part = pl.ds(r, 128)
        low_v[part] = (normed[part] * gains[0:1] + biases[0:1]).astype(BF16)
    for c in ups:
        c.wait()
    block = 256

    def up_step(i, carry):
        cols = pl.ds(pl.multiple_of(i * block, block), block)
        for r in range(0, rows, 256):
            part = pl.ds(r, 256)
            pre = nn(low_v[part], up_v[:, cols])
            cdf = 0.5 + 0.5 * lax.erf(pre * (0.5**0.5))
            act_v[part, cols] = (pre * cdf).astype(BF16)
            if keep:
                density = jnp.exp(pre * pre * -0.5) * 0.3989422804014327
                slope_out[part, cols] = (cdf + pre * density).astype(BF16)
        return carry

    lax.fori_loop(0, up_v.shape[1] // block, up_step, 0)
    for c in downs:
        c.wait()
    for r in range(0, rows, 128):
        part = pl.ds(r, 128)
        total = normed[part] * gains[0:1] + biases[0:1] + nn(act_v[part], down_v[...])
        normed_two, scaled = normalize(total)
        out[part] = (normed_two * gains[1:2] + biases[1:2]).astype(BF16)
        if keep:
            normed_out[part] = normed_two
            scale_out[part] = scaled


def backward_kernel(grads, *refs):
    refs = list(refs)
    meta, whole = refs[:2]
    del refs[:2]
    received = refs.pop(0) if grads else None
    if grads:
        embedded, h_received, mid_t = refs[:3]
        del refs[:3]
    gains, normed_one, scale_one, normed_two, scale_two, slope = refs[:6]
    q_in, k_in, v_in, p_in, adapt_down, adapt_up = refs[6:12]
    del refs[:12]
    qkv_refs, out_refs, up_refs, down_refs = refs[:6], refs[6:12], refs[12:18], refs[18:24]
    del refs[:24]
    dh_out = refs.pop(0)
    if grads:
        grad_down_out, grad_up_out = refs[:2]
        del refs[:2]
    dy_v, qkv_v, out_v, up_v, down_v, p_v, acc, low_v, dpre_v, sems, p_sems = refs[:11]
    del refs[:11]
    if grads:
        h_v, dmid_v = refs
    else:
        (dmid_v,) = refs
    parity = meta[1]
    rows = dy_v.shape[0]
    dy_copy = pack_copy(meta, whole, received, dy_v, sems.at[24], meta[2] == 1)
    downs = down_copies(down_refs, down_v, sems)
    ups = up_copies(up_refs, up_v, sems.at[pl.ds(6, 6)])
    outs = out_copies(out_refs, out_v, parity, sems.at[pl.ds(12, 6)])
    qkvs = qkv_copies(qkv_refs, qkv_v, parity, sems.at[pl.ds(18, 6)])
    for c in downs + ups + outs + qkvs:
        c.start()
    p_copies = [
        pltpu.make_async_copy(p_in.at[pl.ds(3 * j, 3)], p_v.at[pl.ds(3 * j, 3)], p_sems.at[j])
        for j in range(4)
    ]
    for c in p_copies:
        c.start()
    if grads:
        h_copy = pack_copy(meta, embedded, h_received, h_v, sems.at[25], meta[2] == 0)
    dy_copy.wait()
    for r in range(0, rows, 128):
        part = pl.ds(r, 128)
        back = normalize_back(
            normed_two[part], scale_two[part], gains[1:2], dy_v[part].astype(F32)
        )
        acc[part] = back
        low_v[part] = back.astype(BF16)
    for c in downs:
        c.wait()
    block = 256

    def down_step(i, carry):
        cols = pl.ds(pl.multiple_of(i * block, block), block)
        for r in range(0, rows, 256):
            part = pl.ds(r, 256)
            dact = nt(low_v[part], down_v[cols])
            dpre_v[part, cols] = (dact * slope[part, cols].astype(F32)).astype(BF16)
        return carry

    lax.fori_loop(0, down_v.shape[0] // block, down_step, 0)
    for c in ups:
        c.wait()
    for r in range(0, rows, 128):
        part = pl.ds(r, 128)
        total = acc[part] + nt(dpre_v[part], up_v[...])
        back = normalize_back(normed_one[part], scale_one[part], gains[0:1], total)
        acc[part] = back
        low_v[part] = back.astype(BF16)
    for c in outs + qkvs + p_copies:
        c.wait()
    width = qkv_v.shape[3]
    heads = width // HEAD_DIM
    chunk = 256
    factor = HEAD_DIM**-0.5
    dmid_v[...] = jnp.zeros_like(dmid_v)
    eye = (
        lax.broadcasted_iota(jnp.int32, (width, width), 0)
        == lax.broadcasted_iota(jnp.int32, (width, width), 1)
    ).astype(BF16)
    eye_rows = (
        lax.broadcasted_iota(jnp.int32, (rows, rows), 0)
        == lax.broadcasted_iota(jnp.int32, (rows, rows), 1)
    ).astype(BF16)

    def piece(j, carry):
        q, k, v = q_in[j], k_in[j], v_in[j]
        dctx = nt(low_v[...], out_v[pl.ds(j * width, width)]).astype(BF16)
        q_t = nt(eye, q).astype(BF16)
        dctx_t = nt(eye, dctx).astype(BF16)
        zero = jnp.zeros((), BF16)
        dk_t, dv_t = [0.0] * heads, [0.0] * heads
        dq = []
        for c in range(rows // chunk):
            part = slice(c * chunk, (c + 1) * chunk)
            dq_c = jnp.zeros((chunk, width), F32)
            for e in range(heads):
                low = e * HEAD_DIM
                p = p_v[j * heads + e, pl.ds(c * chunk, chunk)]
                dctx_e = jnp.where(lane_mask((chunk, width), low, low + HEAD_DIM), dctx[part], zero)
                k_e = jnp.where(lane_mask(k.shape, low, low + HEAD_DIM), k, zero)
                dp = nt(dctx_e, v)
                p32 = p.astype(F32)
                delta = jnp.sum(p32 * dp, -1, keepdims=True)
                ds = (p32 * (dp - delta)).astype(BF16)
                dq_c = dq_c + nn(ds, k_e)
                dk_t[e] = dk_t[e] + nn(q_t[low : low + HEAD_DIM, part], ds)
                dv_t[e] = dv_t[e] + nn(dctx_t[low : low + HEAD_DIM, part], p)
            dq.append((dq_c * factor).astype(BF16))
        dq = jnp.concatenate(dq, 0)
        dk_t = (jnp.concatenate(dk_t, 0) * factor).astype(BF16)
        dv_t = jnp.concatenate(dv_t, 0).astype(BF16)
        dk = nt(eye_rows, dk_t).astype(BF16)
        dv = nt(eye_rows, dv_t).astype(BF16)
        acc[...] += nt(dq, qkv_v[j, 0]) + nt(dk, qkv_v[j, 1]) + nt(dv, qkv_v[j, 2])
        dmid_v[...] += nt(dq, adapt_up[j, 0]) + nt(dv, adapt_up[j, 1])
        if grads:
            rank = mid_t.shape[0] // 2
            grad_up_out[j, 0] = 2.0 * nn(mid_t[...], dq)[:rank]
            grad_up_out[j, 1] = 2.0 * nn(mid_t[...], dv)[rank:]
        return carry

    lax.fori_loop(0, 4, piece, 0)
    dmid = (2.0 * dmid_v[...]).astype(BF16)
    for r in range(0, rows, 128):
        part = pl.ds(r, 128)
        dh_out[part] = (acc[part] + nt(dmid[r : r + 128], adapt_down[...])).astype(BF16)
    if grads:
        h_copy.wait()
        dmid_t = nt(eye_rows[: dmid.shape[1], : dmid.shape[1]], dmid).astype(BF16)
        grad_down_out[...] = nn(dmid_t, h_v[...])


def params(flops, size):
    return dict(
        compiler_params=pltpu.CompilerParams(vmem_limit_bytes=VMEM_LIMIT),
        cost_estimate=pl.CostEstimate(flops=flops, bytes_accessed=size, transcendentals=0),
    )


def local(
    embedded,
    segment,
    query_key_value_weight,
    attention_output_weight,
    feedforward_up_weight,
    feedforward_down_weight,
    adapter_down_weight,
    adapter_up_weight,
    layer_norm_gain,
    layer_norm_bias,
    cotangent,
):
    section = lax.axis_index("section")
    tensor = lax.axis_index("tensor")
    parity = lax.rem(lax.axis_index("dp"), 2)
    groups, packs = lax.axis_size("tensor"), segment.shape[0]
    assert groups == 4 and packs == groups and lax.axis_size("dp") % 2 == 0
    rows, width = segment.shape[1], embedded.shape[1]
    piece = query_key_value_weight.shape[3]
    hidden = feedforward_up_weight.shape[2] * groups
    rank = adapter_down_weight.shape[3]
    heads = piece * groups // HEAD_DIM
    is_first = (section == 0).astype(jnp.int32)
    meta = jnp.stack([tensor, parity, is_first]).astype(jnp.int32)
    gains, biases = layer_norm_gain[0], layer_norm_bias[0]

    def flip_core(value):
        return lax.ppermute(value, "tensor", [(i, i ^ 1) for i in range(groups)])

    def flip_chip(value):
        return lax.ppermute(value, "tensor", [(i, i ^ 2) for i in range(groups)])

    def flip_plane(value):
        return lax.ppermute(value, "dp", [(i, i ^ 1) for i in range(lax.axis_size("dp"))])

    def flip_section(value):
        return lax.ppermute(value, "section", [(0, 1), (1, 0)])

    def gather(weight, axis):
        half = weight.shape[axis] // 2
        mine = lax.dynamic_slice_in_dim(weight, parity * half, half, axis)
        near = flip_chip(mine)
        far = flip_plane(near)
        return (weight, flip_core(weight), near, far, flip_core(near), flip_core(far))

    up = adapter_up_weight[0]
    up_sib = flip_core(up)
    up_far = flip_chip(up)
    ups = jnp.stack([up, up_sib, up_far, flip_core(up_far)])
    zeros = jnp.zeros_like(ups[:, 0])
    adapt_up = jnp.stack(
        [jnp.concatenate([ups[:, 0], zeros], 1), jnp.concatenate([zeros, ups[:, 1]], 1)], 1
    )
    adapt_down = jnp.concatenate([adapter_down_weight[0, 0], adapter_down_weight[0, 1]], -1)

    qkv = gather(query_key_value_weight[0], 1)
    outw = gather(attention_output_weight[0], 0)
    upw = gather(feedforward_up_weight[0], 1)
    downw = gather(feedforward_down_weight[0], 0)

    segs = lax.dynamic_index_in_dim(segment, tensor, 0, keepdims=False)
    bias = jnp.where(segs[:, None] == segs[None, :], 0.0, -1e9).astype(F32)

    def arr(shape, dtype):
        return jax.ShapeDtypeStruct(shape, dtype)

    def attention(keep, received=None):
        out_shape = [arr((rows, width), F32)]
        out_specs = [VMEM]
        if keep:
            kept_piece = arr((groups, rows, piece), BF16)
            out_shape += [arr((rows, 1), F32)] + [kept_piece] * 3
            out_shape += [arr((heads, rows, rows), BF16), arr((2 * rank, rows), BF16)]
            out_specs += [VMEM] * 4 + [ANY, VMEM]
        return pl.pallas_call(
            partial(attention_kernel, keep),
            name="attention_keep" if keep else "attention",
            out_shape=out_shape,
            in_specs=[SMEM, ANY] + [ANY] * keep + [VMEM] * 5 + [ANY] * 12,
            out_specs=out_specs,
            scratch_shapes=[
                pltpu.VMEM((rows, width), BF16),
                pltpu.VMEM((groups, 3, width, piece), BF16),
                pltpu.VMEM((groups * piece, width), BF16),
                pltpu.VMEM((rows, width), F32),
                pltpu.VMEM((groups, rows, piece), BF16),
                pltpu.VMEM((groups, rows, piece), BF16),
                pltpu.VMEM((groups, rows, piece), BF16),
                pltpu.VMEM((piece // HEAD_DIM, rows, rows), BF16),
                pltpu.SemaphoreType.DMA((13,)),
                pltpu.SemaphoreType.DMA((piece // HEAD_DIM,)),
            ],
            **params(8 * 10**9, 10**7),
        )(
            meta,
            embedded,
            *([received] if keep else []),
            bias,
            adapt_down,
            adapt_up,
            gains,
            biases,
            *qkv,
            *outw,
        )

    def feedforward(keep, normed):
        out_shape = [arr((rows, width), BF16)]
        if keep:
            out_shape += [
                arr((rows, width), F32),
                arr((rows, 1), F32),
                arr((rows, hidden), BF16),
            ]
        return pl.pallas_call(
            partial(feedforward_kernel, keep),
            name="feedforward_keep" if keep else "feedforward",
            out_shape=out_shape,
            in_specs=[VMEM] * 3 + [ANY] * 12,
            out_specs=[VMEM] * len(out_shape),
            scratch_shapes=[
                pltpu.VMEM((width, hidden), BF16),
                pltpu.VMEM((hidden, width), BF16),
                pltpu.VMEM((rows, width), BF16),
                pltpu.VMEM((rows, hidden), BF16),
                pltpu.SemaphoreType.DMA((12,)),
            ],
            **params(8 * 10**9, 10**7),
        )(normed, gains, biases, *upw, *downw)

    def backward(grads, kept, received=None, h_received=None):
        normed_one, scale_one, q, k, v, p, mid, normed_two, scale_two, slope = kept
        out_shape = [arr((rows, width), BF16)]
        if grads:
            out_shape += [
                arr((2 * rank, width), F32),
                arr((groups, 2, rank, piece), F32),
            ]
        extra = [received, embedded, h_received, mid] if grads else []
        extra_specs = [ANY] * 3 + [VMEM] if grads else []
        scratch = [
            pltpu.VMEM((rows, width), BF16),
            pltpu.VMEM((groups, 3, width, piece), BF16),
            pltpu.VMEM((groups * piece, width), BF16),
            pltpu.VMEM((width, hidden), BF16),
            pltpu.VMEM((hidden, width), BF16),
            pltpu.VMEM((heads, rows, rows), BF16),
            pltpu.VMEM((rows, width), F32),
            pltpu.VMEM((rows, width), BF16),
            pltpu.VMEM((rows, hidden), BF16),
            pltpu.SemaphoreType.DMA((26,)),
            pltpu.SemaphoreType.DMA((4,)),
        ]
        if grads:
            scratch.append(pltpu.VMEM((rows, width), BF16))
        scratch.append(pltpu.VMEM((rows, 2 * rank), F32))
        return pl.pallas_call(
            partial(backward_kernel, grads),
            name="backward_grads" if grads else "backward",
            out_shape=out_shape,
            in_specs=[SMEM, ANY] + extra_specs + [VMEM] * 9 + [ANY] + [VMEM] * 2 + [ANY] * 24,
            out_specs=[VMEM] * len(out_shape),
            scratch_shapes=scratch,
            **params(18 * 10**9, 3 * 10**7),
        )(
            meta,
            cotangent,
            *extra,
            gains,
            normed_one,
            scale_one,
            normed_two,
            scale_two,
            slope,
            q,
            k,
            v,
            p,
            adapt_down,
            adapt_up,
            *qkv,
            *outw,
            *upw,
            *downw,
        )

    (normed,) = attention(False)
    (first_layer,) = feedforward(False, normed)
    received = flip_section(first_layer)
    normed_one, scale_one, q, k, v, p, mid = attention(True, received)
    out, normed_two, scale_two, slope = feedforward(True, normed_one)
    layer_outs = lax.all_gather(out, "tensor", axis=0, tiled=True)
    kept = (normed_one, scale_one, q, k, v, p, mid, normed_two, scale_two, slope)
    (dh,) = backward(False, kept)
    back_received = flip_section(dh)
    dinput, grad_down, grad_up = backward(True, kept, back_received, received)
    in_grads = lax.all_gather(dinput, "tensor", axis=0, tiled=True)
    grad_down = grad_down.reshape(2, rank, width)
    own_order = jnp.arange(groups) ^ tensor
    grad_up = jnp.take(grad_up, own_order, axis=0)
    both = lax.psum((grad_down, grad_up), ("dp", "tensor"))
    grad_a = jnp.swapaxes(both[0], 1, 2)
    grad_b = lax.dynamic_index_in_dim(both[1], tensor, 0, keepdims=False)
    return (layer_outs[None], in_grads[None], grad_a[None], grad_b[None])


def solution(mesh):
    in_specs = (
        P("dp", None),
        P("dp", None),
        P("section", None, None, "tensor"),
        P("section", "tensor", None),
        P("section", None, "tensor"),
        P("section", "tensor", None),
        P("section", None, None, None),
        P("section", None, None, "tensor"),
        P("section", None, None),
        P("section", None, None),
        P("dp", None),
    )
    out_specs = (
        P("section", "dp", None),
        P("section", "dp", None),
        P("section", None, None, None),
        P("section", None, None, "tensor"),
    )
    return jax.shard_map(local, mesh=mesh, in_specs=in_specs, out_specs=out_specs, check_vma=False)
```

```python
from functools import partial

import jax
import jax.numpy as jnp
from jax import lax
from jax.experimental import pallas as pl
from jax.experimental.pallas import tpu as pltpu
from jax.sharding import PartitionSpec as P

HEAD_DIM = 64
EPS = 1e-05
VMEM_LIMIT = 60 * 2**20
F32 = jnp.float32
BF16 = jnp.bfloat16
ANY = pl.BlockSpec(memory_space=pl.ANY)
VMEM = pl.BlockSpec(memory_space=pltpu.VMEM)
MESH = pl.DeviceIdType.MESH
SMEM = pl.BlockSpec(memory_space=pltpu.SMEM)


def nn(a, b):
    return jnp.dot(a, b, preferred_element_type=F32)


def nt(a, b):
    return lax.dot_general(a, b, (((1,), (1,)), ((), ())), preferred_element_type=F32)


def lane_mask(shape, low, high):
    lanes = lax.broadcasted_iota(jnp.int32, shape, len(shape) - 1)
    return (lanes >= low) & (lanes < high)


def normalize(total):
    average = jnp.mean(total, -1, keepdims=True)
    centred = total - average
    spread = jnp.mean(centred * centred, -1, keepdims=True)
    scaled = lax.rsqrt(spread + EPS)
    return centred * scaled, scaled


def normalize_back(normed, scaled, gains, incoming):
    weighted = incoming * gains
    return scaled * (
        weighted
        - jnp.mean(weighted, -1, keepdims=True)
        - normed * jnp.mean(weighted * normed, -1, keepdims=True)
    )


def neighbours():
    section, plane, tensor = (lax.axis_index(n) for n in ("section", "dp", "tensor"))
    turned = lax.rem(tensor + 2, 4)
    other = tensor + 1 - 2 * lax.rem(tensor, 2)
    paired = plane + 1 - 2 * lax.rem(plane, 2)
    return (
        (section, plane, other),
        (section, plane, turned),
        (section, paired, tensor),
        (1 - section, plane, tensor),
    )


def meet(devices):
    barrier = pltpu.get_barrier_semaphore()
    for device in devices:
        pl.semaphore_signal(barrier, inc=1, device_id=device, device_id_type=MESH)
    pl.semaphore_wait(barrier, len(devices))


def remote(src, dst, send, recv, device):
    return pltpu.make_async_remote_copy(
        src_ref=src,
        dst_ref=dst,
        send_sem=send,
        recv_sem=recv,
        device_id=device,
        device_id_type=MESH,
    )


def first_kernel(
    embedded,
    segment,
    gains,
    biases,
    adapt_down,
    adapt,
    qkv,
    outw,
    up,
    down,
    received,
    bias,
    adapt_up,
    qkv_g,
    out_g,
    ff_g,
    qkv_v,
    out_v,
    ff_v,
    h_v,
    acc,
    normed,
    q_v,
    low_v,
    act_v,
    result,
    local_sems,
    send,
    recv,
    hop_send,
    hop_recv,
):
    core, far, plane, beyond = neighbours()
    tensor = lax.axis_index("tensor")
    parity = lax.rem(lax.axis_index("dp"), 2)
    rows, width = h_v.shape
    n_qkv, n_out, n_ff, n_adapt = qkv.shape[1], outw.shape[0], up.shape[0], adapt.shape[0]
    slots = 4
    h_half, o_half, f_half = n_qkv // 2, n_out // 2, n_ff // 2
    quarter = f_half // 2

    def own_part(c, p):
        if c < 3:
            return qkv.at[c, pl.ds(p * h_half, h_half)]
        if c == 3:
            return outw.at[pl.ds(p * o_half, o_half)]
        return (up, down)[(c - 4) // 2].at[pl.ds(p * f_half + (c - 4) % 2 * quarter, quarter)]

    def part(c, slot, p):
        if isinstance(c, int) and c < 3:
            return qkv_v.at[c, pl.ds(slot * n_qkv + p * h_half, h_half)]
        if isinstance(c, int) and c == 3:
            return out_v.at[pl.ds(slot * n_out + p * o_half, o_half)]
        i = c - 4
        return ff_v.at[i // 2, slot, pl.ds(p * f_half + lax.rem(i, 2) * quarter, quarter)]

    def link(kind, c, src, dst, device):
        return remote(src, dst, send.at[kind, c], recv.at[kind, c], device)

    def over_far(c, source=None):
        here = part(c, 2, parity)
        return link(0, c, here if source is None else source, here, far)

    def to_plane(c):
        here = part(c, 2, parity)
        return link(1, c, here, here, plane)

    def near_to_core(c):
        return link(2, c, part(c, 2, parity), part(c, 3, parity), core)

    def other_to_core(c):
        return link(3, c, part(c, 2, 1 - parity), part(c, 3, 1 - parity), core)

    def from_plane(c):
        there = part(c, 2, 1 - parity)
        return link(1, c, there, there, plane)

    def pump(c):
        over_far(c).wait_recv()
        to_plane(c).start()
        near_to_core(c).start()

    def relay(c):
        from_plane(c).wait_recv()
        other_to_core(c).start()

    def landed(c):
        near_to_core(c).wait_recv()
        other_to_core(c).wait_recv()

    wholes = (
        (qkv, lambda k: qkv_v.at[:, pl.ds(k * n_qkv, n_qkv)]),
        (outw, lambda k: out_v.at[pl.ds(k * n_out, n_out)]),
        (up, lambda k: ff_v.at[0, k]),
        (down, lambda k: ff_v.at[1, k]),
        (adapt, lambda k: adapt_up.at[pl.ds(k * n_adapt, n_adapt)]),
    )
    meet((core, far, plane, beyond))
    h_copy = pltpu.make_async_copy(
        embedded.at[pl.ds(tensor * rows, rows)], h_v, local_sems.at[len(wholes)]
    )
    h_copy.start()
    adapt_far = link(5, 0, adapt, wholes[4][1](2), far)
    adapt_far.start()
    count = 8
    for c in range(count):
        over_far(c, own_part(c, parity)).start()
    to_core, mine = [], []
    for i, (own, full) in enumerate(wholes):
        to_core.append(link(4, i, own, full(1), core))
        to_core[-1].start()
        mine.append(pltpu.make_async_copy(own, full(0), local_sems.at[i]))
        mine[-1].start()
    ids = segment[pl.ds(tensor, 1), :].astype(F32)
    square = (rows, rows)
    diagonal = lax.broadcasted_iota(jnp.int32, square, 0) == lax.broadcasted_iota(
        jnp.int32, square, 1
    )
    column = jnp.sum(jnp.where(diagonal, ids, 0.0), -1, keepdims=True)
    bias[...] = jnp.where(column == ids, 0.0, -1e9)
    h_copy.wait()
    mid_q, mid_v, _ = middle(h_v[...], adapt_down[...])
    acc[...] = h_v[...].astype(F32)
    adapt_far.wait_recv()
    adapt_core = link(5, 1, wholes[4][1](2), wholes[4][1](3), core)
    adapt_core.start()
    for c in range(4):
        pump(c)
        if c > 0:
            relay(c - 1)
    relay(3)
    for i in (0, 1, 4):
        mine[i].wait()
        to_core[i].wait_recv()
    adapt_core.wait_recv()
    for c in range(4):
        landed(c)
    back = [
        pltpu.make_async_copy(qkv_v, qkv_g, local_sems.at[6]),
        pltpu.make_async_copy(out_v, out_g, local_sems.at[7]),
    ]
    for copy in back:
        copy.start()
    span = q_v.shape[1]

    def group(g, carry):
        attention_group(
            g, span, h_v, mid_q, mid_v, adapt_up, qkv_v, out_v, bias, q_v, acc, None, None
        )
        pump(4 + g)

        @pl.when(g > 0)
        def _():
            relay(3 + g)

        return carry

    lax.fori_loop(0, width // span, group, 0)
    for r in range(0, rows, 128):
        chunk = pl.ds(r, 128)
        first = normalize(acc[chunk])[0] * gains[0:1] + biases[0:1]
        acc[chunk] = first
        low_v[chunk] = first.astype(BF16)
    relay(6)
    for i in (2, 3):
        mine[i].wait()
        to_core[i].wait_recv()
    feedforward_up(low_v, lambda s, cols: ff_v[0, s, :, cols], act_v, None, 0, 2)
    pump(7)
    landed(4)
    landed(5)
    feedforward_up(low_v, lambda s, cols: ff_v[0, s, :, cols], act_v, None, 2, 4)
    for r in range(0, rows, 256):
        chunk = pl.ds(r, 256)
        acc[chunk] += nn(act_v[0, chunk], ff_v[1, 0]) + nn(act_v[1, chunk], ff_v[1, 1])
    relay(7)
    landed(6)
    landed(7)
    back.append(pltpu.make_async_copy(ff_v, ff_g, local_sems.at[8]))
    back[-1].start()
    hops = []
    for r in range(0, rows, 128):
        chunk = pl.ds(r, 128)
        total = acc[chunk] + nn(act_v[2, chunk], ff_v[1, 2]) + nn(act_v[3, chunk], ff_v[1, 3])
        result[chunk] = (normalize(total)[0] * gains[1:2] + biases[1:2]).astype(BF16)
        i = r // 128
        hops.append(
            remote(result.at[chunk], received.at[chunk], hop_send.at[i], hop_recv.at[i], beyond)
        )
        hops[-1].start()
    for c in range(count):
        for copy in (over_far(c), to_plane(c), near_to_core(c), other_to_core(c)):
            copy.wait_send()
    for copy in to_core + [adapt_far, adapt_core]:
        copy.wait_send()
    for copy in back:
        copy.wait()
    for copy in hops:
        copy.wait()


def pack_copy(meta, whole, received, dst, sem, use_received):
    rows = dst.shape[0]
    own = pltpu.make_async_copy(whole.at[pl.ds(meta[0] * rows, rows)], dst, sem)
    if received is None:
        own.start()
    else:
        got = pltpu.make_async_copy(received, dst, sem)

        @pl.when(use_received)
        def _():
            got.start()

        @pl.when(jnp.logical_not(use_received))
        def _():
            own.start()

    return own


def identity(n):
    rows = lax.broadcasted_iota(jnp.int32, (n, n), 0)
    return (rows == lax.broadcasted_iota(jnp.int32, (n, n), 1)).astype(BF16)


def middle(h, adapt_down):
    mid = nt(h, adapt_down).astype(BF16)
    rank = mid.shape[1] // 2
    is_query = lane_mask(mid.shape, 0, rank)
    double = mid * jnp.asarray(2.0, BF16)
    zero = jnp.zeros((), BF16)
    return jnp.where(is_query, double, zero), jnp.where(is_query, zero, double), mid


def attention_group(g, span, h_v, mid_q, mid_v, adapt_up, qkv_v, out_v, bias, q_v, acc, kept, p_step):
    rows = h_v.shape[0]
    heads = span // HEAD_DIM
    chunk = 256
    cols = pl.ds(pl.multiple_of(g * span, span), span)
    h = h_v[...]
    q = nt(h, qkv_v[0, cols]) + nt(mid_q, adapt_up[cols])
    k = nt(h, qkv_v[1, cols]).astype(BF16)
    v = (nt(h, qkv_v[2, cols]) + nt(mid_v, adapt_up[cols])).astype(BF16)
    q_v[...] = q.astype(BF16)
    if kept is not None:
        for ref, value in zip(kept, (q.astype(BF16), k, v)):
            ref[g] = value
    zero = jnp.zeros((), BF16)
    for c in range(rows // chunk):
        part = pl.ds(c * chunk, chunk)
        q_c = q_v[part] * jnp.asarray(HEAD_DIM**-0.5, BF16)
        ctx = jnp.zeros((chunk, span), F32)
        for e in range(heads):
            low = e * HEAD_DIM
            q_e = jnp.where(lane_mask(q_c.shape, low, low + HEAD_DIM), q_c, zero)
            v_e = jnp.where(lane_mask(v.shape, low, low + HEAD_DIM), v, zero)
            s = nt(q_e, k) + bias[part]
            top = jnp.max(s, -1, keepdims=True)
            w = jnp.exp(s - top)
            p = (w * (1.0 / jnp.sum(w, -1, keepdims=True))).astype(BF16)
            if p_step is not None:
                p_step(e, c, part, p)
            ctx = ctx + nn(p, v_e)
        acc[part] += nn(ctx.astype(BF16), out_v[cols])


def attention_kernel(
    meta,
    whole,
    received,
    bias,
    adapt_down,
    adapt_up,
    qkv_g,
    out_g,
    normed_out,
    scale_out,
    q_out,
    k_out,
    v_out,
    p_out,
    mid_out,
    h_v,
    qkv_v,
    out_v,
    acc,
    q_v,
    p_v,
    sems,
    p_sems,
):
    rows = h_v.shape[0]
    h_copy = pack_copy(meta, whole, received, h_v, sems.at[0], meta[2] == 0)
    qkv_copy = pltpu.make_async_copy(qkv_g, qkv_v, sems.at[1])
    out_copy = pltpu.make_async_copy(out_g, out_v, sems.at[2])
    qkv_copy.start()
    out_copy.start()
    h_copy.wait()
    h = h_v[...]
    mid_q, mid_v, mid = middle(h, adapt_down[...])
    mid_out[...] = nt(identity(mid.shape[1]), mid).astype(BF16)
    acc[...] = h.astype(F32)
    qkv_copy.wait()
    out_copy.wait()
    groups, _, span = q_out.shape
    heads = span // HEAD_DIM

    def p_copy(slot, head):
        return pltpu.make_async_copy(p_v.at[slot], p_out.at[head], p_sems.at[slot])

    def group(g, carry):
        def p_step(e, c, part, p):
            if c == 0:

                @pl.when(g > 0)
                def _():
                    p_copy(e, 0).wait()

            p_v[e, part] = p
            if c == rows // 256 - 1:
                p_copy(e, g * heads + e).start()

        attention_group(
            g,
            span,
            h_v,
            mid_q,
            mid_v,
            adapt_up,
            qkv_v,
            out_v,
            bias,
            q_v,
            acc,
            (q_out, k_out, v_out),
            p_step,
        )
        return carry

    lax.fori_loop(0, groups, group, 0)
    for r in range(0, rows, 128):
        part = pl.ds(r, 128)
        normed, scaled = normalize(acc[part])
        normed_out[part] = normed
        scale_out[part] = scaled
    for e in range(heads):
        p_copy(e, 0).wait()


def feedforward_up(low_v, weight, act_v, slope, begin, end):
    rows = low_v.shape[0]
    wide = act_v.shape[2]
    block = 256
    each = wide // block

    def step(i, carry):
        slot = i // each
        cols = pl.ds(pl.multiple_of(lax.rem(i, each) * block, block), block)
        for r in range(0, rows, 256):
            part = pl.ds(r, 256)
            pre = nn(low_v[part], weight(slot, cols))
            cdf = 0.5 + 0.5 * lax.erf(pre * (0.5**0.5))
            act_v[slot, part, cols] = (pre * cdf).astype(BF16)
            if slope is not None:
                density = jnp.exp(pre * pre * -0.5) * 0.3989422804014327
                slope[slot, part, cols] = (cdf + pre * density).astype(BF16)
        return carry

    lax.fori_loop(begin * each, end * each, step, 0)


def feedforward_kernel(
    normed,
    gains,
    biases,
    ff_g,
    out,
    normed_out,
    scale_out,
    slope_out,
    ff_v,
    low_v,
    act_v,
    sems,
):
    rows = normed.shape[0]
    ups = pltpu.make_async_copy(ff_g.at[0], ff_v.at[0], sems.at[0])
    downs = pltpu.make_async_copy(ff_g.at[1], ff_v.at[1], sems.at[1])
    ups.start()
    downs.start()
    for r in range(0, rows, 128):
        part = pl.ds(r, 128)
        low_v[part] = (normed[part] * gains[0:1] + biases[0:1]).astype(BF16)
    ups.wait()
    slots = ff_v.shape[1]
    feedforward_up(low_v, lambda s, cols: ff_v[0, s, :, cols], act_v, slope_out, 0, slots)
    downs.wait()
    for r in range(0, rows, 128):
        part = pl.ds(r, 128)
        total = normed[part] * gains[0:1] + biases[0:1]
        for slot in range(slots):
            total = total + nn(act_v[slot, part], ff_v[1, slot])
        normed_two, scaled = normalize(total)
        out[part] = (normed_two * gains[1:2] + biases[1:2]).astype(BF16)
        normed_out[part] = normed_two
        scale_out[part] = scaled


def backward_kernel(grads, *refs):
    refs = list(refs)
    meta, whole = refs[:2]
    del refs[:2]
    received = refs.pop(0) if grads else None
    if grads:
        embedded, h_received, mid_t, *out_blocks = refs[:7]
        del refs[:7]
    gains, normed_one, scale_one, normed_two, scale_two, slope = refs[:6]
    q_in, k_in, v_in, p_in, adapt_down, adapt_up = refs[6:12]
    qkv_g, out_g, ff_g = refs[12:15]
    del refs[:15]
    dh_out = refs.pop(0)
    if grads:
        grad_down_out, grad_up_out, layer_out = refs[:3]
        del refs[:3]
    dy_v, qkv_v, out_v, ff_v, p_v, acc, low_v, dpre_v, dmid_v, sems, p_sems = refs[:11]
    del refs[:11]
    rows = dy_v.shape[0]
    _, slots, _, wide = ff_v.shape
    dy_copy = pack_copy(meta, whole, received, dy_v, sems.at[0], meta[2] == 1)
    pairs = (
        (ff_g.at[1], ff_v.at[1]),
        (ff_g.at[0], ff_v.at[0]),
        (out_g, out_v),
        (qkv_g, qkv_v),
    )
    downs, ups, outs, qkvs = (
        pltpu.make_async_copy(a, b, sems.at[1 + i]) for i, (a, b) in enumerate(pairs)
    )
    for c in (downs, ups, outs):
        c.start()
    span = 256
    heads = span // HEAD_DIM
    groups = q_in.shape[0]
    p_copies = [
        pltpu.make_async_copy(p_in.at[heads_of], p_v.at[heads_of], p_sems.at[j])
        for j, heads_of in enumerate(pl.ds(heads * j, heads) for j in range(groups))
    ]
    for c in p_copies:
        c.start()
    qkvs.start()
    if grads:
        h_v, blocks_v, in_sems, out_sems = refs
        h_copy = pack_copy(meta, embedded, h_received, h_v, sems.at[5], meta[2] == 0)
        blocks_in = [
            pltpu.make_async_copy(block, blocks_v.at[i], in_sems.at[i])
            for i, block in enumerate(out_blocks)
        ]
        blocks = [
            pltpu.make_async_copy(
                blocks_v.at[i],
                layer_out.at[pl.ds(lax.bitwise_xor(meta[0], i) * rows, rows)],
                out_sems.at[i],
            )
            for i in range(len(out_blocks))
        ]
        for c in blocks_in:
            c.start()
    dy_copy.wait()
    for r in range(0, rows, 128):
        part = pl.ds(r, 128)
        back = normalize_back(
            normed_two[part], scale_two[part], gains[1:2], dy_v[part].astype(F32)
        )
        acc[part] = back
        low_v[part] = back.astype(BF16)
    downs.wait()
    block = 256

    def down_step(i, carry):
        slot = i // (wide // block)
        inner = pl.ds(pl.multiple_of(lax.rem(i, wide // block) * block, block), block)
        for r in range(0, rows, 256):
            part = pl.ds(r, 256)
            dact = nt(low_v[part], ff_v[1, slot, inner])
            dpre_v[slot, part, inner] = (dact * slope[slot, part, inner].astype(F32)).astype(BF16)
        return carry

    lax.fori_loop(0, slots * wide // block, down_step, 0)
    if grads:
        for landed, c in zip(blocks_in, blocks):
            landed.wait()
            c.start()
    ups.wait()
    for r in range(0, rows, 128):
        part = pl.ds(r, 128)
        total = acc[part]
        for slot in range(slots):
            total = total + nt(dpre_v[slot, part], ff_v[0, slot])
        back = normalize_back(normed_one[part], scale_one[part], gains[0:1], total)
        acc[part] = back
        low_v[part] = back.astype(BF16)
    for c in [outs, qkvs] + p_copies:
        c.wait()
    chunk = 256
    factor = HEAD_DIM**-0.5
    dmid_v[...] = jnp.zeros_like(dmid_v)
    eye = identity(span)
    eye_rows = identity(rows)

    def group(g, carry):
        cols = pl.ds(pl.multiple_of(g * span, span), span)
        q, k, v = q_in[g], k_in[g], v_in[g]
        dctx = nt(low_v[...], out_v[cols]).astype(BF16)
        q_t = nt(eye, q).astype(BF16)
        dctx_t = nt(eye, dctx).astype(BF16)
        zero = jnp.zeros((), BF16)
        dk_t, dv_t = [0.0] * heads, [0.0] * heads
        dq = []
        for c in range(rows // chunk):
            part = slice(c * chunk, (c + 1) * chunk)
            dq_c = jnp.zeros((chunk, span), F32)
            for e in range(heads):
                low = e * HEAD_DIM
                p = p_v[g * heads + e, pl.ds(c * chunk, chunk)]
                dctx_e = jnp.where(lane_mask((chunk, span), low, low + HEAD_DIM), dctx[part], zero)
                k_e = jnp.where(lane_mask(k.shape, low, low + HEAD_DIM), k, zero)
                dp = nt(dctx_e, v)
                p32 = p.astype(F32)
                delta = jnp.sum(p32 * dp, -1, keepdims=True)
                ds = (p32 * (dp - delta)).astype(BF16)
                dq_c = dq_c + nn(ds, k_e)
                dk_t[e] = dk_t[e] + nn(q_t[low : low + HEAD_DIM, part], ds)
                dv_t[e] = dv_t[e] + nn(dctx_t[low : low + HEAD_DIM, part], p)
            dq.append((dq_c * factor).astype(BF16))
        dq = jnp.concatenate(dq, 0)
        dk_t = (jnp.concatenate(dk_t, 0) * factor).astype(BF16)
        dv_t = jnp.concatenate(dv_t, 0).astype(BF16)
        dk = nt(eye_rows, dk_t).astype(BF16)
        dv = nt(eye_rows, dv_t).astype(BF16)
        acc[...] += nn(dq, qkv_v[0, cols]) + nn(dk, qkv_v[1, cols]) + nn(dv, qkv_v[2, cols])
        up = adapt_up[cols]
        rank = up.shape[1] // 2
        dmid_q, dmid_v_ = nn(dq, up), nn(dv, up)
        dmid_v[...] += jnp.where(lane_mask(dmid_q.shape, 0, rank), dmid_q, dmid_v_)
        if grads:
            grad_up_out[g, 0] = 2.0 * nn(mid_t[...], dq)[:rank]
            grad_up_out[g, 1] = 2.0 * nn(mid_t[...], dv)[rank:]
        return carry

    lax.fori_loop(0, groups, group, 0)
    dmid = (2.0 * dmid_v[...]).astype(BF16)
    for r in range(0, rows, 128):
        part = pl.ds(r, 128)
        dh_out[part] = (acc[part] + nn(dmid[r : r + 128], adapt_down[...])).astype(BF16)
    if grads:
        h_copy.wait()
        dmid_t = nt(identity(dmid.shape[1]), dmid).astype(BF16)
        grad_down = nn(dmid_t, h_v[...])
        parts, each, _ = grad_down_out.shape
        for i in range(parts):
            grad_down_out[i] = grad_down[i * each : (i + 1) * each]
        for c in blocks:
            c.wait()


def finish_kernel(
    planes,
    dinput,
    grad_down,
    grad_up,
    in_grads,
    down_out,
    up_out,
    from_down,
    from_up,
    plane_down,
    plane_up,
    local_sem,
    row_send,
    row_recv,
    sum_send,
    sum_recv,
):
    section, plane, tensor = (lax.axis_index(n) for n in ("section", "dp", "tensor"))
    core, far, _, _ = neighbours()
    turned = lax.rem(tensor + 2, 4)
    other = tensor + 1 - 2 * lax.rem(tensor, 2)
    across = lax.rem(other + 2, 4)
    sides = ((section, plane, other), (section, plane, turned), (section, plane, across))
    indices = (other, turned, across)
    ring = [(section, lax.rem(plane + m, planes), tensor) for m in range(1, planes)]
    meet((*sides, *ring))
    rows = dinput.shape[0]
    parts = 4
    step = rows // parts

    def block(index, i):
        return in_grads.at[pl.ds(index * rows + i * step, step)]

    sent = []
    for i in range(parts):
        copy = remote(
            dinput.at[pl.ds(i * step, step)], block(tensor, i), row_send.at[0, i], row_recv.at[0, i], far
        )
        copy.start()
        sent.append(copy)
    tensor_copies = []
    for i, device in enumerate(sides):
        for which, (src, dst) in enumerate(
            ((grad_down.at[indices[i]], from_down.at[i]), (grad_up.at[i + 1], from_up.at[i]))
        ):
            n = 2 * i + which
            copy = remote(src, dst, sum_send.at[n], sum_recv.at[n], device)
            copy.start()
            tensor_copies.append(copy)
    mine = pltpu.make_async_copy(dinput, in_grads.at[pl.ds(tensor * rows, rows)], local_sem)
    mine.start()
    to_core = remote(
        dinput, in_grads.at[pl.ds(tensor * rows, rows)], row_send.at[2, 0], row_recv.at[2, 0], core
    )
    to_core.start()
    sent.append(to_core)
    for copy in tensor_copies:
        copy.wait()
    plane_down[plane] = grad_down[tensor] + from_down[0] + from_down[1] + from_down[2]
    plane_up[plane] = grad_up[0] + from_up[0] + from_up[1] + from_up[2]
    base = 2 * len(sides)
    ring_copies = []
    for m, device in enumerate(ring):
        for which, ref in enumerate((plane_down, plane_up)):
            n = base + 2 * m + which
            copy = remote(ref.at[plane], ref.at[plane], sum_send.at[n], sum_recv.at[n], device)
            copy.start()
            ring_copies.append(copy)
    relays = []

    def relay(i):
        landed = block(turned, i)
        remote(landed, landed, row_send.at[0, i], row_recv.at[0, i], far).wait_recv()
        copy = remote(landed, landed, row_send.at[1, i], row_recv.at[1, i], core)
        copy.start()
        relays.append(copy)

    relay(0)
    for m in range(1, planes):
        source = lax.rem(plane + planes - m, planes)
        for which, ref in enumerate((plane_down, plane_up)):
            n = base + 2 * (m - 1) + which
            remote(
                ref.at[source], ref.at[source], sum_send.at[n], sum_recv.at[n], ring[m - 1]
            ).wait_recv()
    for copy in ring_copies:
        copy.wait_send()
    down_total, up_total = plane_down[0], plane_up[0]
    for m in range(1, planes):
        down_total = down_total + plane_down[m]
        up_total = up_total + plane_up[m]
    up_out[...] = up_total
    down_out[tensor] = down_total
    base += 2 * len(ring)
    last = []
    for i, device in enumerate(sides):
        n = base + i
        copy = remote(
            down_out.at[tensor], down_out.at[tensor], sum_send.at[n], sum_recv.at[n], device
        )
        copy.start()
        last.append(copy)
    for i in range(1, parts):
        relay(i)
    for i, device in enumerate(sides):
        n = base + i
        landed = down_out.at[indices[i]]
        remote(landed, landed, sum_send.at[n], sum_recv.at[n], device).wait_recv()
    for copy in last:
        copy.wait_send()
    to_core.wait_recv()
    for i in range(parts):
        landed = block(across, i)
        remote(landed, landed, row_send.at[1, i], row_recv.at[1, i], core).wait_recv()
    for copy in sent + relays:
        copy.wait_send()
    mine.wait()


def params(flops, size, collective=None):
    extra = {} if collective is None else dict(collective_id=collective, has_side_effects=True)
    return dict(
        compiler_params=pltpu.CompilerParams(vmem_limit_bytes=VMEM_LIMIT, **extra),
        cost_estimate=pl.CostEstimate(flops=flops, bytes_accessed=size, transcendentals=0),
    )


def local(
    embedded,
    segment,
    query_key_value_weight,
    attention_output_weight,
    feedforward_up_weight,
    feedforward_down_weight,
    adapter_down_weight,
    adapter_up_weight,
    layer_norm_gain,
    layer_norm_bias,
    cotangent,
):
    section = lax.axis_index("section")
    tensor = lax.axis_index("tensor")
    parity = lax.rem(lax.axis_index("dp"), 2)
    slots, packs, planes = lax.axis_size("tensor"), segment.shape[0], lax.axis_size("dp")
    assert slots == 4 and packs == slots and planes % 2 == 0
    rows, width = segment.shape[1], embedded.shape[1]
    piece = query_key_value_weight.shape[3]
    wide = feedforward_up_weight.shape[2]
    rank = adapter_down_weight.shape[3]
    span = 256
    groups = width // span
    heads = width // HEAD_DIM
    is_first = (section == 0).astype(jnp.int32)
    meta = jnp.stack([tensor, parity, is_first]).astype(jnp.int32)
    gains, biases = layer_norm_gain[0], layer_norm_bias[0]

    def flip_core(value):
        return lax.ppermute(value, "tensor", [(i, i ^ 1) for i in range(slots)])

    def flip_chip(value):
        return lax.ppermute(value, "tensor", [(i, i ^ 2) for i in range(slots)])

    def flip_section(value):
        return lax.ppermute(value, "section", [(0, 1), (1, 0)])

    def arr(shape, dtype):
        return jax.ShapeDtypeStruct(shape, dtype)

    qkv = jnp.swapaxes(query_key_value_weight[0], 1, 2)
    adapt = adapter_up_weight[0].reshape(2 * rank, piece).T
    adapt_down = jnp.swapaxes(adapter_down_weight[0], 1, 2).reshape(2 * rank, width)
    chunks, hops = 8, rows // 128
    received, bias, adapt_up, qkv_g, out_g, ff_g = pl.pallas_call(
        first_kernel,
        name="first_layer",
        out_shape=[
            arr((rows, width), BF16),
            arr((rows, rows), F32),
            arr((width, 2 * rank), BF16),
            arr((3, width, width), BF16),
            arr((width, width), BF16),
            arr((2, slots, width, wide), BF16),
        ],
        in_specs=[ANY] + [VMEM] * 4 + [ANY] * 5,
        out_specs=[ANY] + [VMEM] * 2 + [ANY] * 3,
        scratch_shapes=[
            pltpu.VMEM((3, width, width), BF16),
            pltpu.VMEM((width, width), BF16),
            pltpu.VMEM((2, slots, width, wide), BF16),
            pltpu.VMEM((rows, width), BF16),
            pltpu.VMEM((rows, width), F32),
            pltpu.VMEM((rows, width), F32),
            pltpu.VMEM((rows, span), BF16),
            pltpu.VMEM((rows, width), BF16),
            pltpu.VMEM((slots, rows, wide), BF16),
            pltpu.VMEM((rows, width), BF16),
            pltpu.SemaphoreType.DMA((9,)),
            pltpu.SemaphoreType.DMA((6, chunks)),
            pltpu.SemaphoreType.DMA((6, chunks)),
            pltpu.SemaphoreType.DMA((hops,)),
            pltpu.SemaphoreType.DMA((hops,)),
        ],
        **params(16 * 10**9, 3 * 10**7, 0),
    )(
        embedded,
        segment,
        gains,
        biases,
        adapt_down,
        adapt,
        qkv,
        attention_output_weight[0],
        feedforward_up_weight[0],
        feedforward_down_weight[0],
    )

    def attention():
        kept_piece = arr((groups, rows, span), BF16)
        return pl.pallas_call(
            attention_kernel,
            name="attention",
            out_shape=[
                arr((rows, width), F32),
                arr((rows, 1), F32),
                kept_piece,
                kept_piece,
                kept_piece,
                arr((heads, rows, rows), BF16),
                arr((2 * rank, rows), BF16),
            ],
            in_specs=[SMEM, ANY, ANY] + [VMEM] * 3 + [ANY] * 2,
            out_specs=[VMEM] * 5 + [ANY, VMEM],
            scratch_shapes=[
                pltpu.VMEM((rows, width), BF16),
                pltpu.VMEM((3, width, width), BF16),
                pltpu.VMEM((width, width), BF16),
                pltpu.VMEM((rows, width), F32),
                pltpu.VMEM((rows, span), BF16),
                pltpu.VMEM((span // HEAD_DIM, rows, rows), BF16),
                pltpu.SemaphoreType.DMA((3,)),
                pltpu.SemaphoreType.DMA((span // HEAD_DIM,)),
            ],
            **params(8 * 10**9, 10**7),
        )(meta, embedded, received, bias, adapt_down, adapt_up, qkv_g, out_g)

    def feedforward(normed):
        return pl.pallas_call(
            feedforward_kernel,
            name="feedforward",
            out_shape=[
                arr((rows, width), BF16),
                arr((rows, width), F32),
                arr((rows, 1), F32),
                arr((slots, rows, wide), BF16),
            ],
            in_specs=[VMEM] * 3 + [ANY],
            out_specs=[VMEM] * 4,
            scratch_shapes=[
                pltpu.VMEM((2, slots, width, wide), BF16),
                pltpu.VMEM((rows, width), BF16),
                pltpu.VMEM((slots, rows, wide), BF16),
                pltpu.SemaphoreType.DMA((2,)),
            ],
            **params(8 * 10**9, 10**7),
        )(normed, gains, biases, ff_g)

    def backward(grads, kept, *extra):
        normed_one, scale_one, q, k, v, p, normed_two, scale_two, slope = kept
        out_shape = [arr((rows, width), BF16)]
        out_specs = [VMEM]
        if grads:
            out_shape += [
                arr((slots, 2 * rank // slots, width), F32),
                arr((groups, 2, rank, span), F32),
                arr((packs * rows, width), BF16),
            ]
            out_specs += [VMEM, VMEM, ANY]
        extra_specs = [ANY] * 3 + [VMEM] + [ANY] * 4 if grads else []
        scratch = [
            pltpu.VMEM((rows, width), BF16),
            pltpu.VMEM((3, width, width), BF16),
            pltpu.VMEM((width, width), BF16),
            pltpu.VMEM((2, slots, width, wide), BF16),
            pltpu.VMEM((heads, rows, rows), BF16),
            pltpu.VMEM((rows, width), F32),
            pltpu.VMEM((rows, width), BF16),
            pltpu.VMEM((slots, rows, wide), BF16),
            pltpu.VMEM((rows, 2 * rank), F32),
            pltpu.SemaphoreType.DMA((6,)),
            pltpu.SemaphoreType.DMA((groups,)),
        ]
        if grads:
            scratch += [
                pltpu.VMEM((rows, width), BF16),
                pltpu.VMEM((slots, rows, width), BF16),
                pltpu.SemaphoreType.DMA((slots,)),
                pltpu.SemaphoreType.DMA((slots,)),
            ]
        return pl.pallas_call(
            partial(backward_kernel, grads),
            name="backward_grads" if grads else "backward",
            out_shape=out_shape,
            in_specs=[SMEM, ANY] + extra_specs + [VMEM] * 9 + [ANY] + [VMEM] * 2 + [ANY] * 3,
            out_specs=out_specs,
            scratch_shapes=scratch,
            **params(18 * 10**9, 3 * 10**7),
        )(
            meta,
            cotangent,
            *extra,
            gains,
            normed_one,
            scale_one,
            normed_two,
            scale_two,
            slope,
            q,
            k,
            v,
            p,
            adapt_down,
            adapt_up,
            qkv_g,
            out_g,
            ff_g,
        )

    normed_one, scale_one, q, k, v, p, mid = attention()
    out, normed_two, scale_two, slope = feedforward(normed_one)
    out_far = flip_chip(out)
    out_blocks = (out, flip_core(out), out_far, flip_core(out_far))
    kept = (normed_one, scale_one, q, k, v, p, normed_two, scale_two, slope)
    (dh,) = backward(False, kept)
    back_received = flip_section(dh)
    dinput, grad_down, grad_up, layer_outs = backward(
        True, kept, back_received, embedded, received, mid, *out_blocks
    )
    grad_up = jnp.moveaxis(grad_up, 0, 2).reshape(2, rank, slots, piece).transpose(2, 0, 1, 3)
    sums = 2 * (slots - 1) + 2 * (planes - 1) + slots - 1
    part = (2 * rank // slots, width)
    in_grads, grad_a, grad_b = pl.pallas_call(
        partial(finish_kernel, planes),
        name="finish",
        out_shape=[
            arr((packs * rows, width), BF16),
            arr((slots, *part), F32),
            arr((2, rank, piece), F32),
        ],
        in_specs=[VMEM] * 3,
        out_specs=[ANY, VMEM, VMEM],
        scratch_shapes=[
            pltpu.VMEM((slots - 1, *part), F32),
            pltpu.VMEM((slots - 1, 2, rank, piece), F32),
            pltpu.VMEM((planes, *part), F32),
            pltpu.VMEM((planes, 2, rank, piece), F32),
            pltpu.SemaphoreType.DMA,
            pltpu.SemaphoreType.DMA((3, 4)),
            pltpu.SemaphoreType.DMA((3, 4)),
            pltpu.SemaphoreType.DMA((sums,)),
            pltpu.SemaphoreType.DMA((sums,)),
        ],
        **params(0, 10**7, 1),
    )(dinput, grad_down, grad_up)
    grad_a = jnp.swapaxes(grad_a.reshape(2, rank, width), 1, 2)
    return (layer_outs[None], in_grads[None], grad_a[None], grad_b[None])


def solution(mesh):
    in_specs = (
        P("dp", None),
        P("dp", None),
        P("section", None, None, "tensor"),
        P("section", "tensor", None),
        P("section", None, "tensor"),
        P("section", "tensor", None),
        P("section", None, None, None),
        P("section", None, None, "tensor"),
        P("section", None, None),
        P("section", None, None),
        P("dp", None),
    )
    out_specs = (
        P("section", "dp", None),
        P("section", "dp", None),
        P("section", None, None, None),
        P("section", None, None, "tensor"),
    )
    return jax.shard_map(local, mesh=mesh, in_specs=in_specs, out_specs=out_specs, check_vma=False)
```

```python
from functools import partial

import jax
import jax.numpy as jnp
from jax import lax
from jax.experimental import pallas as pl
from jax.experimental.pallas import tpu as pltpu
from jax.sharding import PartitionSpec as P

HEAD_DIM = 64
EPS = 1e-05
VMEM_LIMIT = 60 * 2**20
F32 = jnp.float32
BF16 = jnp.bfloat16
ANY = pl.BlockSpec(memory_space=pl.ANY)
VMEM = pl.BlockSpec(memory_space=pltpu.VMEM)
MESH = pl.DeviceIdType.MESH
SMEM = pl.BlockSpec(memory_space=pltpu.SMEM)


def nn(a, b):
    return jnp.dot(a, b, preferred_element_type=F32)


def nt(a, b):
    return lax.dot_general(a, b, (((1,), (1,)), ((), ())), preferred_element_type=F32)


def lane_mask(shape, low, high):
    lanes = lax.broadcasted_iota(jnp.int32, shape, len(shape) - 1)
    return (lanes >= low) & (lanes < high)


def normalize(total):
    average = jnp.mean(total, -1, keepdims=True)
    centred = total - average
    spread = jnp.mean(centred * centred, -1, keepdims=True)
    scaled = lax.rsqrt(spread + EPS)
    return centred * scaled, scaled


def normalize_back(normed, scaled, gains, incoming):
    weighted = incoming * gains
    return scaled * (
        weighted
        - jnp.mean(weighted, -1, keepdims=True)
        - normed * jnp.mean(weighted * normed, -1, keepdims=True)
    )


def neighbours():
    section, plane, tensor = (lax.axis_index(n) for n in ("section", "dp", "tensor"))
    turned = lax.rem(tensor + 2, 4)
    other = tensor + 1 - 2 * lax.rem(tensor, 2)
    paired = plane + 1 - 2 * lax.rem(plane, 2)
    return (
        (section, plane, other),
        (section, plane, turned),
        (section, paired, tensor),
        (1 - section, plane, tensor),
    )


def meet(devices):
    barrier = pltpu.get_barrier_semaphore()
    for device in devices:
        pl.semaphore_signal(barrier, inc=1, device_id=device, device_id_type=MESH)
    pl.semaphore_wait(barrier, len(devices))


def remote(src, dst, send, recv, device):
    return pltpu.make_async_remote_copy(
        src_ref=src,
        dst_ref=dst,
        send_sem=send,
        recv_sem=recv,
        device_id=device,
        device_id_type=MESH,
    )


def identity(n):
    rows = lax.broadcasted_iota(jnp.int32, (n, n), 0)
    return (rows == lax.broadcasted_iota(jnp.int32, (n, n), 1)).astype(BF16)


def blocks_of(rows, size):
    return [pl.ds(r, size) for r in range(0, rows, size)]


class Gather:
    cuts, ahead = 4, 3
    count = 1 + 2 * cuts + 3
    first_qkv = 1 + 2 * cuts

    def __init__(self, own, gathered, partners, sems):
        self.qkv, self.outw, self.up, self.down, self.adapt = own
        self.qkv_v, self.out_v, self.ff_v, self.adapt_v = gathered
        self.core, self.far, self.plane = partners
        self.send, self.recv, self.local = sems
        self.parity = lax.rem(lax.axis_index("dp"), 2)
        self.n_qkv, self.n_out = self.qkv.shape[1], self.outw.shape[0]
        self.n_ff, self.n_adapt = self.up.shape[0], self.adapt.shape[0]

    def part(self, c, slot, p):
        if c == 0:
            half = self.n_out // 2
            return self.out_v.at[pl.ds(slot * self.n_out + p * half, half)]
        if c >= self.first_qkv:
            half = self.n_qkv // 2
            return self.qkv_v.at[c - self.first_qkv, pl.ds(slot * self.n_qkv + p * half, half)]
        which, i = divmod(c - 1, self.cuts)
        half = self.n_ff // 2
        size = half // self.cuts
        return self.ff_v.at[which, slot, pl.ds(p * half + i * size, size)]

    def whole(self, i, slot):
        if i == 0:
            return self.qkv_v.at[:, pl.ds(slot * self.n_qkv, self.n_qkv)]
        if i == 1:
            return self.out_v.at[pl.ds(slot * self.n_out, self.n_out)]
        if i == 4:
            return self.adapt_v.at[pl.ds(slot * self.n_adapt, self.n_adapt)]
        return self.ff_v.at[i - 2, slot]

    def link(self, kind, c, src, dst, device):
        return remote(src, dst, self.send.at[kind, c], self.recv.at[kind, c], device)

    def over_far(self, c):
        return self.link(0, c, self.part(c, 0, self.parity), self.part(c, 2, self.parity), self.far)

    def to_plane(self, c):
        here = self.part(c, 2, self.parity)
        return self.link(1, c, here, here, self.plane)

    def from_plane(self, c):
        there = self.part(c, 2, 1 - self.parity)
        return self.link(1, c, there, there, self.plane)

    def near_to_core(self, c):
        p = self.parity
        return self.link(2, c, self.part(c, 2, p), self.part(c, 3, p), self.core)

    def other_to_core(self, c):
        p = 1 - self.parity
        return self.link(3, c, self.part(c, 2, p), self.part(c, 3, p), self.core)

    def load(self, i):
        own = (self.qkv, self.outw, self.up, self.down, self.adapt)[i]
        return pltpu.make_async_copy(own, self.whole(i, 0), self.local.at[i])

    def to_core(self, i):
        return self.link(4, i, self.whole(i, 0), self.whole(i, 1), self.core)

    def adapt_far(self):
        return self.link(5, 0, self.whole(4, 0), self.whole(4, 2), self.far)

    def adapt_core(self):
        return self.link(5, 1, self.whole(4, 2), self.whole(4, 3), self.core)

    def pump(self, begin, end):
        for c in range(begin, end):
            self.over_far(c).wait_recv()
            self.to_plane(c).start()
            self.near_to_core(c).start()
            if c + self.ahead < self.count:
                self.over_far(c + self.ahead).start()
            if c > 0:
                self.relay(c - 1)

    def relay(self, c):
        self.from_plane(c).wait_recv()
        self.other_to_core(c).start()

    def landed(self, begin, end):
        for c in range(begin, end):
            self.near_to_core(c).wait_recv()
            self.other_to_core(c).wait_recv()

    def sent(self):
        for c in range(self.count):
            for copy in (self.over_far(c), self.to_plane(c)):
                copy.wait_send()
            for copy in (self.near_to_core(c), self.other_to_core(c)):
                copy.wait_send()
        for i in range(5):
            self.to_core(i).wait_send()
        self.adapt_far().wait_send()
        self.adapt_core().wait_send()


def middle(h, adapt_down):
    rank = adapt_down.shape[0] // 2
    mid = nt(h, adapt_down[...]).astype(BF16)
    is_query = lane_mask(mid.shape, 0, rank)
    double = mid * jnp.asarray(2.0, BF16)
    zero = jnp.zeros((), BF16)
    return mid, jnp.where(is_query, double, zero), jnp.where(is_query, zero, double)


def project(h_v, adapt_down, w, ready):
    for part in blocks_of(h_v.shape[0], 256):
        ready(part)
        h = h_v[part]
        mid, mid_q, mid_v = middle(h, adapt_down)
        w.mid_t[:, part] = nt(identity(mid.shape[1]), mid).astype(BF16)
        for s, (ref, low) in enumerate(((w.q_v, mid_q), (w.k_v, None), (w.v_v, mid_v))):
            value = nt(h, w.qkv_v[s])
            if low is not None:
                value = value + nt(low, w.adapt_v[...])
            value = value.astype(BF16)
            span = ref.shape[2]
            for g in range(ref.shape[0]):
                ref[g, part] = value[:, g * span : (g + 1) * span]


def attend(q_v, k, v, bias, give):
    rows, span = k.shape
    chunk = 256
    zero = jnp.zeros((), BF16)
    for part in blocks_of(rows, chunk):
        q_c = q_v[part] * jnp.asarray(HEAD_DIM**-0.5, BF16)
        ctx = jnp.zeros((chunk, span), F32)
        inverse = jnp.zeros((chunk, span), F32)
        weights = []
        for e in range(span // HEAD_DIM):
            low = e * HEAD_DIM
            of_head = lane_mask(q_c.shape, low, low + HEAD_DIM)
            v_e = jnp.where(lane_mask(v.shape, low, low + HEAD_DIM), v, zero)
            s = nt(jnp.where(of_head, q_c, zero), k) + bias[part]
            weight = jnp.exp(s - jnp.max(s, -1, keepdims=True))
            scale = 1.0 / jnp.sum(weight, -1, keepdims=True)
            weight = weight.astype(BF16)
            ctx = ctx + nn(weight, v_e) * scale
            inverse = jnp.where(of_head, scale, inverse)
            give(part, e, weight, None)
        give(part, None, ctx.astype(BF16), inverse)


def attention_out(h_v, context, gains, biases, w, keep):
    groups, rows, span = context.shape
    for part in blocks_of(rows, 256):
        total = h_v[part].astype(F32)
        for g in range(groups):
            total = total + nn(context[g, part], w.out_v[g * span : (g + 1) * span])
        normed, scaled = normalize(total)
        if keep:
            w.n1_v[part] = normed
            w.s1_v[part] = scaled
        first = normed * gains[0:1] + biases[0:1]
        w.acc[part] = first
        w.low_v[part] = first.astype(BF16)


def feedforward_up(w, begin, end, keep):
    def step(slot, carry):
        for part in blocks_of(w.low_v.shape[0], 128):
            pre = nn(w.low_v[part], w.ff_v[0, slot])
            cdf = 0.5 + 0.5 * lax.erf(pre * (0.5**0.5))
            w.act_v[slot, part] = (pre * cdf).astype(BF16)
            if keep:
                density = jnp.exp(pre * pre * -0.5) * 0.3989422804014327
                w.slope_v[slot, part] = (cdf + pre * density).astype(BF16)
        return carry

    lax.fori_loop(begin, end, step, 0)


def backward(w, gains, adapt_down, incoming, give, sums=None):
    rows = w.acc.shape[0]
    slots = w.ff_v.shape[1]
    groups, _, span = w.q_v.shape
    for part in blocks_of(rows, 256):
        back = normalize_back(w.n2_v[part], w.s2_v[part], gains[1:2], incoming(part))
        w.acc[part] = back
        w.low_v[part] = back.astype(BF16)

        def step(slot, carry):
            dact = nt(w.low_v[part], w.ff_v[1, slot])
            w.act_v[slot, part] = (dact * w.slope_v[slot, part].astype(F32)).astype(BF16)
            return carry

        lax.fori_loop(0, slots, step, 0)
        total = w.acc[part]
        for slot in range(slots):
            total = total + nt(w.act_v[slot, part], w.ff_v[0, slot])
        back = normalize_back(w.n1_v[part], w.s1_v[part], gains[0:1], total)
        w.acc[part] = back
        dctx = nt(back.astype(BF16), w.out_v[...])
        for g in range(groups):
            scaled = dctx[:, g * span : (g + 1) * span] * w.inv_v[g, part]
            w.dctx_v[g, part] = scaled.astype(BF16)
    heads = span // HEAD_DIM
    factor = HEAD_DIM**-0.5

    def group(g, carry):
        q, k, v = w.q_v[g], w.k_v[g], w.v_v[g]
        dctx, ctx = w.dctx_v[g], w.ctx_v[g].astype(F32)
        q_t, dctx_t = q.T, dctx.T
        zero = jnp.zeros((), BF16)
        dq = jnp.zeros((rows, span), F32)
        dk_t, dv_t = [], []
        for e in range(heads):
            low, high = e * HEAD_DIM, (e + 1) * HEAD_DIM
            of_head = lane_mask((rows, span), low, high)
            weight = w.p_v[g * heads + e]
            dctx_e = jnp.where(of_head, dctx, zero)
            delta = jnp.sum(dctx_e.astype(F32) * ctx, -1, keepdims=True)
            ds = (weight.astype(F32) * (nt(dctx_e, v) - delta)).astype(BF16)
            dq = dq + nn(ds, jnp.where(of_head, k, zero))
            dk_t.append(nn(q_t[low:high], ds))
            dv_t.append(nn(dctx_t[low:high], weight))
        w.dq_v[g] = (dq * factor).astype(BF16)
        w.dk_v[g] = (jnp.concatenate(dk_t, 0) * factor).astype(BF16).T
        w.dv_v[g] = jnp.concatenate(dv_t, 0).astype(BF16).T
        return carry

    lax.fori_loop(0, groups, group, 0)
    rank = adapt_down.shape[0] // 2
    for part in blocks_of(rows, 256):
        dmid_q = dmid_v = 0.0
        for g in range(groups):
            cols = slice(g * span, (g + 1) * span)
            dmid_q = dmid_q + nn(w.dq_v[g, part], w.adapt_v[cols])
            dmid_v = dmid_v + nn(w.dv_v[g, part], w.adapt_v[cols])
        dmid = 2.0 * jnp.where(lane_mask(dmid_q.shape, 0, rank), dmid_q, dmid_v)
        w.dmid_v[part] = dmid.astype(BF16)
    if sums is not None:
        sums()
    for part in blocks_of(rows, 128):
        total = w.acc[part]
        for g in range(groups):
            cols = slice(g * span, (g + 1) * span)
            for s, ref in enumerate((w.dq_v, w.dk_v, w.dv_v)):
                total = total + nn(ref[g, part], w.qkv_v[s, cols])
        give(part, (total + nn(w.dmid_v[part], adapt_down[...])).astype(BF16))


class Refs:
    def __init__(self, names, refs):
        self.__dict__.update(zip(names, refs, strict=True))


def whole_kernel(planes, names, *refs):
    embedded, segment, gains, biases, adapt_down, adapt, qkv, outw, up, down, cotangent = refs[:11]
    layer_outs, in_grads, down_out, up_out = refs[11:15]
    w = Refs(names, refs[15:])
    section, plane, tensor = (lax.axis_index(n) for n in ("section", "dp", "tensor"))
    core, far, paired, beyond = neighbours()
    turned = lax.rem(tensor + 2, 4)
    other = tensor + 1 - 2 * lax.rem(tensor, 2)
    across = lax.rem(other + 2, 4)
    indices = (other, turned, across)
    sides = tuple((section, plane, i) for i in indices)
    ring = [(section, lax.rem(plane + m, planes), tensor) for m in range(1, planes)]
    rows, width = w.h_v.shape
    groups = w.q_v.shape[0]

    own = pl.ds(tensor * rows, rows)
    gather = Gather(
        (qkv, outw, up, down, w.adapt_own),
        (w.qkv_v, w.out_v, w.ff_v, w.adapt_v),
        (core, far, paired),
        (w.send, w.recv, w.local),
    )
    for i in (1, 0, 2, 3):
        gather.load(i).start()
    pack_copies = [
        pltpu.make_async_copy(embedded.at[pl.ds(i * rows, rows)], w.slope_v.at[i], w.packs.at[i])
        for i in range(len(indices) + 1)
    ]
    for copy in pack_copies:
        copy.start()
    h_copy = pltpu.make_async_copy(embedded.at[own], w.h_v, w.local.at[5])
    h_copy.start()
    cot_copy = pltpu.make_async_copy(cotangent.at[own], w.cot_v, w.local.at[6])
    cot_copy.start()
    adapt_t = nt(identity(adapt.shape[1]), adapt[...]).astype(BF16)
    w.adapt_own[...] = adapt_t
    w.adapt_v[: adapt.shape[1]] = adapt_t
    meet((*sides, *ring, beyond))

    for i in (1, 2, 3, 0):
        gather.load(i).wait()
    for c in range(gather.ahead):
        gather.over_far(c).start()
    gather.adapt_far().start()
    for i in (4, 1, 2, 3, 0):
        gather.to_core(i).start()
    for copy in pack_copies:
        copy.wait()
    square = (rows, rows)
    diagonal = lax.broadcasted_iota(jnp.int32, square, 0) == lax.broadcasted_iota(
        jnp.int32, square, 1
    )
    piece = adapt.shape[1]

    def context_to(k):
        return remote(
            w.ctx_out.at[k], w.ctx_in.at[k], w.ctx_send.at[k], w.ctx_recv.at[k], sides[k - 1]
        )

    for step, k in enumerate((3, 2, 1, 0)):
        pack = (tensor, *indices)[k]
        ids = segment[pl.ds(pack, 1), :].astype(F32)
        column = jnp.sum(jnp.where(diagonal, ids, 0.0), -1, keepdims=True)
        w.bias[...] = jnp.where(column == ids, 0.0, -1e9)
        h = w.slope_v[pack]
        _, mid_q, mid_v = middle(h, adapt_down)
        w.q_own[...] = (nt(h, w.qkv_v[0, :piece]) + nt(mid_q, w.adapt_own[...])).astype(BF16)
        k_own = nt(h, w.qkv_v[1, :piece]).astype(BF16)
        v_own = (nt(h, w.qkv_v[2, :piece]) + nt(mid_v, w.adapt_own[...])).astype(BF16)
        target = w.ctx_out if k else w.ctx_in

        def give(part, head, value, inverse, k=k, target=target):
            if head is None:
                target[k, part] = value

        attend(w.q_own, k_own, v_own, w.bias, give)
        if k:
            context_to(k).start()
        if step:
            gather.pump(step - 1, step)
    h_copy.wait()
    for k in (1, 2, 3):
        context_to(k).wait_recv()
    gather.to_core(1).wait_recv()
    gather.landed(0, 1)
    attention_out(w.h_v, w.ctx_in, gains, biases, w, False)
    gather.adapt_far().wait_recv()
    gather.adapt_core().start()
    ups, downs = 1 + gather.cuts, 1 + 2 * gather.cuts
    gather.pump(3, ups - 1)
    for i in (2, 3):
        gather.to_core(i).wait_recv()
    feedforward_up(w, 0, 2, False)
    gather.pump(ups - 1, ups + 1)
    gather.landed(1, ups)
    feedforward_up(w, 2, 4, False)
    gather.pump(ups + 1, ups + 2)
    for part in blocks_of(rows, 256):
        w.acc[part] += nn(w.act_v[0, part], w.ff_v[1, 0]) + nn(w.act_v[1, part], w.ff_v[1, 1])
    gather.pump(ups + 2, downs + 1)
    gather.landed(ups, downs)

    def hop(way, i, src, dst):
        return remote(src, dst, w.hop_send.at[way, i], w.hop_recv.at[way, i], beyond)

    pieces = blocks_of(rows, 128)
    for i, part in enumerate(pieces):
        total = w.acc[part] + nn(w.act_v[2, part], w.ff_v[1, 2]) + nn(w.act_v[3, part], w.ff_v[1, 3])
        w.hop_v[part] = (normalize(total)[0] * gains[1:2] + biases[1:2]).astype(BF16)
        hop(0, i, w.hop_v.at[part], w.recv_v.at[part]).start()
    gather.pump(downs + 1, gather.count)
    gather.relay(gather.count - 1)
    for i in (0, 4):
        gather.to_core(i).wait_recv()
    gather.adapt_core().wait_recv()
    gather.landed(downs, gather.count)

    def ready(part):
        for i in range(part.start // 128, (part.start + part.size) // 128):
            hop(0, i, w.hop_v.at[pieces[i]], w.recv_v.at[pieces[i]]).wait_recv()

        @pl.when(section == 1)
        def _():
            w.h_v[part] = w.recv_v[part]

    project(w.h_v, adapt_down, w, ready)

    def attend_group(g, carry):
        def give(part, head, value, inverse):
            if head is None:
                w.ctx_v[g, part] = value
                w.inv_v[g, part] = inverse
            else:
                w.p_v[g * (w.q_v.shape[2] // HEAD_DIM) + head, part] = value

        attend(w.q_v.at[g], w.k_v[g], w.v_v[g], w.bias, give)
        return carry

    lax.fori_loop(0, groups, attend_group, 0)
    attention_out(w.h_v, w.ctx_v, gains, biases, w, True)
    feedforward_up(w, 0, 4, True)

    def block(out, index, i):
        return out.at[pl.ds(index * rows + i * 128, 128)]

    def rows_far(n, src, out, i):
        return remote(
            src.at[pieces[i]], block(out, tensor, i), w.row_send.at[n, 0, i], w.row_recv.at[n, 0, i], far
        )

    def rows_core(n, src, out, i):
        return remote(
            src.at[pieces[i]], block(out, tensor, i), w.row_send.at[n, 1, i], w.row_recv.at[n, 1, i], core
        )

    def rows_mine(n, src, out, i):
        return pltpu.make_async_copy(src.at[pieces[i]], block(out, tensor, i), w.local.at[7 + 4 * n + i])

    def rows_relay(n, out, i):
        landed = block(out, turned, i)
        return remote(landed, landed, w.row_send.at[n, 2, i], w.row_recv.at[n, 2, i], core)

    def spread(n, src, out, i):
        for make in (rows_far, rows_core, rows_mine):
            make(n, src, out, i).start()

    def relay_rows(n, src, out, i):
        rows_far(n, src, out, i).wait_recv()
        rows_relay(n, out, i).start()

    def gathered(n, src, out):
        for i in range(len(pieces)):
            rows_core(n, src, out, i).wait_recv()
            rows_relay(n, out, i).wait_recv()
            for make in (rows_far, rows_core):
                make(n, src, out, i).wait_send()
            rows_relay(n, out, i).wait_send()
            rows_mine(n, src, out, i).wait()

    for i, part in enumerate(pieces):
        total = w.acc[part]
        for slot in range(w.ff_v.shape[1]):
            total = total + nn(w.act_v[slot, part], w.ff_v[1, slot])
        normed, scaled = normalize(total)
        w.n2_v[part] = normed
        w.s2_v[part] = scaled
        w.layer_v[part] = (normed * gains[1:2] + biases[1:2]).astype(BF16)
        spread(0, w.layer_v, layer_outs, i)

    cot_copy.wait()

    def hand_over(part, value):
        i = part.start // 128
        w.dh_v[part] = value
        hop(1, i, w.dh_v.at[part], w.back_v.at[part]).start()

    backward(w, gains, adapt_down, lambda part: w.cot_v[part].astype(F32), hand_over)
    for i in range(len(pieces)):
        relay_rows(0, w.layer_v, layer_outs, i)

    def incoming(part):
        for i in range(part.start // 128, (part.start + part.size) // 128):
            hop(1, i, w.dh_v.at[pieces[i]], w.back_v.at[pieces[i]]).wait_recv()
        return jnp.where(section == 0, w.back_v[part], w.cot_v[part]).astype(F32)

    def hand_out(part, value):
        w.din_v[part] = value
        spread(1, w.din_v, in_grads, part.start // 128)

    rank = adapt_down.shape[0] // 2
    tensor_copies = []

    def summed(n, src, dst, device):
        return remote(src, dst, w.sum_send.at[n], w.sum_recv.at[n], device)

    def adapter_gradients():
        dmid_t = nt(identity(2 * rank), w.dmid_v[...]).astype(BF16)
        grad_down = nn(dmid_t, w.h_v[...])
        parts, each, _ = w.grad_down.shape
        for i in range(parts):
            w.grad_down[i] = grad_down[i * each : (i + 1) * each]
        up_q, up_v = (
            jnp.concatenate([2.0 * nn(w.mid_t[...], ref[g]) for g in range(groups)], 1)
            for ref in (w.dq_v, w.dv_v)
        )
        for i in range(parts):
            cols = slice(i * piece, (i + 1) * piece)
            w.grad_up[i, 0] = up_q[:rank, cols]
            w.grad_up[i, 1] = up_v[rank:, cols]
        for i, device in enumerate(sides):
            for src, dst in (
                (w.grad_down.at[indices[i]], w.from_down.at[i]),
                (w.grad_up.at[i + 1], w.from_up.at[i]),
            ):
                tensor_copies.append(summed(len(tensor_copies), src, dst, device))
                tensor_copies[-1].start()

    backward(w, gains, adapt_down, incoming, hand_out, adapter_gradients)
    for copy in tensor_copies:
        copy.wait()
    w.plane_down[plane] = w.grad_down[tensor] + w.from_down[0] + w.from_down[1] + w.from_down[2]
    w.plane_up[plane] = w.grad_up[0] + w.from_up[0] + w.from_up[1] + w.from_up[2]
    base = len(tensor_copies)
    totals = (w.plane_down, w.plane_up)
    for m, device in enumerate(ring):
        for k, ref in enumerate(totals):
            summed(base + 2 * m + k, ref.at[plane], ref.at[plane], device).start()
    relay_rows(1, w.din_v, in_grads, 0)
    for m, device in enumerate(ring):
        source = lax.rem(plane + planes - m - 1, planes)
        for k, ref in enumerate(totals):
            summed(base + 2 * m + k, ref.at[source], ref.at[source], device).wait_recv()
    for m, device in enumerate(ring):
        for k, ref in enumerate(totals):
            summed(base + 2 * m + k, ref.at[plane], ref.at[plane], device).wait_send()
    down_total, up_total = w.plane_down[0], w.plane_up[0]
    for m in range(1, planes):
        down_total = down_total + w.plane_down[m]
        up_total = up_total + w.plane_up[m]
    up_out[...] = up_total
    down_out[tensor] = down_total
    base += 2 * len(ring)
    last = []
    for i, device in enumerate(sides):
        last.append(summed(base + i, down_out.at[tensor], down_out.at[tensor], device))
        last[-1].start()
    for i in range(1, len(pieces)):
        relay_rows(1, w.din_v, in_grads, i)
    for i, device in enumerate(sides):
        landed = down_out.at[indices[i]]
        summed(base + i, landed, landed, device).wait_recv()
    for copy in last:
        copy.wait_send()
    for way, src, dst in ((0, w.hop_v, w.recv_v), (1, w.dh_v, w.back_v)):
        for i, part in enumerate(pieces):
            hop(way, i, src.at[part], dst.at[part]).wait_send()
    gather.sent()
    for k in (1, 2, 3):
        context_to(k).wait_send()
    gathered(0, w.layer_v, layer_outs)
    gathered(1, w.din_v, in_grads)


def local(
    embedded,
    segment,
    query_key_value_weight,
    attention_output_weight,
    feedforward_up_weight,
    feedforward_down_weight,
    adapter_down_weight,
    adapter_up_weight,
    layer_norm_gain,
    layer_norm_bias,
    cotangent,
):
    slots, packs, planes = lax.axis_size("tensor"), segment.shape[0], lax.axis_size("dp")
    assert slots == 4 and packs == slots and planes % 2 == 0
    rows, width = segment.shape[1], embedded.shape[1]
    piece = query_key_value_weight.shape[3]
    wide = feedforward_up_weight.shape[2]
    assert wide == width
    rank = adapter_down_weight.shape[3]
    span = 256
    groups = width // span
    heads = width // HEAD_DIM

    def arr(shape, dtype):
        return jax.ShapeDtypeStruct(shape, dtype)

    low_rows = pltpu.VMEM((rows, width), BF16)
    full_rows = pltpu.VMEM((rows, width), F32)
    of_heads = pltpu.VMEM((groups, rows, span), BF16)
    of_hidden = pltpu.VMEM((slots, rows, wide), BF16)
    down_part = (2 * rank // slots, width)
    up_part = (2, rank, piece)
    sums = 2 * (slots - 1) + 2 * (planes - 1) + slots - 1
    scratch = dict(
        qkv_v=pltpu.VMEM((3, width, width), BF16),
        out_v=pltpu.VMEM((width, width), BF16),
        ff_v=pltpu.VMEM((2, slots, width, wide), BF16),
        adapt_v=pltpu.VMEM((width, 2 * rank), BF16),
        adapt_own=pltpu.VMEM((piece, 2 * rank), BF16),
        q_own=pltpu.VMEM((rows, piece), BF16),
        ctx_out=pltpu.VMEM((slots, rows, piece), BF16),
        ctx_in=pltpu.VMEM((slots, rows, piece), BF16),
        inv_v=pltpu.VMEM((groups, rows, span), F32),
        p_v=pltpu.VMEM((heads, rows, rows), BF16),
        s1_v=pltpu.VMEM((rows, 1), F32),
        s2_v=pltpu.VMEM((rows, 1), F32),
        bias=pltpu.VMEM((rows, rows), F32),
        mid_t=pltpu.VMEM((2 * rank, rows), BF16),
        dmid_v=pltpu.VMEM((rows, 2 * rank), BF16),
        grad_down=pltpu.VMEM((slots, *down_part), F32),
        grad_up=pltpu.VMEM((slots, *up_part), F32),
        from_down=pltpu.VMEM((slots - 1, *down_part), F32),
        from_up=pltpu.VMEM((slots - 1, *up_part), F32),
        plane_down=pltpu.VMEM((planes, *down_part), F32),
        plane_up=pltpu.VMEM((planes, *up_part), F32),
        local=pltpu.SemaphoreType.DMA((15,)),
        packs=pltpu.SemaphoreType.DMA((packs,)),
        send=pltpu.SemaphoreType.DMA((6, Gather.count)),
        recv=pltpu.SemaphoreType.DMA((6, Gather.count)),
        ctx_send=pltpu.SemaphoreType.DMA((slots,)),
        ctx_recv=pltpu.SemaphoreType.DMA((slots,)),
        hop_send=pltpu.SemaphoreType.DMA((2, rows // 128)),
        hop_recv=pltpu.SemaphoreType.DMA((2, rows // 128)),
        row_send=pltpu.SemaphoreType.DMA((2, 3, rows // 128)),
        row_recv=pltpu.SemaphoreType.DMA((2, 3, rows // 128)),
        sum_send=pltpu.SemaphoreType.DMA((sums,)),
        sum_recv=pltpu.SemaphoreType.DMA((sums,)),
    )
    scratch |= dict.fromkeys(("h_v", "recv_v", "back_v", "cot_v", "low_v"), low_rows)
    scratch |= dict.fromkeys(("hop_v", "layer_v", "dh_v", "din_v"), low_rows)
    scratch |= dict.fromkeys(("acc", "n1_v", "n2_v"), full_rows)
    scratch |= dict.fromkeys(("q_v", "k_v", "v_v", "ctx_v"), of_heads)
    scratch |= dict.fromkeys(("dq_v", "dk_v", "dv_v", "dctx_v"), of_heads)
    scratch |= dict.fromkeys(("act_v", "slope_v"), of_hidden)
    layer_outs, in_grads, grad_a, grad_b = pl.pallas_call(
        partial(whole_kernel, planes, tuple(scratch)),
        name="encoder_layers",
        out_shape=[
            arr((packs * rows, width), BF16),
            arr((packs * rows, width), BF16),
            arr((slots, *down_part), F32),
            arr(up_part, F32),
        ],
        in_specs=[ANY] + [VMEM] * 5 + [ANY] * 5,
        out_specs=[ANY] * 2 + [VMEM] * 2,
        scratch_shapes=list(scratch.values()),
        compiler_params=pltpu.CompilerParams(
            vmem_limit_bytes=VMEM_LIMIT, collective_id=0, has_side_effects=True
        ),
        cost_estimate=pl.CostEstimate(
            flops=7 * 10**10, bytes_accessed=3 * 10**7, transcendentals=0
        ),
    )(
        embedded,
        segment,
        layer_norm_gain[0],
        layer_norm_bias[0],
        jnp.swapaxes(adapter_down_weight[0], 1, 2).reshape(2 * rank, width),
        adapter_up_weight[0].reshape(2 * rank, piece),
        jnp.swapaxes(query_key_value_weight[0], 1, 2),
        attention_output_weight[0],
        feedforward_up_weight[0],
        feedforward_down_weight[0],
        cotangent,
    )
    grad_a = jnp.swapaxes(grad_a.reshape(2, rank, width), 1, 2)
    return (layer_outs[None], in_grads[None], grad_a[None], grad_b[None])


def solution(mesh):
    in_specs = (
        P("dp", None),
        P("dp", None),
        P("section", None, None, "tensor"),
        P("section", "tensor", None),
        P("section", None, "tensor"),
        P("section", "tensor", None),
        P("section", None, None, None),
        P("section", None, None, "tensor"),
        P("section", None, None),
        P("section", None, None),
        P("dp", None),
    )
    out_specs = (
        P("section", "dp", None),
        P("section", "dp", None),
        P("section", None, None, None),
        P("section", None, None, "tensor"),
    )
    return jax.shard_map(local, mesh=mesh, in_specs=in_specs, out_specs=out_specs, check_vma=False)
```

```python
from functools import partial

import jax
import jax.numpy as jnp
from jax import lax
from jax.experimental import pallas as pl
from jax.experimental.pallas import tpu as pltpu
from jax.sharding import PartitionSpec as P

HEAD_DIM = 64
EPS = 1e-05
VMEM_LIMIT = 115 * 2**19
F32 = jnp.float32
BF16 = jnp.bfloat16
ANY = pl.BlockSpec(memory_space=pl.ANY)
VMEM = pl.BlockSpec(memory_space=pltpu.VMEM)
MESH = pl.DeviceIdType.MESH
SMEM = pl.BlockSpec(memory_space=pltpu.SMEM)


def nn(a, b):
    return jnp.dot(a, b, preferred_element_type=F32)


def nt(a, b):
    return lax.dot_general(a, b, (((1,), (1,)), ((), ())), preferred_element_type=F32)


def lane_mask(shape, low, high):
    lanes = lax.broadcasted_iota(jnp.int32, shape, len(shape) - 1)
    return (lanes >= low) & (lanes < high)


def normalize(total):
    average = jnp.mean(total, -1, keepdims=True)
    centred = total - average
    spread = jnp.mean(centred * centred, -1, keepdims=True)
    scaled = lax.rsqrt(spread + EPS)
    return centred * scaled, scaled


def normalize_back(normed, scaled, gains, incoming):
    weighted = incoming * gains
    return scaled * (
        weighted
        - jnp.mean(weighted, -1, keepdims=True)
        - normed * jnp.mean(weighted * normed, -1, keepdims=True)
    )


def neighbours():
    section, plane, tensor = (lax.axis_index(n) for n in ("section", "dp", "tensor"))
    turned = lax.rem(tensor + 2, 4)
    other = tensor + 1 - 2 * lax.rem(tensor, 2)
    paired = plane + 1 - 2 * lax.rem(plane, 2)
    return (
        (section, plane, other),
        (section, plane, turned),
        (section, paired, tensor),
        (1 - section, plane, tensor),
    )


def meet(devices):
    barrier = pltpu.get_barrier_semaphore()
    for device in devices:
        pl.semaphore_signal(barrier, inc=1, device_id=device, device_id_type=MESH)
    pl.semaphore_wait(barrier, len(devices))


def remote(src, dst, send, recv, device):
    return pltpu.make_async_remote_copy(
        src_ref=src,
        dst_ref=dst,
        send_sem=send,
        recv_sem=recv,
        device_id=device,
        device_id_type=MESH,
    )


def identity(n):
    rows = lax.broadcasted_iota(jnp.int32, (n, n), 0)
    return (rows == lax.broadcasted_iota(jnp.int32, (n, n), 1)).astype(BF16)


def blocks_of(rows, size):
    return [pl.ds(r, size) for r in range(0, rows, size)]


class Gather:
    cuts, ahead = 4, 3
    count = 1 + 2 * cuts + 3
    first_qkv = 1 + 2 * cuts

    def __init__(self, own, gathered, partners, sems):
        self.qkv, self.outw, self.up, self.down, self.adapt = own
        self.qkv_v, self.out_v, self.ff_v, self.adapt_v = gathered
        self.core, self.far, self.plane = partners
        self.send, self.recv, self.local = sems
        self.parity = lax.rem(lax.axis_index("dp"), 2)
        self.n_qkv, self.n_out = self.qkv.shape[1], self.outw.shape[0]
        self.n_ff, self.n_adapt = self.up.shape[0], self.adapt.shape[0]

    def part(self, c, slot, p):
        if c == 0:
            half = self.n_out // 2
            return self.out_v.at[pl.ds(slot * self.n_out + p * half, half)]
        if c >= self.first_qkv:
            half = self.n_qkv // 2
            return self.qkv_v.at[c - self.first_qkv, pl.ds(slot * self.n_qkv + p * half, half)]
        which, i = divmod(c - 1, self.cuts)
        half = self.n_ff // 2
        size = half // self.cuts
        return self.ff_v.at[which, slot, pl.ds(p * half + i * size, size)]

    def whole(self, i, slot):
        if i == 0:
            return self.qkv_v.at[:, pl.ds(slot * self.n_qkv, self.n_qkv)]
        if i == 1:
            return self.out_v.at[pl.ds(slot * self.n_out, self.n_out)]
        if i == 4:
            return self.adapt_v.at[pl.ds(slot * self.n_adapt, self.n_adapt)]
        return self.ff_v.at[i - 2, slot]

    def link(self, kind, c, src, dst, device):
        return remote(src, dst, self.send.at[kind, c], self.recv.at[kind, c], device)

    def over_far(self, c):
        return self.link(0, c, self.part(c, 0, self.parity), self.part(c, 2, self.parity), self.far)

    def to_plane(self, c):
        here = self.part(c, 2, self.parity)
        return self.link(1, c, here, here, self.plane)

    def from_plane(self, c):
        there = self.part(c, 2, 1 - self.parity)
        return self.link(1, c, there, there, self.plane)

    def near_to_core(self, c):
        p = self.parity
        return self.link(2, c, self.part(c, 2, p), self.part(c, 3, p), self.core)

    def other_to_core(self, c):
        p = 1 - self.parity
        return self.link(3, c, self.part(c, 2, p), self.part(c, 3, p), self.core)

    def load(self, i):
        own = (self.qkv, self.outw, self.up, self.down, self.adapt)[i]
        return pltpu.make_async_copy(own, self.whole(i, 0), self.local.at[i])

    def to_core(self, i):
        return self.link(4, i, self.whole(i, 0), self.whole(i, 1), self.core)

    def adapt_far(self):
        return self.link(5, 0, self.whole(4, 0), self.whole(4, 2), self.far)

    def adapt_core(self):
        return self.link(5, 1, self.whole(4, 2), self.whole(4, 3), self.core)

    def pump(self, begin, end):
        for c in range(begin, end):
            self.over_far(c).wait_recv()
            self.to_plane(c).start()
            self.near_to_core(c).start()
            if c + self.ahead < self.count:
                self.over_far(c + self.ahead).start()
            if c > 0:
                self.relay(c - 1)

    def relay(self, c):
        self.from_plane(c).wait_recv()
        self.other_to_core(c).start()

    def landed(self, begin, end):
        for c in range(begin, end):
            self.near_to_core(c).wait_recv()
            self.other_to_core(c).wait_recv()

    def sent(self):
        for c in range(self.count):
            for copy in (self.over_far(c), self.to_plane(c)):
                copy.wait_send()
            for copy in (self.near_to_core(c), self.other_to_core(c)):
                copy.wait_send()
        for i in range(5):
            self.to_core(i).wait_send()
        self.adapt_far().wait_send()
        self.adapt_core().wait_send()


def middle(h, adapt_down):
    rank = adapt_down.shape[0] // 2
    mid = nt(h, adapt_down[...]).astype(BF16)
    is_query = lane_mask(mid.shape, 0, rank)
    double = mid * jnp.asarray(2.0, BF16)
    zero = jnp.zeros((), BF16)
    return mid, jnp.where(is_query, double, zero), jnp.where(is_query, zero, double)


def project(h_v, adapt_down, w, ready):
    for part in blocks_of(h_v.shape[0], 256):
        ready(part)
        h = h_v[part]
        mid, mid_q, mid_v = middle(h, adapt_down)
        w.mid_t[:, part] = nt(identity(mid.shape[1]), mid).astype(BF16)
        for s, (ref, low) in enumerate(((w.q_v, mid_q), (w.k_v, None), (w.v_v, mid_v))):
            value = nt(h, w.qkv_v[s])
            if low is not None:
                value = value + nt(low, w.adapt_v[...])
            value = value.astype(BF16)
            span = ref.shape[2]
            for g in range(ref.shape[0]):
                ref[g, part] = value[:, g * span : (g + 1) * span]


def attend(q_v, k, v, bias, give):
    rows, span = k.shape
    chunk = 256
    zero = jnp.zeros((), BF16)
    for part in blocks_of(rows, chunk):
        q_c = q_v[part] * jnp.asarray(HEAD_DIM**-0.5, BF16)
        ctx = jnp.zeros((chunk, span), F32)
        inverse = jnp.zeros((chunk, span), F32)
        weights = []
        for e in range(span // HEAD_DIM):
            low = e * HEAD_DIM
            of_head = lane_mask(q_c.shape, low, low + HEAD_DIM)
            v_e = jnp.where(lane_mask(v.shape, low, low + HEAD_DIM), v, zero)
            s = nt(jnp.where(of_head, q_c, zero), k) + bias[part]
            weight = jnp.exp(s - jnp.max(s, -1, keepdims=True))
            scale = 1.0 / jnp.sum(weight, -1, keepdims=True)
            weight = weight.astype(BF16)
            ctx = ctx + nn(weight, v_e) * scale
            inverse = jnp.where(of_head, scale, inverse)
            give(part, e, weight, None)
        give(part, None, ctx.astype(BF16), inverse)


def attention_out(h_v, context, gains, biases, w, keep):
    groups, rows, span = context.shape
    for part in blocks_of(rows, 256):
        total = h_v[part].astype(F32)
        for g in range(groups):
            total = total + nn(context[g, part], w.out_v[g * span : (g + 1) * span])
        normed, scaled = normalize(total)
        if keep:
            w.n1_v[part] = normed
            w.s1_v[part] = scaled
        first = normed * gains[0:1] + biases[0:1]
        w.acc[part] = first
        w.low_v[part] = first.astype(BF16)


def feedforward_up(w, keep, ready):
    def step(slot, carry):
        ready(slot)
        for part in blocks_of(w.low_v.shape[0], 128):
            pre = nn(w.low_v[part], w.ff_v[0, slot])
            cdf = 0.5 + 0.5 * lax.erf(pre * (0.5**0.5))
            w.act_v[slot, part] = (pre * cdf).astype(BF16)
            if keep:
                density = jnp.exp(pre * pre * -0.5) * 0.3989422804014327
                w.slope_v[slot, part] = (cdf + pre * density).astype(BF16)
        return carry

    lax.fori_loop(0, w.act_v.shape[0], step, 0)


def backward(w, gains, adapt_down, incoming, give, sums):
    rows = w.acc.shape[0]
    slots = w.ff_v.shape[1]
    groups, _, span = w.q_v.shape
    for part in blocks_of(rows, 256):
        back = normalize_back(w.n2_v[part], w.s2_v[part], gains[1:2], incoming(part))
        w.acc[part] = back
        w.low_v[part] = back.astype(BF16)

        def step(slot, carry):
            dact = nt(w.low_v[part], w.ff_v[1, slot])
            w.act_v[slot, part] = (dact * w.slope_v[slot, part].astype(F32)).astype(BF16)
            return carry

        lax.fori_loop(0, slots, step, 0)
        total = w.acc[part]
        for slot in range(slots):
            total = total + nt(w.act_v[slot, part], w.ff_v[0, slot])
        back = normalize_back(w.n1_v[part], w.s1_v[part], gains[0:1], total)
        w.acc[part] = back
        dctx = nt(back.astype(BF16), w.out_v[...])
        for g in range(groups):
            scaled = dctx[:, g * span : (g + 1) * span] * w.inv_v[g, part]
            w.dctx_v[g, part] = scaled.astype(BF16)
    heads = span // HEAD_DIM
    factor = HEAD_DIM**-0.5

    def group(g, carry):
        q, k, v = w.q_v[g], w.k_v[g], w.v_v[g]
        dctx, ctx = w.dctx_v[g], w.ctx_v[g].astype(F32)
        q_t, dctx_t = q.T, dctx.T
        zero = jnp.zeros((), BF16)
        dq = jnp.zeros((rows, span), F32)
        dk_t, dv_t = [], []
        for e in range(heads):
            low, high = e * HEAD_DIM, (e + 1) * HEAD_DIM
            of_head = lane_mask((rows, span), low, high)
            weight = w.p_v[g * heads + e]
            dctx_e = jnp.where(of_head, dctx, zero)
            delta = jnp.sum(dctx_e.astype(F32) * ctx, -1, keepdims=True)
            ds = (weight.astype(F32) * (nt(dctx_e, v) - delta)).astype(BF16)
            dq = dq + nn(ds, jnp.where(of_head, k, zero))
            dk_t.append(nn(q_t[low:high], ds))
            dv_t.append(nn(dctx_t[low:high], weight))
        w.dq_v[g] = (dq * factor).astype(BF16)
        w.dk_v[g] = (jnp.concatenate(dk_t, 0) * factor).astype(BF16).T
        w.dv_v[g] = jnp.concatenate(dv_t, 0).astype(BF16).T
        return carry

    lax.fori_loop(0, groups, group, 0)
    rank = adapt_down.shape[0] // 2
    for part in blocks_of(rows, 256):
        dmid_q = dmid_v = 0.0
        for g in range(groups):
            cols = slice(g * span, (g + 1) * span)
            dmid_q = dmid_q + nn(w.dq_v[g, part], w.adapt_v[cols])
            dmid_v = dmid_v + nn(w.dv_v[g, part], w.adapt_v[cols])
        dmid = 2.0 * jnp.where(lane_mask(dmid_q.shape, 0, rank), dmid_q, dmid_v)
        w.dmid_v[part] = dmid.astype(BF16)
    sums()
    for part in blocks_of(rows, 128):
        total = w.acc[part]
        for g in range(groups):
            cols = slice(g * span, (g + 1) * span)
            for s, ref in enumerate((w.dq_v, w.dk_v, w.dv_v)):
                total = total + nn(ref[g, part], w.qkv_v[s, cols])
        give(part, (total + nn(w.dmid_v[part], adapt_down[...])).astype(BF16))


class Refs:
    def __init__(self, names, refs):
        self.__dict__.update(zip(names, refs, strict=True))


def whole_kernel(planes, names, *refs):
    embedded, segment, gains, biases, adapt_down, adapt, qkv, outw, up, down, cotangent = refs[:11]
    layer_outs, in_grads, down_out, up_out = refs[11:15]
    w = Refs(names, refs[15:])
    section, plane, tensor = (lax.axis_index(n) for n in ("section", "dp", "tensor"))
    core, far, paired, beyond = neighbours()
    turned = lax.rem(tensor + 2, 4)
    other = tensor + 1 - 2 * lax.rem(tensor, 2)
    across = lax.rem(other + 2, 4)
    indices = (other, turned, across)
    sides = tuple((section, plane, i) for i in indices)
    ring = [(section, lax.rem(plane + m, planes), tensor) for m in range(1, planes)]
    rows, width = w.h_v.shape
    groups = w.q_v.shape[0]

    own = pl.ds(tensor * rows, rows)
    gather = Gather(
        (qkv, outw, up, down, w.adapt_own),
        (w.qkv_v, w.out_v, w.ff_v, w.adapt_v),
        (core, far, paired),
        (w.send, w.recv, w.local),
    )
    for i in (1, 0, 2, 3):
        gather.load(i).start()
    pack_copies = [
        pltpu.make_async_copy(embedded.at[pl.ds(i * rows, rows)], w.slope_v.at[i], w.packs.at[i])
        for i in range(len(indices) + 1)
    ]
    for copy in pack_copies:
        copy.start()
    h_copy = pltpu.make_async_copy(embedded.at[own], w.h_v, w.local.at[5])
    h_copy.start()
    cot_copy = pltpu.make_async_copy(cotangent.at[own], w.cot_v, w.local.at[6])
    cot_copy.start()
    adapt_t = nt(identity(adapt.shape[1]), adapt[...]).astype(BF16)
    w.adapt_own[...] = adapt_t
    w.adapt_v[: adapt.shape[1]] = adapt_t
    meet((*sides, *ring, beyond))

    for i in (1, 2, 3, 0):
        gather.load(i).wait()
    for c in range(gather.ahead):
        gather.over_far(c).start()
    gather.adapt_far().start()
    for i in (4, 1, 2, 3, 0):
        gather.to_core(i).start()
    for copy in pack_copies:
        copy.wait()
    square = (rows, rows)
    diagonal = lax.broadcasted_iota(jnp.int32, square, 0) == lax.broadcasted_iota(
        jnp.int32, square, 1
    )
    piece = adapt.shape[1]

    def index_of(k):
        high = lax.rem(tensor // 2 + k // 2, 2)
        return 2 * high + lax.rem(lax.rem(tensor, 2) + lax.rem(k, 2), 2)

    def context_to(k):
        device = (section, plane, index_of(k))
        return remote(w.ctx_out.at[k], w.ctx_in.at[k], w.ctx_send.at[k], w.ctx_recv.at[k], device)

    def attend_pack(step, carry):
        k = 3 - step
        pack = index_of(k)
        ids = segment[pl.ds(pack, 1), :].astype(F32)
        column = jnp.sum(jnp.where(diagonal, ids, 0.0), -1, keepdims=True)
        w.bias[...] = jnp.where(column == ids, 0.0, -1e9)
        h = w.slope_v[pack]
        _, mid_q, mid_v = middle(h, adapt_down)
        w.q_own[...] = (nt(h, w.qkv_v[0, :piece]) + nt(mid_q, w.adapt_own[...])).astype(BF16)
        k_own = nt(h, w.qkv_v[1, :piece]).astype(BF16)
        v_own = (nt(h, w.qkv_v[2, :piece]) + nt(mid_v, w.adapt_own[...])).astype(BF16)

        def give(part, head, value, inverse):
            if head is None:
                w.ctx_out[k, part] = value

        attend(w.q_own, k_own, v_own, w.bias, give)

        @pl.when(step < 3)
        def _():
            context_to(k).start()

        for i in (1, 2, 3):

            @pl.when(step == i)
            def _():
                gather.pump(i - 1, i)

        return carry

    lax.fori_loop(0, 4, attend_pack, 0)
    w.ctx_in[0] = w.ctx_out[0]
    h_copy.wait()
    for k in (1, 2, 3):
        context_to(k).wait_recv()
    gather.to_core(1).wait_recv()
    gather.landed(0, 1)
    attention_out(w.h_v, w.ctx_in, gains, biases, w, False)
    gather.adapt_far().wait_recv()
    gather.adapt_core().start()
    ups, downs = 1 + gather.cuts, 1 + 2 * gather.cuts
    gather.pump(3, ups - 1)
    for i in (2, 3):
        gather.to_core(i).wait_recv()

    def rest_of_up(slot):
        @pl.when(slot == 2)
        def _():
            gather.pump(ups - 1, ups + 1)
            gather.landed(1, ups)

    feedforward_up(w, False, rest_of_up)
    gather.pump(ups + 1, ups + 2)
    for part in blocks_of(rows, 256):
        w.acc[part] += nn(w.act_v[0, part], w.ff_v[1, 0]) + nn(w.act_v[1, part], w.ff_v[1, 1])
    gather.pump(ups + 2, downs + 1)
    gather.landed(ups, downs)

    def hop(way, i, src, dst):
        return remote(src, dst, w.hop_send.at[way, i], w.hop_recv.at[way, i], beyond)

    pieces = blocks_of(rows, 128)
    for i, part in enumerate(pieces):
        total = w.acc[part] + nn(w.act_v[2, part], w.ff_v[1, 2]) + nn(w.act_v[3, part], w.ff_v[1, 3])
        w.hop_v[part] = (normalize(total)[0] * gains[1:2] + biases[1:2]).astype(BF16)
        hop(0, i, w.hop_v.at[part], w.recv_v.at[part]).start()
    gather.pump(downs + 1, gather.count)
    gather.relay(gather.count - 1)
    for i in (0, 4):
        gather.to_core(i).wait_recv()
    gather.adapt_core().wait_recv()
    gather.landed(downs, gather.count)

    def ready(part):
        for i in range(part.start // 128, (part.start + part.size) // 128):
            hop(0, i, w.hop_v.at[pieces[i]], w.recv_v.at[pieces[i]]).wait_recv()

        @pl.when(section == 1)
        def _():
            w.h_v[part] = w.recv_v[part]

    project(w.h_v, adapt_down, w, ready)

    def attend_group(g, carry):
        def give(part, head, value, inverse):
            if head is None:
                w.ctx_v[g, part] = value
                w.inv_v[g, part] = inverse
            else:
                w.p_v[g * (w.q_v.shape[2] // HEAD_DIM) + head, part] = value

        attend(w.q_v.at[g], w.k_v[g], w.v_v[g], w.bias, give)
        return carry

    lax.fori_loop(0, groups, attend_group, 0)
    attention_out(w.h_v, w.ctx_v, gains, biases, w, True)
    feedforward_up(w, True, lambda slot: None)

    def block(out, index, i):
        return out.at[pl.ds(index * rows + i * 128, 128)]

    def rows_far(n, src, out, i):
        return remote(
            src.at[pieces[i]], block(out, tensor, i), w.row_send.at[n, 0, i], w.row_recv.at[n, 0, i], far
        )

    def rows_core(n, src, out, i):
        return remote(
            src.at[pieces[i]], block(out, tensor, i), w.row_send.at[n, 1, i], w.row_recv.at[n, 1, i], core
        )

    def rows_mine(n, src, out, i):
        return pltpu.make_async_copy(src.at[pieces[i]], block(out, tensor, i), w.local.at[7 + 4 * n + i])

    def rows_relay(n, out, i):
        landed = block(out, turned, i)
        return remote(landed, landed, w.row_send.at[n, 2, i], w.row_recv.at[n, 2, i], core)

    def spread(n, src, out, i):
        for make in (rows_far, rows_core, rows_mine):
            make(n, src, out, i).start()

    def relay_rows(n, src, out, i):
        rows_far(n, src, out, i).wait_recv()
        rows_relay(n, out, i).start()

    def gathered(n, src, out):
        for i in range(len(pieces)):
            rows_core(n, src, out, i).wait_recv()
            rows_relay(n, out, i).wait_recv()
            for make in (rows_far, rows_core):
                make(n, src, out, i).wait_send()
            rows_relay(n, out, i).wait_send()
            rows_mine(n, src, out, i).wait()

    for i, part in enumerate(pieces):
        total = w.acc[part]
        for slot in range(w.ff_v.shape[1]):
            total = total + nn(w.act_v[slot, part], w.ff_v[1, slot])
        normed, scaled = normalize(total)
        w.n2_v[part] = normed
        w.s2_v[part] = scaled
        w.layer_v[part] = (normed * gains[1:2] + biases[1:2]).astype(BF16)
        spread(0, w.layer_v, layer_outs, i)

    cot_copy.wait()
    rank = adapt_down.shape[0] // 2

    def incoming(again, part):
        @pl.when(again == 1)
        def _():
            for i in range(part.start // 128, (part.start + part.size) // 128):
                hop(1, i, w.dh_v.at[pieces[i]], w.back_v.at[pieces[i]]).wait_recv()

        @pl.when(jnp.logical_and(again == 1, section == 0))
        def _():
            w.cot_v[part] = w.back_v[part]

        return w.cot_v[part].astype(F32)

    def summed(n, src, dst, device):
        return remote(src, dst, w.sum_send.at[n], w.sum_recv.at[n], device)

    def over_tensor(landing):
        copies = []
        for i, device in enumerate(sides):
            slot = indices[i] if landing else tensor
            for src, dst in (
                (w.grad_down, w.from_down.at[slot]),
                (w.grad_up.at[i + 1], w.from_up.at[i]),
            ):
                copies.append(summed(len(copies), src, dst, device))
        return copies

    def adapter_gradients(again):
        @pl.when(again == 1)
        def _():
            dmid_t = nt(identity(2 * rank), w.dmid_v[...]).astype(BF16)
            grad_down = nn(dmid_t, w.h_v[...])
            for j in range(2):
                w.grad_down[j] = grad_down[j * rank : (j + 1) * rank]
            up_q, up_v = (
                jnp.concatenate([2.0 * nn(w.mid_t[...], ref[g]) for g in range(groups)], 1)
                for ref in (w.dq_v, w.dv_v)
            )
            for i in range(len(sides) + 1):
                cols = slice(i * piece, (i + 1) * piece)
                w.grad_up[i, 0] = up_q[:rank, cols]
                w.grad_up[i, 1] = up_v[rank:, cols]
            w.from_down[tensor] = w.grad_down[...]
            for copy in over_tensor(False):
                copy.start()

    def hand_over(again, part, value):
        i = part.start // 128

        @pl.when(again == 0)
        def _():
            w.dh_v[part] = value
            hop(1, i, w.dh_v.at[part], w.back_v.at[part]).start()

        @pl.when(again == 1)
        def _():
            w.din_v[part] = value
            spread(1, w.din_v, in_grads, i)

    def back(again, carry):
        backward(
            w,
            gains,
            adapt_down,
            partial(incoming, again),
            partial(hand_over, again),
            partial(adapter_gradients, again),
        )

        @pl.when(again == 0)
        def _():
            for i in range(len(pieces)):
                relay_rows(0, w.layer_v, layer_outs, i)

        return carry

    lax.fori_loop(0, 2, back, 0)

    tensor_copies = over_tensor(True)
    for copy in tensor_copies:
        copy.wait()
    w.plane_down[plane] = w.from_down[0] + w.from_down[1] + w.from_down[2] + w.from_down[3]
    w.plane_up[plane] = w.grad_up[0] + w.from_up[0] + w.from_up[1] + w.from_up[2]
    base = len(tensor_copies)
    totals = (w.plane_down, w.plane_up)
    for m, device in enumerate(ring):
        for k, ref in enumerate(totals):
            summed(base + 2 * m + k, ref.at[plane], ref.at[plane], device).start()
    relay_rows(1, w.din_v, in_grads, 0)
    for m, device in enumerate(ring):
        source = lax.rem(plane + planes - m - 1, planes)
        for k, ref in enumerate(totals):
            summed(base + 2 * m + k, ref.at[source], ref.at[source], device).wait_recv()
    for m, device in enumerate(ring):
        for k, ref in enumerate(totals):
            summed(base + 2 * m + k, ref.at[plane], ref.at[plane], device).wait_send()
    down_total, up_total = w.plane_down[0], w.plane_up[0]
    for m in range(1, planes):
        down_total = down_total + w.plane_down[m]
        up_total = up_total + w.plane_up[m]
    up_out[...] = up_total
    down_out[...] = down_total
    for i in range(1, len(pieces)):
        relay_rows(1, w.din_v, in_grads, i)
    for way, src, dst in ((0, w.hop_v, w.recv_v), (1, w.dh_v, w.back_v)):
        for i, part in enumerate(pieces):
            hop(way, i, src.at[part], dst.at[part]).wait_send()
    gather.sent()
    for k in (1, 2, 3):
        context_to(k).wait_send()
    gathered(0, w.layer_v, layer_outs)
    gathered(1, w.din_v, in_grads)


def local(
    embedded,
    segment,
    query_key_value_weight,
    attention_output_weight,
    feedforward_up_weight,
    feedforward_down_weight,
    adapter_down_weight,
    adapter_up_weight,
    layer_norm_gain,
    layer_norm_bias,
    cotangent,
):
    slots, packs, planes = lax.axis_size("tensor"), segment.shape[0], lax.axis_size("dp")
    assert slots == 4 and packs == slots and planes % 2 == 0
    rows, width = segment.shape[1], embedded.shape[1]
    piece = query_key_value_weight.shape[3]
    wide = feedforward_up_weight.shape[2]
    assert wide == width
    rank = adapter_down_weight.shape[3]
    span = 256
    groups = width // span
    heads = width // HEAD_DIM

    def arr(shape, dtype):
        return jax.ShapeDtypeStruct(shape, dtype)

    low_rows = pltpu.VMEM((rows, width), BF16)
    full_rows = pltpu.VMEM((rows, width), F32)
    of_heads = pltpu.VMEM((groups, rows, span), BF16)
    of_hidden = pltpu.VMEM((slots, rows, wide), BF16)
    down_part = (2, rank, width)
    up_part = (2, rank, piece)
    sums = 2 * (slots - 1) + 2 * (planes - 1)
    scratch = dict(
        qkv_v=pltpu.VMEM((3, width, width), BF16),
        out_v=pltpu.VMEM((width, width), BF16),
        ff_v=pltpu.VMEM((2, slots, width, wide), BF16),
        adapt_v=pltpu.VMEM((width, 2 * rank), BF16),
        adapt_own=pltpu.VMEM((piece, 2 * rank), BF16),
        q_own=pltpu.VMEM((rows, piece), BF16),
        ctx_out=pltpu.VMEM((slots, rows, piece), BF16),
        ctx_in=pltpu.VMEM((slots, rows, piece), BF16),
        inv_v=pltpu.VMEM((groups, rows, span), F32),
        p_v=pltpu.VMEM((heads, rows, rows), BF16),
        s1_v=pltpu.VMEM((rows, 1), F32),
        s2_v=pltpu.VMEM((rows, 1), F32),
        bias=pltpu.VMEM((rows, rows), F32),
        mid_t=pltpu.VMEM((2 * rank, rows), BF16),
        dmid_v=pltpu.VMEM((rows, 2 * rank), BF16),
        grad_down=pltpu.VMEM(down_part, F32),
        grad_up=pltpu.VMEM((slots, *up_part), F32),
        from_down=pltpu.VMEM((slots, *down_part), F32),
        from_up=pltpu.VMEM((slots - 1, *up_part), F32),
        plane_down=pltpu.VMEM((planes, *down_part), F32),
        plane_up=pltpu.VMEM((planes, *up_part), F32),
        local=pltpu.SemaphoreType.DMA((15,)),
        packs=pltpu.SemaphoreType.DMA((packs,)),
        send=pltpu.SemaphoreType.DMA((6, Gather.count)),
        recv=pltpu.SemaphoreType.DMA((6, Gather.count)),
        ctx_send=pltpu.SemaphoreType.DMA((slots,)),
        ctx_recv=pltpu.SemaphoreType.DMA((slots,)),
        hop_send=pltpu.SemaphoreType.DMA((2, rows // 128)),
        hop_recv=pltpu.SemaphoreType.DMA((2, rows // 128)),
        row_send=pltpu.SemaphoreType.DMA((2, 3, rows // 128)),
        row_recv=pltpu.SemaphoreType.DMA((2, 3, rows // 128)),
        sum_send=pltpu.SemaphoreType.DMA((sums,)),
        sum_recv=pltpu.SemaphoreType.DMA((sums,)),
    )
    scratch |= dict.fromkeys(("h_v", "recv_v", "back_v", "cot_v", "low_v"), low_rows)
    scratch |= dict.fromkeys(("hop_v", "layer_v", "dh_v", "din_v"), low_rows)
    scratch |= dict.fromkeys(("acc", "n1_v", "n2_v"), full_rows)
    scratch |= dict.fromkeys(("q_v", "k_v", "v_v", "ctx_v"), of_heads)
    scratch |= dict.fromkeys(("dq_v", "dk_v", "dv_v", "dctx_v"), of_heads)
    scratch |= dict.fromkeys(("act_v", "slope_v"), of_hidden)
    layer_outs, in_grads, grad_a, grad_b = pl.pallas_call(
        partial(whole_kernel, planes, tuple(scratch)),
        name="encoder_layers",
        out_shape=[
            pltpu.VMEM((packs * rows, width), BF16),
            pltpu.VMEM((packs * rows, width), BF16),
            arr(down_part, F32),
            arr(up_part, F32),
        ],
        in_specs=[ANY] + [VMEM] * 5 + [ANY] * 5,
        out_specs=[VMEM] * 4,
        scratch_shapes=list(scratch.values()),
        compiler_params=pltpu.CompilerParams(
            vmem_limit_bytes=VMEM_LIMIT, collective_id=0, has_side_effects=True
        ),
        cost_estimate=pl.CostEstimate(
            flops=7 * 10**10, bytes_accessed=3 * 10**7, transcendentals=0
        ),
    )(
        embedded,
        segment,
        layer_norm_gain[0],
        layer_norm_bias[0],
        jnp.swapaxes(adapter_down_weight[0], 1, 2).reshape(2 * rank, width),
        adapter_up_weight[0].reshape(2 * rank, piece),
        jnp.swapaxes(query_key_value_weight[0], 1, 2),
        attention_output_weight[0],
        feedforward_up_weight[0],
        feedforward_down_weight[0],
        cotangent,
    )
    grad_a = jnp.swapaxes(grad_a, 1, 2)
    return (layer_outs[None], in_grads[None], grad_a[None], grad_b[None])


def solution(mesh):
    in_specs = (
        P("dp", None),
        P("dp", None),
        P("section", None, None, "tensor"),
        P("section", "tensor", None),
        P("section", None, "tensor"),
        P("section", "tensor", None),
        P("section", None, None, None),
        P("section", None, None, "tensor"),
        P("section", None, None),
        P("section", None, None),
        P("dp", None),
    )
    out_specs = (
        P("section", "dp", None),
        P("section", "dp", None),
        P("section", None, None, None),
        P("section", None, None, "tensor"),
    )
    return jax.shard_map(local, mesh=mesh, in_specs=in_specs, out_specs=out_specs, check_vma=False)
```

```python
from functools import partial

import jax
import jax.numpy as jnp
from jax import lax
from jax.experimental import pallas as pl
from jax.experimental.pallas import tpu as pltpu
from jax.sharding import PartitionSpec as P

HEAD_DIM = 64
EPS = 1e-05
VMEM_LIMIT = 115 * 2**19
F32 = jnp.float32
BF16 = jnp.bfloat16
ANY = pl.BlockSpec(memory_space=pl.ANY)
VMEM = pl.BlockSpec(memory_space=pltpu.VMEM)
MESH = pl.DeviceIdType.MESH
SMEM = pl.BlockSpec(memory_space=pltpu.SMEM)


def nn(a, b):
    return jnp.dot(a, b, preferred_element_type=F32)


def nt(a, b):
    return lax.dot_general(a, b, (((1,), (1,)), ((), ())), preferred_element_type=F32)


def lane_mask(shape, low, high):
    lanes = lax.broadcasted_iota(jnp.int32, shape, len(shape) - 1)
    return (lanes >= low) & (lanes < high)


def normalize(total):
    average = jnp.mean(total, -1, keepdims=True)
    centred = total - average
    spread = jnp.mean(centred * centred, -1, keepdims=True)
    scaled = lax.rsqrt(spread + EPS)
    return centred * scaled, scaled


def normalize_back(normed, scaled, gains, incoming):
    weighted = incoming * gains
    return scaled * (
        weighted
        - jnp.mean(weighted, -1, keepdims=True)
        - normed * jnp.mean(weighted * normed, -1, keepdims=True)
    )


def neighbours():
    section, plane, tensor = (lax.axis_index(n) for n in ("section", "dp", "tensor"))
    turned = lax.rem(tensor + 2, 4)
    other = tensor + 1 - 2 * lax.rem(tensor, 2)
    paired = plane + 1 - 2 * lax.rem(plane, 2)
    return (
        (section, plane, other),
        (section, plane, turned),
        (section, paired, tensor),
        (1 - section, plane, tensor),
        (1 - section, plane, turned),
    )


def meet(devices):
    barrier = pltpu.get_barrier_semaphore()
    for device in devices:
        pl.semaphore_signal(barrier, inc=1, device_id=device, device_id_type=MESH)
    pl.semaphore_wait(barrier, len(devices))


def remote(src, dst, send, recv, device):
    return pltpu.make_async_remote_copy(
        src_ref=src,
        dst_ref=dst,
        send_sem=send,
        recv_sem=recv,
        device_id=device,
        device_id_type=MESH,
    )


def identity(n):
    rows = lax.broadcasted_iota(jnp.int32, (n, n), 0)
    return (rows == lax.broadcasted_iota(jnp.int32, (n, n), 1)).astype(BF16)


def blocks_of(rows, size):
    return [pl.ds(r, size) for r in range(0, rows, size)]


class Gather:
    items, ahead, ahead_own = 8, 2, 8
    through = 5

    def __init__(self, own, gathered, resting, partners, sems):
        self.qkv, self.outw, self.up, self.down, self.adapt = own
        self.qkv_v, self.out_v, self.ff_v, self.adapt_v = gathered
        self.resting_v = resting
        self.core, self.far, self.plane, self.beyond, self.corner = partners
        self.send, self.recv, self.local = sems
        self.parity = lax.rem(lax.axis_index("dp"), 2)
        self.n_qkv, self.n_out = self.qkv.shape[1], self.outw.shape[0]
        self.n_ff, self.n_adapt = self.up.shape[0], self.adapt.shape[0]

    def block(self, i, slot, third):
        if i == 0:
            size = self.n_out // 3
            return self.out_v.at[pl.ds(slot * self.n_out + third * size, size)]
        if i >= 5:
            size = self.n_qkv // 3
            return self.qkv_v.at[i - 5, pl.ds(slot * self.n_qkv + third * size, size)]
        which, j = divmod(i - 1, 2)
        rows = self.n_ff // 3
        size = rows // 2
        return self.ff_v.at[which, slot, pl.ds(third * rows + j * size, size)]

    def resting(self, i):
        size = self.n_out // 3 if i == 0 else self.n_ff // 6
        return self.resting_v.at[i // 4, pl.ds(i % 4 * (self.n_ff // 6), size)]

    def whole(self, i, slot):
        if i == 0:
            return self.qkv_v.at[:, pl.ds(slot * self.n_qkv, self.n_qkv)]
        if i == 1:
            return self.out_v.at[pl.ds(slot * self.n_out, self.n_out)]
        if i == 4:
            return self.adapt_v.at[pl.ds(slot * self.n_adapt, self.n_adapt)]
        return self.ff_v.at[i - 2, slot]

    def link(self, kind, i, src, dst, device):
        return remote(src, dst, self.send.at[kind, i], self.recv.at[kind, i], device)

    def over_far(self, i):
        p = self.parity
        return self.link(0, i, self.block(i, 0, p), self.block(i, 2, p), self.far)

    def to_plane(self, i, third):
        here = self.block(i, 2, third)
        return self.link(1, i, here, here, self.plane)

    def pass_on(self, i, kind):
        third = (self.parity, 1 - self.parity, 2)[kind]
        return self.link(2 + kind, i, self.block(i, 2, third), self.block(i, 3, third), self.core)

    def to_corner(self, i):
        return self.link(7, i, self.block(i, 0, 2), self.resting(i), self.corner)

    def to_beyond(self, i):
        return self.link(8, i, self.resting(i), self.block(i, 2, 2), self.beyond)

    def last_far(self, i):
        return self.link(9, i, self.block(i, 0, 2), self.block(i, 2, 2), self.far)

    def last_plane(self, i):
        here = self.block(i, 2, 2)
        return self.link(10, i, here, here, self.plane)

    def load(self, i):
        own = (self.qkv, self.outw, self.up, self.down, self.adapt)[i]
        return pltpu.make_async_copy(own, self.whole(i, 0), self.local.at[i])

    def to_core(self, i):
        return self.link(5, i, self.whole(i, 0), self.whole(i, 1), self.core)

    def adapt_far(self):
        return self.link(6, 0, self.whole(4, 0), self.whole(4, 2), self.far)

    def adapt_core(self):
        return self.link(6, 1, self.whole(4, 2), self.whole(4, 3), self.core)

    def when_last(self, i, mine):
        here = i % 2
        return pl.when(self.parity == (here if mine else 1 - here))

    def issue(self, i, through):
        self.over_far(i).start()
        if through:
            self.to_corner(i).start()
        else:

            @self.when_last(i, True)
            def _():
                self.last_far(i).start()

    def pump(self, i, through):
        self.over_far(i).wait_recv()
        self.to_plane(i, self.parity).start()
        self.pass_on(i, 0).start()
        if not through:

            @self.when_last(i, True)
            def _():
                self.last_far(i).wait_recv()
                self.last_plane(i).start()
                self.pass_on(i, 2).start()

    def relay(self, i, through):
        self.to_plane(i, 1 - self.parity).wait_recv()
        self.pass_on(i, 1).start()
        if not through:

            @self.when_last(i, False)
            def _():
                self.last_plane(i).wait_recv()
                self.pass_on(i, 2).start()

    def relay_last(self, i):
        self.to_beyond(i).wait_recv()
        self.pass_on(i, 2).start()

    def help(self, i):
        self.to_corner(i).wait_recv()
        self.to_beyond(i).start()

    def landed(self, *items):
        for i in items:
            for kind in range(3):
                self.pass_on(i, kind).wait_recv()

    def sent(self, section):
        for i in range(self.items):
            self.over_far(i).wait_send()
            self.to_plane(i, self.parity).wait_send()
            for kind in range(3):
                self.pass_on(i, kind).wait_send()
            if section == 0 and i < self.through:
                self.to_corner(i).wait_send()
            else:

                @self.when_last(i, True)
                def _():
                    self.last_far(i).wait_send()
                    self.last_plane(i).wait_send()

        for i in range(5):
            self.to_core(i).wait_send()
        self.adapt_far().wait_send()
        self.adapt_core().wait_send()


def middle(h, adapt_down):
    rank = adapt_down.shape[0] // 2
    mid = nt(h, adapt_down[...]).astype(BF16)
    is_query = lane_mask(mid.shape, 0, rank)
    double = mid * jnp.asarray(2.0, BF16)
    zero = jnp.zeros((), BF16)
    return mid, jnp.where(is_query, double, zero), jnp.where(is_query, zero, double)


def project(h_v, adapt_down, w, ready):
    for part in blocks_of(h_v.shape[0], 256):
        ready(part)
        h = h_v[part]
        mid, mid_q, mid_v = middle(h, adapt_down)
        w.mid_t[:, part] = nt(identity(mid.shape[1]), mid).astype(BF16)
        for s, (ref, low) in enumerate(((w.q_v, mid_q), (w.k_v, None), (w.v_v, mid_v))):
            value = nt(h, w.qkv_v[s])
            if low is not None:
                value = value + nt(low, w.adapt_v[...])
            value = value.astype(BF16)
            span = ref.shape[2]
            for g in range(ref.shape[0]):
                ref[g, part] = value[:, g * span : (g + 1) * span]


def attend(q_v, k, v, bias, give):
    rows, span = k.shape
    chunk = 256
    zero = jnp.zeros((), BF16)
    for part in blocks_of(rows, chunk):
        q_c = q_v[part] * jnp.asarray(HEAD_DIM**-0.5, BF16)
        ctx = jnp.zeros((chunk, span), F32)
        inverse = jnp.zeros((chunk, span), F32)
        weights = []
        for e in range(span // HEAD_DIM):
            low = e * HEAD_DIM
            of_head = lane_mask(q_c.shape, low, low + HEAD_DIM)
            v_e = jnp.where(lane_mask(v.shape, low, low + HEAD_DIM), v, zero)
            s = nt(jnp.where(of_head, q_c, zero), k) + bias[part]
            weight = jnp.exp(s - jnp.max(s, -1, keepdims=True))
            scale = 1.0 / jnp.sum(weight, -1, keepdims=True)
            weight = weight.astype(BF16)
            ctx = ctx + nn(weight, v_e) * scale
            inverse = jnp.where(of_head, scale, inverse)
            give(part, e, weight, None)
        give(part, None, ctx.astype(BF16), inverse)


def attention_out(h_v, context, gains, biases, w, keep):
    groups, rows, span = context.shape
    for part in blocks_of(rows, 256):
        total = h_v[part].astype(F32)
        for g in range(groups):
            total = total + nn(context[g, part], w.out_v[g * span : (g + 1) * span])
        normed, scaled = normalize(total)
        if keep:
            w.n1_v[part] = normed
            w.s1_v[part] = scaled
        first = normed * gains[0:1] + biases[0:1]
        w.acc[part] = first
        w.low_v[part] = first.astype(BF16)


def feedforward_up(w, keep, ready):
    def step(slot, carry):
        ready(slot)
        for part in blocks_of(w.low_v.shape[0], 128):
            pre = nn(w.low_v[part], w.ff_v[0, slot])
            cdf = 0.5 + 0.5 * lax.erf(pre * (0.5**0.5))
            w.act_v[slot, part] = (pre * cdf).astype(BF16)
            if keep:
                density = jnp.exp(pre * pre * -0.5) * 0.3989422804014327
                w.slope_v[slot, part] = (cdf + pre * density).astype(BF16)
        return carry

    lax.fori_loop(0, w.act_v.shape[0], step, 0)


def backward(w, gains, adapt_down, incoming, give, sums):
    rows = w.acc.shape[0]
    slots = w.ff_v.shape[1]
    groups, _, span = w.q_v.shape
    for part in blocks_of(rows, 256):
        back = normalize_back(w.n2_v[part], w.s2_v[part], gains[1:2], incoming(part))
        w.acc[part] = back
        w.low_v[part] = back.astype(BF16)

        def step(slot, carry):
            dact = nt(w.low_v[part], w.ff_v[1, slot])
            w.act_v[slot, part] = (dact * w.slope_v[slot, part].astype(F32)).astype(BF16)
            return carry

        lax.fori_loop(0, slots, step, 0)
        total = w.acc[part]
        for slot in range(slots):
            total = total + nt(w.act_v[slot, part], w.ff_v[0, slot])
        back = normalize_back(w.n1_v[part], w.s1_v[part], gains[0:1], total)
        w.acc[part] = back
        dctx = nt(back.astype(BF16), w.out_v[...])
        for g in range(groups):
            scaled = dctx[:, g * span : (g + 1) * span] * w.inv_v[g, part]
            w.dctx_v[g, part] = scaled.astype(BF16)
    heads = span // HEAD_DIM
    factor = HEAD_DIM**-0.5

    def group(g, carry):
        q, k, v = w.q_v[g], w.k_v[g], w.v_v[g]
        dctx, ctx = w.dctx_v[g], w.ctx_v[g].astype(F32)
        q_t, dctx_t = q.T, dctx.T
        zero = jnp.zeros((), BF16)
        dq = jnp.zeros((rows, span), F32)
        dk_t, dv_t = [], []
        for e in range(heads):
            low, high = e * HEAD_DIM, (e + 1) * HEAD_DIM
            of_head = lane_mask((rows, span), low, high)
            weight = w.p_v[g * heads + e]
            dctx_e = jnp.where(of_head, dctx, zero)
            delta = jnp.sum(dctx_e.astype(F32) * ctx, -1, keepdims=True)
            ds = (weight.astype(F32) * (nt(dctx_e, v) - delta)).astype(BF16)
            dq = dq + nn(ds, jnp.where(of_head, k, zero))
            dk_t.append(nn(q_t[low:high], ds))
            dv_t.append(nn(dctx_t[low:high], weight))
        w.dq_v[g] = (dq * factor).astype(BF16)
        w.dk_v[g] = (jnp.concatenate(dk_t, 0) * factor).astype(BF16).T
        w.dv_v[g] = jnp.concatenate(dv_t, 0).astype(BF16).T
        return carry

    lax.fori_loop(0, groups, group, 0)
    rank = adapt_down.shape[0] // 2
    for part in blocks_of(rows, 256):
        dmid_q = dmid_v = 0.0
        for g in range(groups):
            cols = slice(g * span, (g + 1) * span)
            dmid_q = dmid_q + nn(w.dq_v[g, part], w.adapt_v[cols])
            dmid_v = dmid_v + nn(w.dv_v[g, part], w.adapt_v[cols])
        dmid = 2.0 * jnp.where(lane_mask(dmid_q.shape, 0, rank), dmid_q, dmid_v)
        w.dmid_v[part] = dmid.astype(BF16)
    sums()
    for part in blocks_of(rows, 128):
        total = w.acc[part]
        for g in range(groups):
            cols = slice(g * span, (g + 1) * span)
            for s, ref in enumerate((w.dq_v, w.dk_v, w.dv_v)):
                total = total + nn(ref[g, part], w.qkv_v[s, cols])
        give(part, (total + nn(w.dmid_v[part], adapt_down[...])).astype(BF16))


class Refs:
    def __init__(self, names, refs):
        self.__dict__.update(zip(names, refs, strict=True))


def whole_kernel(planes, names, *refs):
    embedded, segment, gains, biases, adapt_down, adapt, qkv, outw, up, down, cotangent = refs[:11]
    layer_outs, in_grads, down_out, up_out = refs[11:15]
    w = Refs(names, refs[15:])
    section, plane, tensor = (lax.axis_index(n) for n in ("section", "dp", "tensor"))
    core, far, paired, beyond, corner = neighbours()
    turned = lax.rem(tensor + 2, 4)
    other = tensor + 1 - 2 * lax.rem(tensor, 2)
    across = lax.rem(other + 2, 4)
    indices = (other, turned, across)
    sides = tuple((section, plane, i) for i in indices)
    ring = [(section, lax.rem(plane + m, planes), tensor) for m in range(1, planes)]
    rows, width = w.h_v.shape
    groups = w.q_v.shape[0]

    own = pl.ds(tensor * rows, rows)
    gather = Gather(
        (qkv, outw, up, down, w.adapt_own),
        (w.qkv_v, w.out_v, w.ff_v, w.adapt_v),
        w.act_v,
        (core, far, paired, beyond, corner),
        (w.send, w.recv, w.local),
    )
    for i in (1, 0, 2, 3):
        gather.load(i).start()
    pack_copies = [
        pltpu.make_async_copy(embedded.at[pl.ds(i * rows, rows)], w.slope_v.at[i], w.packs.at[i])
        for i in range(len(indices) + 1)
    ]
    for copy in pack_copies:
        copy.start()
    h_copy = pltpu.make_async_copy(embedded.at[own], w.h_v, w.local.at[5])
    h_copy.start()
    cot_copy = pltpu.make_async_copy(cotangent.at[own], w.cot_v, w.local.at[6])
    cot_copy.start()
    adapt_t = nt(identity(adapt.shape[1]), adapt[...]).astype(BF16)
    w.adapt_own[...] = adapt_t
    w.adapt_v[: adapt.shape[1]] = adapt_t
    meet((*sides, *ring, beyond, corner))

    for i in (1, 2, 3, 0):
        gather.load(i).wait()
    gather.adapt_far().start()
    for i in (4, 1, 2, 3, 0):
        gather.to_core(i).start()
    for copy in pack_copies:
        copy.wait()
    h_copy.wait()
    square = (rows, rows)
    piece = adapt.shape[1]
    pieces = blocks_of(rows, 128)

    def mask(pack):
        diagonal = lax.broadcasted_iota(jnp.int32, square, 0) == lax.broadcasted_iota(
            jnp.int32, square, 1
        )
        ids = segment[pl.ds(pack, 1), :].astype(F32)
        column = jnp.sum(jnp.where(diagonal, ids, 0.0), -1, keepdims=True)
        w.bias[...] = jnp.where(column == ids, 0.0, -1e9)

    def index_of(k):
        high = lax.rem(tensor // 2 + k // 2, 2)
        return 2 * high + lax.rem(lax.rem(tensor, 2) + lax.rem(k, 2), 2)

    def context_to(k):
        device = (section, plane, index_of(k))
        return remote(w.ctx_out.at[k], w.ctx_in.at[k], w.ctx_send.at[k], w.ctx_recv.at[k], device)

    def attend_pack(step, carry):
        k = 3 - step
        pack = index_of(k)
        mask(pack)
        h = w.slope_v[pack]
        _, mid_q, mid_v = middle(h, adapt_down)
        w.q_own[...] = (nt(h, w.qkv_v[0, :piece]) + nt(mid_q, w.adapt_own[...])).astype(BF16)
        k_own = nt(h, w.qkv_v[1, :piece]).astype(BF16)
        v_own = (nt(h, w.qkv_v[2, :piece]) + nt(mid_v, w.adapt_own[...])).astype(BF16)

        def give(part, head, value, inverse):
            if head is None:
                w.ctx_out[k, part] = value

        attend(w.q_own, k_own, v_own, w.bias, give)

        @pl.when(step < 3)
        def _():
            context_to(k).start()

        for i in (1, 2, 3):

            @pl.when(step == i)
            def _():
                gather.pump(i - 1, True)
                ask(i - 1 + gather.ahead)
                if i > 1:
                    gather.relay(i - 2, True)
                if i > 2:
                    gather.relay_last(i - 3)

        return carry

    def hop(way, i, src, dst):
        return remote(src, dst, w.hop_send.at[way, i], w.hop_recv.at[way, i], beyond)

    def ask(i):
        if i < gather.items:
            gather.issue(i, i < gather.through)

    @pl.when(section == 0)
    def _():
        for i in range(gather.ahead):
            ask(i)
        lax.fori_loop(0, 4, attend_pack, 0)
        w.ctx_in[0] = w.ctx_out[0]
        gather.adapt_far().wait_recv()
        gather.adapt_core().start()
        for k in (1, 2, 3):
            context_to(k).wait_recv()
        gather.to_core(1).wait_recv()
        gather.landed(0)
        attention_out(w.h_v, w.ctx_in, gains, biases, w, False)
        gather.pump(3, True)
        ask(3 + gather.ahead)
        gather.relay(2, True)
        gather.relay_last(1)
        for i in (2, 3):
            gather.to_core(i).wait_recv()

        def rest_of_up(slot):
            @pl.when(slot == 2)
            def _():
                gather.relay_last(2)
                gather.landed(1, 2)

            @pl.when(slot == 3)
            def _():
                gather.pump(4, True)
                ask(4 + gather.ahead)
                gather.relay(3, True)

        feedforward_up(w, False, rest_of_up)
        gather.relay_last(3)
        for part in blocks_of(rows, 256):
            w.acc[part] += nn(w.act_v[0, part], w.ff_v[1, 0]) + nn(w.act_v[1, part], w.ff_v[1, 1])
        gather.relay(4, True)
        gather.relay_last(4)
        gather.landed(3, 4)
        for i, part in enumerate(pieces):
            total = w.acc[part]
            for slot in (2, 3):
                total = total + nn(w.act_v[slot, part], w.ff_v[1, slot])
            w.hop_v[part] = (normalize(total)[0] * gains[1:2] + biases[1:2]).astype(BF16)
            hop(0, i, w.hop_v.at[part], w.recv_v.at[part]).start()
        for i in range(5, gather.items):
            gather.pump(i, False)
            ask(i + gather.ahead)
            if i > 5:
                gather.relay(i - 1, False)
        gather.relay(gather.items - 1, False)

    order = (5, 6, 7, 0, 1, 2, 3, 4)

    def own_step(n):
        gather.pump(order[n], False)
        if n + gather.ahead_own < gather.items:
            gather.issue(order[n + gather.ahead_own], False)
        if n > 0:
            gather.relay(order[n - 1], False)

    @pl.when(section == 1)
    def _():
        mask(tensor)
        gather.adapt_far().wait_recv()
        gather.adapt_core().start()
        for n in range(gather.ahead_own):
            gather.issue(order[n], False)
        for i in range(gather.through):
            gather.help(i)
            if i > 1:
                own_step(i - 2)
        for n in (3, 4, 5):
            own_step(n)
        for i in range(gather.through):
            gather.to_beyond(i).wait_send()
        gather.to_core(1).wait_recv()
        gather.landed(0)

    for i in (0, 4):
        gather.to_core(i).wait_recv()
    gather.adapt_core().wait_recv()
    gather.landed(5, 6, 7)

    def ready(part):
        @pl.when(section == 1)
        def _():
            for i in range(part.start // 128, (part.start + part.size) // 128):
                hop(0, i, w.hop_v.at[pieces[i]], w.recv_v.at[pieces[i]]).wait_recv()
            w.h_v[part] = w.recv_v[part]

    project(w.h_v, adapt_down, w, ready)

    def attend_group(g, carry):
        def give(part, head, value, inverse):
            if head is None:
                w.ctx_v[g, part] = value
                w.inv_v[g, part] = inverse
            else:
                w.p_v[g * (w.q_v.shape[2] // HEAD_DIM) + head, part] = value

        attend(w.q_v.at[g], w.k_v[g], w.v_v[g], w.bias, give)
        @pl.when(jnp.logical_and(section == 1, g == 0))
        def _():
            own_step(6)

        return carry

    lax.fori_loop(0, groups, attend_group, 0)
    attention_out(w.h_v, w.ctx_v, gains, biases, w, True)

    @pl.when(section == 1)
    def _():
        own_step(7)
        for i in (2, 3):
            gather.to_core(i).wait_recv()
        gather.landed(1, 2)

    def rest_of_down(slot):
        @pl.when(jnp.logical_and(section == 1, slot == 3))
        def _():
            gather.relay(order[7], False)

    feedforward_up(w, True, rest_of_down)

    @pl.when(section == 1)
    def _():
        gather.landed(3, 4)

    def block(out, index, part):
        return out.at[pl.ds(index * rows + part.start, part.size)]

    def rows_to(n, way, i, src, out, part, device):
        sems = w.row_send.at[n, way, i], w.row_recv.at[n, way, i]
        return remote(src.at[part], block(out, tensor, part), *sems, device)

    def rows_far(n, i, src, out, part):
        return rows_to(n, 0, i, src, out, part, far)

    def rows_core(n, i, src, out, part):
        return rows_to(n, 1, i, src, out, part, core)

    def rows_mine(n, i, src, out, part):
        return pltpu.make_async_copy(src.at[part], block(out, tensor, part), w.local.at[7 + 4 * n + i])

    def rows_relay(n, i, out, part):
        landed = block(out, turned, part)
        return remote(landed, landed, w.row_send.at[n, 2, i], w.row_recv.at[n, 2, i], core)

    def spread(n, i, src, out, part):
        for make in (rows_far, rows_core, rows_mine):
            make(n, i, src, out, part).start()

    def relay_rows(n, i, src, out, part):
        rows_far(n, i, src, out, part).wait_recv()
        rows_relay(n, i, out, part).start()

    def gathered(n, i, src, out, part):
        rows_core(n, i, src, out, part).wait()
        rows_relay(n, i, out, part).wait()
        rows_mine(n, i, src, out, part).wait()

    ends = (pl.ds(0, 128), pl.ds(128, 128), pl.ds(256, rows - 256))

    def through_corner(src):
        sems = w.row_send.at[1, 1, 3], w.row_recv.at[1, 1, 3]
        return remote(src.at[ends[0]], w.back_v.at[ends[0]], *sems, corner)

    def through_beyond():
        sems = w.row_send.at[1, 0, 3], w.row_recv.at[1, 0, 3]
        return remote(w.back_v.at[ends[0]], block(in_grads, turned, ends[0]), *sems, beyond)

    for i, part in enumerate(pieces):
        total = w.acc[part]
        for slot in range(w.ff_v.shape[1]):
            total = total + nn(w.act_v[slot, part], w.ff_v[1, slot])
        normed, scaled = normalize(total)
        w.n2_v[part] = normed
        w.s2_v[part] = scaled
        w.layer_v[part] = (normed * gains[1:2] + biases[1:2]).astype(BF16)
        spread(0, i, w.layer_v, layer_outs, part)

    cot_copy.wait()
    rank = adapt_down.shape[0] // 2

    def incoming(again, part):
        @pl.when(jnp.logical_and(again == 1, section == 0))
        def _():
            for i in range(part.start // 128, (part.start + part.size) // 128):
                hop(1, i, w.dh_v.at[pieces[i]], w.back_v.at[pieces[i]]).wait_recv()
            w.cot_v[part] = w.back_v[part]

        return w.cot_v[part].astype(F32)

    def summed(n, src, dst, device):
        return remote(src, dst, w.sum_send.at[n], w.sum_recv.at[n], device)

    def over_tensor(landing):
        copies = []
        for i, device in enumerate(sides):
            slot = indices[i] if landing else tensor
            for src, dst in (
                (w.grad_down, w.from_down.at[slot]),
                (w.grad_up.at[i + 1], w.from_up.at[i]),
            ):
                copies.append(summed(len(copies), src, dst, device))
        return copies

    def adapter_gradients(again):
        @pl.when(again == 1)
        def _():
            dmid_t = nt(identity(2 * rank), w.dmid_v[...]).astype(BF16)
            grad_down = nn(dmid_t, w.h_v[...])
            for j in range(2):
                w.grad_down[j] = grad_down[j * rank : (j + 1) * rank]
            up_q, up_v = (
                jnp.concatenate([2.0 * nn(w.mid_t[...], ref[g]) for g in range(groups)], 1)
                for ref in (w.dq_v, w.dv_v)
            )
            for i in range(len(sides) + 1):
                cols = slice(i * piece, (i + 1) * piece)
                w.grad_up[i, 0] = up_q[:rank, cols]
                w.grad_up[i, 1] = up_v[rank:, cols]
            w.from_down[tensor] = w.grad_down[...]
            for copy in over_tensor(False):
                copy.start()

    def hand_over(again, part, value):
        i = part.start // 128

        @pl.when(jnp.logical_and(again == 0, section == 1))
        def _():
            w.dh_v[part] = value
            hop(1, i, w.dh_v.at[part], w.back_v.at[part]).start()
            for n, end in enumerate(ends):
                if end.start + end.size == part.start + part.size:
                    spread(1, n, w.dh_v, in_grads, end)

        @pl.when(jnp.logical_and(again == 1, section == 0))
        def _():
            w.dh_v[part] = value
            for n, end in enumerate(ends):
                if end.start + end.size == part.start + part.size:
                    if n:
                        rows_far(1, n, w.dh_v, in_grads, end).start()
                    else:
                        through_corner(w.dh_v).start()
                    rows_core(1, n, w.dh_v, in_grads, end).start()
                    rows_mine(1, n, w.dh_v, in_grads, end).start()

    def back(again, carry):
        backward(
            w,
            gains,
            adapt_down,
            partial(incoming, again),
            partial(hand_over, again),
            partial(adapter_gradients, again),
        )

        @pl.when(again == 0)
        def _():
            for i, part in enumerate(pieces):
                relay_rows(0, i, w.layer_v, layer_outs, part)

        return carry

    lax.fori_loop(0, 2, back, 0)

    @pl.when(section == 1)
    def _():
        for n, end in enumerate(ends):
            relay_rows(1, n, w.dh_v, in_grads, end)
        through_corner(w.dh_v).wait_recv()
        through_beyond().start()

    tensor_copies = over_tensor(True)
    for copy in tensor_copies:
        copy.wait()
    w.plane_down[plane] = w.from_down[0] + w.from_down[1] + w.from_down[2] + w.from_down[3]
    w.plane_up[plane] = w.grad_up[0] + w.from_up[0] + w.from_up[1] + w.from_up[2]
    base = len(tensor_copies)
    totals = (w.plane_down, w.plane_up)
    for m, device in enumerate(ring):
        for k, ref in enumerate(totals):
            summed(base + 2 * m + k, ref.at[plane], ref.at[plane], device).start()

    @pl.when(section == 0)
    def _():
        relay_rows(1, 1, w.dh_v, in_grads, ends[1])

    for m, device in enumerate(ring):
        source = lax.rem(plane + planes - m - 1, planes)
        for k, ref in enumerate(totals):
            summed(base + 2 * m + k, ref.at[source], ref.at[source], device).wait_recv()
    for m, device in enumerate(ring):
        for k, ref in enumerate(totals):
            summed(base + 2 * m + k, ref.at[plane], ref.at[plane], device).wait_send()
    down_total, up_total = w.plane_down[0], w.plane_up[0]
    for m in range(1, planes):
        down_total = down_total + w.plane_down[m]
        up_total = up_total + w.plane_up[m]
    up_out[...] = up_total
    down_out[...] = down_total

    @pl.when(section == 0)
    def _():
        through_beyond().wait_recv()
        rows_relay(1, 0, in_grads, ends[0]).start()
        relay_rows(1, 2, w.dh_v, in_grads, ends[2])
        through_corner(w.dh_v).wait_send()
        for n in (1, 2):
            rows_far(1, n, w.dh_v, in_grads, ends[n]).wait_send()
        for i, part in enumerate(pieces):
            hop(0, i, w.hop_v.at[part], w.recv_v.at[part]).wait_send()
        for k in (1, 2, 3):
            context_to(k).wait_send()
        gather.sent(0)

    @pl.when(section == 1)
    def _():
        through_beyond().wait_send()
        for n, end in enumerate(ends):
            rows_far(1, n, w.dh_v, in_grads, end).wait_send()
        for i, part in enumerate(pieces):
            hop(1, i, w.dh_v.at[part], w.back_v.at[part]).wait_send()
        gather.sent(1)

    for i, part in enumerate(pieces):
        rows_far(0, i, w.layer_v, layer_outs, part).wait_send()
        gathered(0, i, w.layer_v, layer_outs, part)
    for n, end in enumerate(ends):
        gathered(1, n, w.dh_v, in_grads, end)


def local(
    embedded,
    segment,
    query_key_value_weight,
    attention_output_weight,
    feedforward_up_weight,
    feedforward_down_weight,
    adapter_down_weight,
    adapter_up_weight,
    layer_norm_gain,
    layer_norm_bias,
    cotangent,
):
    slots, packs, planes = lax.axis_size("tensor"), segment.shape[0], lax.axis_size("dp")
    assert slots == 4 and packs == slots and planes % 2 == 0
    rows, width = segment.shape[1], embedded.shape[1]
    piece = query_key_value_weight.shape[3]
    wide = feedforward_up_weight.shape[2]
    assert wide == width
    rank = adapter_down_weight.shape[3]
    span = 256
    groups = width // span
    heads = width // HEAD_DIM

    def arr(shape, dtype):
        return jax.ShapeDtypeStruct(shape, dtype)

    low_rows = pltpu.VMEM((rows, width), BF16)
    full_rows = pltpu.VMEM((rows, width), F32)
    of_heads = pltpu.VMEM((groups, rows, span), BF16)
    of_hidden = pltpu.VMEM((slots, rows, wide), BF16)
    down_part = (2, rank, width)
    up_part = (2, rank, piece)
    sums = 2 * (slots - 1) + 2 * (planes - 1)
    scratch = dict(
        qkv_v=pltpu.VMEM((3, width, width), BF16),
        out_v=pltpu.VMEM((width, width), BF16),
        ff_v=pltpu.VMEM((2, slots, width, wide), BF16),
        adapt_v=pltpu.VMEM((width, 2 * rank), BF16),
        adapt_own=pltpu.VMEM((piece, 2 * rank), BF16),
        q_own=pltpu.VMEM((rows, piece), BF16),
        ctx_out=pltpu.VMEM((slots, rows, piece), BF16),
        ctx_in=pltpu.VMEM((slots, rows, piece), BF16),
        inv_v=pltpu.VMEM((groups, rows, span), F32),
        p_v=pltpu.VMEM((heads, rows, rows), BF16),
        s1_v=pltpu.VMEM((rows, 1), F32),
        s2_v=pltpu.VMEM((rows, 1), F32),
        bias=pltpu.VMEM((rows, rows), F32),
        mid_t=pltpu.VMEM((2 * rank, rows), BF16),
        dmid_v=pltpu.VMEM((rows, 2 * rank), BF16),
        grad_down=pltpu.VMEM(down_part, F32),
        grad_up=pltpu.VMEM((slots, *up_part), F32),
        from_down=pltpu.VMEM((slots, *down_part), F32),
        from_up=pltpu.VMEM((slots - 1, *up_part), F32),
        plane_down=pltpu.VMEM((planes, *down_part), F32),
        plane_up=pltpu.VMEM((planes, *up_part), F32),
        local=pltpu.SemaphoreType.DMA((15,)),
        packs=pltpu.SemaphoreType.DMA((packs,)),
        send=pltpu.SemaphoreType.DMA((11, Gather.items)),
        recv=pltpu.SemaphoreType.DMA((11, Gather.items)),
        ctx_send=pltpu.SemaphoreType.DMA((slots,)),
        ctx_recv=pltpu.SemaphoreType.DMA((slots,)),
        hop_send=pltpu.SemaphoreType.DMA((2, rows // 128)),
        hop_recv=pltpu.SemaphoreType.DMA((2, rows // 128)),
        row_send=pltpu.SemaphoreType.DMA((2, 3, rows // 128)),
        row_recv=pltpu.SemaphoreType.DMA((2, 3, rows // 128)),
        sum_send=pltpu.SemaphoreType.DMA((sums,)),
        sum_recv=pltpu.SemaphoreType.DMA((sums,)),
    )
    scratch |= dict.fromkeys(("h_v", "recv_v", "back_v", "cot_v", "low_v"), low_rows)
    scratch |= dict.fromkeys(("hop_v", "layer_v", "dh_v"), low_rows)
    scratch |= dict.fromkeys(("acc", "n1_v", "n2_v"), full_rows)
    scratch |= dict.fromkeys(("q_v", "k_v", "v_v", "ctx_v"), of_heads)
    scratch |= dict.fromkeys(("dq_v", "dk_v", "dv_v", "dctx_v"), of_heads)
    scratch |= dict.fromkeys(("act_v", "slope_v"), of_hidden)
    layer_outs, in_grads, grad_a, grad_b = pl.pallas_call(
        partial(whole_kernel, planes, tuple(scratch)),
        name="encoder_layers",
        out_shape=[
            pltpu.VMEM((packs * rows, width), BF16),
            pltpu.VMEM((packs * rows, width), BF16),
            arr(down_part, F32),
            arr(up_part, F32),
        ],
        in_specs=[ANY] + [VMEM] * 5 + [ANY] * 5,
        out_specs=[VMEM] * 4,
        scratch_shapes=list(scratch.values()),
        compiler_params=pltpu.CompilerParams(
            vmem_limit_bytes=VMEM_LIMIT, collective_id=0, has_side_effects=True
        ),
        cost_estimate=pl.CostEstimate(
            flops=7 * 10**10, bytes_accessed=3 * 10**7, transcendentals=0
        ),
    )(
        embedded,
        segment,
        layer_norm_gain[0],
        layer_norm_bias[0],
        jnp.swapaxes(adapter_down_weight[0], 1, 2).reshape(2 * rank, width),
        adapter_up_weight[0].reshape(2 * rank, piece),
        jnp.swapaxes(query_key_value_weight[0], 1, 2),
        attention_output_weight[0],
        feedforward_up_weight[0],
        feedforward_down_weight[0],
        cotangent,
    )
    grad_a = jnp.swapaxes(grad_a, 1, 2)
    return (layer_outs[None], in_grads[None], grad_a[None], grad_b[None])


def solution(mesh):
    in_specs = (
        P("dp", None),
        P("dp", None),
        P("section", None, None, "tensor"),
        P("section", "tensor", None),
        P("section", None, "tensor"),
        P("section", "tensor", None),
        P("section", None, None, None),
        P("section", None, None, "tensor"),
        P("section", None, None),
        P("section", None, None),
        P("dp", None),
    )
    out_specs = (
        P("section", "dp", None),
        P("section", "dp", None),
        P("section", None, None, None),
        P("section", None, None, "tensor"),
    )
    return jax.shard_map(local, mesh=mesh, in_specs=in_specs, out_specs=out_specs, check_vma=False)
```

```python
from functools import partial

import jax
import jax.numpy as jnp
from jax import lax
from jax.experimental import pallas as pl
from jax.experimental.pallas import tpu as pltpu
from jax.sharding import PartitionSpec as P

HEAD_DIM = 64
EPS = 1e-05
VMEM_LIMIT = 115 * 2**19
F32 = jnp.float32
BF16 = jnp.bfloat16
ANY = pl.BlockSpec(memory_space=pl.ANY)
VMEM = pl.BlockSpec(memory_space=pltpu.VMEM)
MESH = pl.DeviceIdType.MESH
SMEM = pl.BlockSpec(memory_space=pltpu.SMEM)


def nn(a, b):
    return jnp.dot(a, b, preferred_element_type=F32)


def nt(a, b):
    return lax.dot_general(a, b, (((1,), (1,)), ((), ())), preferred_element_type=F32)


def lane_mask(shape, low, high):
    lanes = lax.broadcasted_iota(jnp.int32, shape, len(shape) - 1)
    return (lanes >= low) & (lanes < high)


def normalize(total):
    average = jnp.mean(total, -1, keepdims=True)
    centred = total - average
    spread = jnp.mean(centred * centred, -1, keepdims=True)
    scaled = lax.rsqrt(spread + EPS)
    return centred * scaled, scaled


def normalize_back(normed, scaled, gains, incoming):
    weighted = incoming * gains
    return scaled * (
        weighted
        - jnp.mean(weighted, -1, keepdims=True)
        - normed * jnp.mean(weighted * normed, -1, keepdims=True)
    )


def neighbours():
    section, plane, tensor = (lax.axis_index(n) for n in ("section", "dp", "tensor"))
    turned = lax.rem(tensor + 2, 4)
    other = tensor + 1 - 2 * lax.rem(tensor, 2)
    paired = plane + 1 - 2 * lax.rem(plane, 2)
    return (
        (section, plane, other),
        (section, plane, turned),
        (section, paired, tensor),
        (1 - section, plane, tensor),
        (1 - section, plane, turned),
    )


def meet(devices):
    barrier = pltpu.get_barrier_semaphore()
    for device in devices:
        pl.semaphore_signal(barrier, inc=1, device_id=device, device_id_type=MESH)
    pl.semaphore_wait(barrier, len(devices))


def remote(src, dst, send, recv, device):
    return pltpu.make_async_remote_copy(
        src_ref=src,
        dst_ref=dst,
        send_sem=send,
        recv_sem=recv,
        device_id=device,
        device_id_type=MESH,
    )


def identity(n):
    rows = lax.broadcasted_iota(jnp.int32, (n, n), 0)
    return (rows == lax.broadcasted_iota(jnp.int32, (n, n), 1)).astype(BF16)


def blocks_of(rows, size):
    return [pl.ds(r, size) for r in range(0, rows, size)]


class Gather:
    items, ahead, ahead_own = 8, 2, 8
    through = 5

    def __init__(self, own, gathered, resting, partners, sems):
        self.qkv, self.outw, self.up, self.down, self.adapt = own
        self.qkv_v, self.out_v, self.ff_v, self.adapt_v = gathered
        self.resting_v = resting
        self.core, self.far, self.plane, self.beyond, self.corner = partners
        self.send, self.recv, self.local = sems
        self.parity = lax.rem(lax.axis_index("dp"), 2)
        self.n_qkv, self.n_out = self.qkv.shape[1], self.outw.shape[0]
        self.n_ff, self.n_adapt = self.up.shape[0], self.adapt.shape[0]

    def block(self, i, slot, third):
        if i == 0:
            size = self.n_out // 3
            return self.out_v.at[pl.ds(slot * self.n_out + third * size, size)]
        if i >= 5:
            size = self.n_qkv // 3
            return self.qkv_v.at[i - 5, pl.ds(slot * self.n_qkv + third * size, size)]
        which, j = divmod(i - 1, 2)
        rows = self.n_ff // 3
        size = rows // 2
        return self.ff_v.at[which, slot, pl.ds(third * rows + j * size, size)]

    def resting(self, i):
        size = self.n_out // 3 if i == 0 else self.n_ff // 6
        return self.resting_v.at[i // 4, pl.ds(i % 4 * (self.n_ff // 6), size)]

    def whole(self, i, slot):
        if i == 0:
            return self.qkv_v.at[:, pl.ds(slot * self.n_qkv, self.n_qkv)]
        if i == 1:
            return self.out_v.at[pl.ds(slot * self.n_out, self.n_out)]
        if i == 4:
            return self.adapt_v.at[pl.ds(slot * self.n_adapt, self.n_adapt)]
        return self.ff_v.at[i - 2, slot]

    def link(self, kind, i, src, dst, device):
        return remote(src, dst, self.send.at[kind, i], self.recv.at[kind, i], device)

    def over_far(self, i):
        p = self.parity
        return self.link(0, i, self.block(i, 0, p), self.block(i, 2, p), self.far)

    def to_plane(self, i, third):
        here = self.block(i, 2, third)
        return self.link(1, i, here, here, self.plane)

    def pass_on(self, i, kind):
        third = (self.parity, 1 - self.parity, 2)[kind]
        return self.link(2 + kind, i, self.block(i, 2, third), self.block(i, 3, third), self.core)

    def to_corner(self, i):
        return self.link(7, i, self.block(i, 0, 2), self.resting(i), self.corner)

    def to_beyond(self, i):
        return self.link(8, i, self.resting(i), self.block(i, 2, 2), self.beyond)

    def last_far(self, i):
        return self.link(9, i, self.block(i, 0, 2), self.block(i, 2, 2), self.far)

    def last_plane(self, i):
        here = self.block(i, 2, 2)
        return self.link(10, i, here, here, self.plane)

    def load(self, i):
        own = (self.qkv, self.outw, self.up, self.down, self.adapt)[i]
        return pltpu.make_async_copy(own, self.whole(i, 0), self.local.at[i])

    def to_core(self, i):
        return self.link(5, i, self.whole(i, 0), self.whole(i, 1), self.core)

    def adapt_far(self):
        return self.link(6, 0, self.whole(4, 0), self.whole(4, 2), self.far)

    def adapt_core(self):
        return self.link(6, 1, self.whole(4, 2), self.whole(4, 3), self.core)

    def when_last(self, i, mine):
        here = i % 2
        return pl.when(self.parity == (here if mine else 1 - here))

    def issue(self, i, through):
        self.over_far(i).start()
        if through:
            self.to_corner(i).start()
        else:

            @self.when_last(i, True)
            def _():
                self.last_far(i).start()

    def pump(self, i, through):
        self.over_far(i).wait_recv()
        self.to_plane(i, self.parity).start()
        self.pass_on(i, 0).start()
        if not through:

            @self.when_last(i, True)
            def _():
                self.last_far(i).wait_recv()
                self.last_plane(i).start()
                self.pass_on(i, 2).start()

    def relay(self, i, through):
        self.to_plane(i, 1 - self.parity).wait_recv()
        self.pass_on(i, 1).start()
        if not through:

            @self.when_last(i, False)
            def _():
                self.last_plane(i).wait_recv()
                self.pass_on(i, 2).start()

    def relay_last(self, i):
        self.to_beyond(i).wait_recv()
        self.pass_on(i, 2).start()

    def help(self, i):
        self.to_corner(i).wait_recv()
        self.to_beyond(i).start()

    def landed(self, *items):
        for i in items:
            for kind in range(3):
                self.pass_on(i, kind).wait_recv()

    def sent(self, section):
        for i in range(self.items):
            self.over_far(i).wait_send()
            self.to_plane(i, self.parity).wait_send()
            for kind in range(3):
                self.pass_on(i, kind).wait_send()
            if section == 0 and i < self.through:
                self.to_corner(i).wait_send()
            else:

                @self.when_last(i, True)
                def _():
                    self.last_far(i).wait_send()
                    self.last_plane(i).wait_send()

        for i in range(5):
            self.to_core(i).wait_send()
        self.adapt_far().wait_send()
        self.adapt_core().wait_send()


def middle(h, adapt_down):
    rank = adapt_down.shape[0] // 2
    mid = nt(h, adapt_down[...]).astype(BF16)
    is_query = lane_mask(mid.shape, 0, rank)
    double = mid * jnp.asarray(2.0, BF16)
    zero = jnp.zeros((), BF16)
    return mid, jnp.where(is_query, double, zero), jnp.where(is_query, zero, double)


def project(h_v, adapt_down, w, ready):
    for part in blocks_of(h_v.shape[0], 256):
        ready(part)
        h = h_v[part]
        mid, mid_q, mid_v = middle(h, adapt_down)
        w.mid_t[:, part] = nt(identity(mid.shape[1]), mid).astype(BF16)
        for s, (ref, low) in enumerate(((w.q_v, mid_q), (w.k_v, None), (w.v_v, mid_v))):
            value = nt(h, w.qkv_v[s])
            if low is not None:
                value = value + nt(low, w.adapt_v[...])
            value = value.astype(BF16)
            span = ref.shape[2]
            for g in range(ref.shape[0]):
                ref[g, part] = value[:, g * span : (g + 1) * span]


def attend(q_v, k, v, bias, give):
    rows, span = k.shape
    chunk = 256
    zero = jnp.zeros((), BF16)
    for part in blocks_of(rows, chunk):
        q_c = q_v[part] * jnp.asarray(HEAD_DIM**-0.5, BF16)
        ctx = jnp.zeros((chunk, span), F32)
        inverse = jnp.zeros((chunk, span), F32)
        weights = []
        for e in range(span // HEAD_DIM):
            low = e * HEAD_DIM
            of_head = lane_mask(q_c.shape, low, low + HEAD_DIM)
            v_e = jnp.where(lane_mask(v.shape, low, low + HEAD_DIM), v, zero)
            s = nt(jnp.where(of_head, q_c, zero), k) + bias[part]
            weight = jnp.exp(s - jnp.max(s, -1, keepdims=True))
            scale = 1.0 / jnp.sum(weight, -1, keepdims=True)
            weight = weight.astype(BF16)
            ctx = ctx + nn(weight, v_e) * scale
            inverse = jnp.where(of_head, scale, inverse)
            give(part, e, weight, None)
        give(part, None, ctx.astype(BF16), inverse)


def attention_out(h_v, context, gains, biases, w, keep):
    groups, rows, span = context.shape
    for part in blocks_of(rows, 256):
        total = h_v[part].astype(F32)
        for g in range(groups):
            total = total + nn(context[g, part], w.out_v[g * span : (g + 1) * span])
        normed, scaled = normalize(total)
        if keep:
            w.n1_v[part] = normed
            w.s1_v[part] = scaled
        first = normed * gains[0:1] + biases[0:1]
        w.acc[part] = first
        w.low_v[part] = first.astype(BF16)


def feedforward_up(w, keep, ready):
    def step(slot, carry):
        ready(slot)
        for part in blocks_of(w.low_v.shape[0], 128):
            pre = nn(w.low_v[part], w.ff_v[0, slot])
            cdf = 0.5 + 0.5 * lax.erf(pre * (0.5**0.5))
            w.act_v[slot, part] = (pre * cdf).astype(BF16)
            if keep:
                density = jnp.exp(pre * pre * -0.5) * 0.3989422804014327
                w.slope_v[slot, part] = (cdf + pre * density).astype(BF16)
        return carry

    lax.fori_loop(0, w.act_v.shape[0], step, 0)


def backward(w, gains, adapt_down, incoming, give, sums):
    rows = w.acc.shape[0]
    slots = w.ff_v.shape[1]
    groups, _, span = w.q_v.shape
    for part in blocks_of(rows, 256):
        back = normalize_back(w.n2_v[part], w.s2_v[part], gains[1:2], incoming(part))
        w.acc[part] = back
        w.low_v[part] = back.astype(BF16)

        def step(slot, carry):
            dact = nt(w.low_v[part], w.ff_v[1, slot])
            w.act_v[slot, part] = (dact * w.slope_v[slot, part].astype(F32)).astype(BF16)
            return carry

        lax.fori_loop(0, slots, step, 0)
        total = w.acc[part]
        for slot in range(slots):
            total = total + nt(w.act_v[slot, part], w.ff_v[0, slot])
        back = normalize_back(w.n1_v[part], w.s1_v[part], gains[0:1], total)
        w.acc[part] = back
        dctx = nt(back.astype(BF16), w.out_v[...])
        for g in range(groups):
            scaled = dctx[:, g * span : (g + 1) * span] * w.inv_v[g, part]
            w.dctx_v[g, part] = scaled.astype(BF16)
    heads = span // HEAD_DIM
    factor = HEAD_DIM**-0.5

    def group(g, carry):
        q, k, v = w.q_v[g], w.k_v[g], w.v_v[g]
        dctx, ctx = w.dctx_v[g], w.ctx_v[g].astype(F32)
        q_t, dctx_t = q.T, dctx.T
        zero = jnp.zeros((), BF16)
        dq = jnp.zeros((rows, span), F32)
        dk_t, dv_t = [], []
        for e in range(heads):
            low, high = e * HEAD_DIM, (e + 1) * HEAD_DIM
            of_head = lane_mask((rows, span), low, high)
            weight = w.p_v[g * heads + e]
            dctx_e = jnp.where(of_head, dctx, zero)
            delta = jnp.sum(dctx_e.astype(F32) * ctx, -1, keepdims=True)
            ds = (weight.astype(F32) * (nt(dctx_e, v) - delta)).astype(BF16)
            dq = dq + nn(ds, jnp.where(of_head, k, zero))
            dk_t.append(nn(q_t[low:high], ds))
            dv_t.append(nn(dctx_t[low:high], weight))
        w.dq_v[g] = (dq * factor).astype(BF16)
        w.dk_v[g] = (jnp.concatenate(dk_t, 0) * factor).astype(BF16).T
        w.dv_v[g] = jnp.concatenate(dv_t, 0).astype(BF16).T
        return carry

    lax.fori_loop(0, groups, group, 0)
    rank = adapt_down.shape[0] // 2
    for part in blocks_of(rows, 256):
        dmid_q = dmid_v = 0.0
        for g in range(groups):
            cols = slice(g * span, (g + 1) * span)
            dmid_q = dmid_q + nn(w.dq_v[g, part], w.adapt_v[cols])
            dmid_v = dmid_v + nn(w.dv_v[g, part], w.adapt_v[cols])
        dmid = 2.0 * jnp.where(lane_mask(dmid_q.shape, 0, rank), dmid_q, dmid_v)
        w.dmid_v[part] = dmid.astype(BF16)
    sums()
    for part in blocks_of(rows, 256):
        total = w.acc[part]
        for g in range(groups):
            cols = slice(g * span, (g + 1) * span)
            for s, ref in enumerate((w.dq_v, w.dk_v, w.dv_v)):
                total = total + nn(ref[g, part], w.qkv_v[s, cols])
        give(part, (total + nn(w.dmid_v[part], adapt_down[...])).astype(BF16))


class Refs:
    def __init__(self, names, refs):
        self.__dict__.update(zip(names, refs, strict=True))


def whole_kernel(planes, names, *refs):
    embedded, segment, gains, biases, adapt_down, adapt, qkv, outw, up, down, cotangent = refs[:11]
    layer_outs, in_grads, down_out, up_out = refs[11:15]
    w = Refs(names, refs[15:])
    section, plane, tensor = (lax.axis_index(n) for n in ("section", "dp", "tensor"))
    core, far, paired, beyond, corner = neighbours()
    turned = lax.rem(tensor + 2, 4)
    other = tensor + 1 - 2 * lax.rem(tensor, 2)
    across = lax.rem(other + 2, 4)
    indices = (other, turned, across)
    sides = tuple((section, plane, i) for i in indices)
    ring = [(section, lax.rem(plane + m, planes), tensor) for m in range(1, planes)]
    rows, width = w.h_v.shape
    groups = w.q_v.shape[0]

    own = pl.ds(tensor * rows, rows)
    gather = Gather(
        (qkv, outw, up, down, w.adapt_own),
        (w.qkv_v, w.out_v, w.ff_v, w.adapt_v),
        w.act_v,
        (core, far, paired, beyond, corner),
        (w.send, w.recv, w.local),
    )
    for i in (1, 0, 2, 3):
        gather.load(i).start()
    pack_copies = [
        pltpu.make_async_copy(embedded.at[pl.ds(i * rows, rows)], w.slope_v.at[i], w.packs.at[i])
        for i in range(len(indices) + 1)
    ]
    for copy in pack_copies:
        copy.start()
    h_copy = pltpu.make_async_copy(embedded.at[own], w.h_v, w.local.at[5])
    h_copy.start()
    cot_copy = pltpu.make_async_copy(cotangent.at[own], w.cot_v, w.local.at[6])
    cot_copy.start()
    adapt_t = nt(identity(adapt.shape[1]), adapt[...]).astype(BF16)
    w.adapt_own[...] = adapt_t
    w.adapt_v[: adapt.shape[1]] = adapt_t
    meet((*sides, *ring, beyond, corner))

    for i in (1, 2, 3, 0):
        gather.load(i).wait()
    gather.adapt_far().start()
    for i in (4, 1, 2, 3, 0):
        gather.to_core(i).start()
    for copy in pack_copies:
        copy.wait()
    h_copy.wait()
    square = (rows, rows)
    piece = adapt.shape[1]
    pieces = blocks_of(rows, 256)

    def mask(pack):
        diagonal = lax.broadcasted_iota(jnp.int32, square, 0) == lax.broadcasted_iota(
            jnp.int32, square, 1
        )
        ids = segment[pl.ds(pack, 1), :].astype(F32)
        column = jnp.sum(jnp.where(diagonal, ids, 0.0), -1, keepdims=True)
        w.bias[...] = jnp.where(column == ids, 0.0, -1e9)

    def index_of(k):
        high = lax.rem(tensor // 2 + k // 2, 2)
        return 2 * high + lax.rem(lax.rem(tensor, 2) + lax.rem(k, 2), 2)

    def context_to(k):
        device = (section, plane, index_of(k))
        return remote(w.ctx_out.at[k], w.ctx_in.at[k], w.ctx_send.at[k], w.ctx_recv.at[k], device)

    def attend_pack(step, carry):
        k = 3 - step
        pack = index_of(k)
        mask(pack)
        h = w.slope_v[pack]
        _, mid_q, mid_v = middle(h, adapt_down)
        w.q_own[...] = (nt(h, w.qkv_v[0, :piece]) + nt(mid_q, w.adapt_own[...])).astype(BF16)
        k_own = nt(h, w.qkv_v[1, :piece]).astype(BF16)
        v_own = (nt(h, w.qkv_v[2, :piece]) + nt(mid_v, w.adapt_own[...])).astype(BF16)

        def give(part, head, value, inverse):
            if head is None:
                w.ctx_out[k, part] = value

        attend(w.q_own, k_own, v_own, w.bias, give)

        @pl.when(step < 3)
        def _():
            context_to(k).start()

        for i in (1, 2, 3):

            @pl.when(step == i)
            def _():
                gather.pump(i - 1, True)
                ask(i - 1 + gather.ahead)
                if i > 1:
                    gather.relay(i - 2, True)
                if i > 2:
                    gather.relay_last(i - 3)

        return carry

    def hop(way, i, src, dst):
        return remote(src, dst, w.hop_send.at[way, i], w.hop_recv.at[way, i], beyond)

    def ask(i):
        if i < gather.items:
            gather.issue(i, i < gather.through)

    @pl.when(section == 0)
    def _():
        for i in range(gather.ahead):
            ask(i)
        lax.fori_loop(0, 4, attend_pack, 0)
        w.ctx_in[0] = w.ctx_out[0]
        gather.adapt_far().wait_recv()
        gather.adapt_core().start()
        for k in (1, 2, 3):
            context_to(k).wait_recv()
        gather.to_core(1).wait_recv()
        gather.landed(0)
        attention_out(w.h_v, w.ctx_in, gains, biases, w, False)
        gather.pump(3, True)
        ask(3 + gather.ahead)
        gather.relay(2, True)
        gather.relay_last(1)
        for i in (2, 3):
            gather.to_core(i).wait_recv()

        def rest_of_up(slot):
            @pl.when(slot == 2)
            def _():
                gather.relay_last(2)
                gather.landed(1, 2)

            @pl.when(slot == 3)
            def _():
                gather.pump(4, True)
                ask(4 + gather.ahead)
                gather.relay(3, True)

        feedforward_up(w, False, rest_of_up)
        gather.relay_last(3)
        for part in blocks_of(rows, 256):
            w.acc[part] += nn(w.act_v[0, part], w.ff_v[1, 0]) + nn(w.act_v[1, part], w.ff_v[1, 1])
        gather.relay(4, True)
        gather.relay_last(4)
        gather.landed(3, 4)
        for i, part in enumerate(pieces):
            total = w.acc[part]
            for slot in (2, 3):
                total = total + nn(w.act_v[slot, part], w.ff_v[1, slot])
            w.hop_v[part] = (normalize(total)[0] * gains[1:2] + biases[1:2]).astype(BF16)
            hop(0, i, w.hop_v.at[part], w.recv_v.at[part]).start()
        for i in range(5, gather.items):
            gather.pump(i, False)
            ask(i + gather.ahead)
            if i > 5:
                gather.relay(i - 1, False)
        gather.relay(gather.items - 1, False)

    order = (5, 6, 7, 0, 1, 2, 3, 4)

    def own_step(n):
        gather.pump(order[n], False)
        if n + gather.ahead_own < gather.items:
            gather.issue(order[n + gather.ahead_own], False)
        if n > 0:
            gather.relay(order[n - 1], False)

    @pl.when(section == 1)
    def _():
        mask(tensor)
        gather.adapt_far().wait_recv()
        gather.adapt_core().start()
        for n in range(gather.ahead_own):
            gather.issue(order[n], False)
        for i in range(gather.through):
            gather.help(i)
            if i > 0:
                own_step(i - 1)
        for n in (4, 5, 6):
            own_step(n)
        for i in range(gather.through):
            gather.to_beyond(i).wait_send()
        gather.to_core(1).wait_recv()
        gather.landed(0)

    for i in (0, 4):
        gather.to_core(i).wait_recv()
    gather.adapt_core().wait_recv()
    gather.landed(5, 6, 7)

    def ready(part):
        @pl.when(section == 1)
        def _():
            hop(0, part.start // 256, w.hop_v.at[part], w.recv_v.at[part]).wait_recv()
            w.h_v[part] = w.recv_v[part]

    project(w.h_v, adapt_down, w, ready)

    def attend_group(g, carry):
        def give(part, head, value, inverse):
            if head is None:
                w.ctx_v[g, part] = value
                w.inv_v[g, part] = inverse
            else:
                w.p_v[g * (w.q_v.shape[2] // HEAD_DIM) + head, part] = value

        attend(w.q_v.at[g], w.k_v[g], w.v_v[g], w.bias, give)
        @pl.when(jnp.logical_and(section == 1, g == 0))
        def _():
            own_step(7)


        return carry

    lax.fori_loop(0, groups, attend_group, 0)
    attention_out(w.h_v, w.ctx_v, gains, biases, w, True)

    @pl.when(section == 1)
    def _():
        for i in (2, 3):
            gather.to_core(i).wait_recv()
        gather.landed(1, 2)

    def rest_of_down(slot):
        @pl.when(jnp.logical_and(section == 1, slot == 3))
        def _():
            gather.relay(order[7], False)

    feedforward_up(w, True, rest_of_down)

    @pl.when(section == 1)
    def _():
        gather.landed(3, 4)

    def block(out, index, part):
        return out.at[pl.ds(index * rows + part.start, part.size)]

    def rows_to(n, way, i, src, out, part, device):
        sems = w.row_send.at[n, way, i], w.row_recv.at[n, way, i]
        return remote(src.at[part], block(out, tensor, part), *sems, device)

    def rows_far(n, i, src, out, part):
        return rows_to(n, 0, i, src, out, part, far)

    def rows_core(n, i, src, out, part):
        return rows_to(n, 1, i, src, out, part, core)

    def rows_mine(n, i, src, out, part):
        return pltpu.make_async_copy(src.at[part], block(out, tensor, part), w.local.at[7 + 4 * n + i])

    def rows_relay(n, i, out, part):
        landed = block(out, turned, part)
        return remote(landed, landed, w.row_send.at[n, 2, i], w.row_recv.at[n, 2, i], core)

    def spread(n, i, src, out, part):
        for make in (rows_far, rows_core, rows_mine):
            make(n, i, src, out, part).start()

    def relay_rows(n, i, src, out, part):
        rows_far(n, i, src, out, part).wait_recv()
        rows_relay(n, i, out, part).start()

    def gathered(n, i, src, out, part):
        rows_core(n, i, src, out, part).wait()
        rows_relay(n, i, out, part).wait()
        rows_mine(n, i, src, out, part).wait()

    ends = (pl.ds(0, 128), pl.ds(128, 128), pl.ds(256, rows - 256))

    def through_corner(src):
        sems = w.row_send.at[1, 1, 3], w.row_recv.at[1, 1, 3]
        return remote(src.at[ends[0]], w.back_v.at[ends[0]], *sems, corner)

    def through_beyond():
        sems = w.row_send.at[1, 0, 3], w.row_recv.at[1, 0, 3]
        return remote(w.back_v.at[ends[0]], block(in_grads, turned, ends[0]), *sems, beyond)

    for i, part in enumerate(pieces):
        total = w.acc[part]
        for slot in range(w.ff_v.shape[1]):
            total = total + nn(w.act_v[slot, part], w.ff_v[1, slot])
        normed, scaled = normalize(total)
        w.n2_v[part] = normed
        w.s2_v[part] = scaled
        w.layer_v[part] = (normed * gains[1:2] + biases[1:2]).astype(BF16)
        spread(0, i, w.layer_v, layer_outs, part)

    cot_copy.wait()
    rank = adapt_down.shape[0] // 2

    def incoming(again, part):
        @pl.when(jnp.logical_and(again == 1, section == 0))
        def _():
            hop(1, part.start // 256, w.dh_v.at[part], w.back_v.at[part]).wait_recv()
            w.cot_v[part] = w.back_v[part]

        return w.cot_v[part].astype(F32)

    def summed(n, src, dst, device):
        return remote(src, dst, w.sum_send.at[n], w.sum_recv.at[n], device)

    def over_tensor(landing):
        copies = []
        for i, device in enumerate(sides):
            slot = indices[i] if landing else tensor
            for src, dst in (
                (w.grad_down, w.from_down.at[slot]),
                (w.grad_up.at[i + 1], w.from_up.at[i]),
            ):
                copies.append(summed(len(copies), src, dst, device))
        return copies

    def adapter_gradients(again):
        @pl.when(again == 1)
        def _():
            dmid_t = nt(identity(2 * rank), w.dmid_v[...]).astype(BF16)
            grad_down = nn(dmid_t, w.h_v[...])
            for j in range(2):
                w.grad_down[j] = grad_down[j * rank : (j + 1) * rank]
            up_q, up_v = (
                jnp.concatenate([2.0 * nn(w.mid_t[...], ref[g]) for g in range(groups)], 1)
                for ref in (w.dq_v, w.dv_v)
            )
            for i in range(len(sides) + 1):
                cols = slice(i * piece, (i + 1) * piece)
                w.grad_up[i, 0] = up_q[:rank, cols]
                w.grad_up[i, 1] = up_v[rank:, cols]
            w.from_down[tensor] = w.grad_down[...]
            for copy in over_tensor(False):
                copy.start()

    def hand_over(again, part, value):
        here = [n for n, end in enumerate(ends) if 0 <= end.start - part.start < part.size]

        @pl.when(jnp.logical_and(again == 0, section == 1))
        def _():
            w.dh_v[part] = value
            hop(1, part.start // 256, w.dh_v.at[part], w.back_v.at[part]).start()
            for n in here:
                spread(1, n, w.dh_v, in_grads, ends[n])

        @pl.when(jnp.logical_and(again == 1, section == 0))
        def _():
            w.dh_v[part] = value
            for n in here:
                if n:
                    rows_far(1, n, w.dh_v, in_grads, ends[n]).start()
                else:
                    through_corner(w.dh_v).start()
                rows_core(1, n, w.dh_v, in_grads, ends[n]).start()
                rows_mine(1, n, w.dh_v, in_grads, ends[n]).start()

    def back(again, carry):
        backward(
            w,
            gains,
            adapt_down,
            partial(incoming, again),
            partial(hand_over, again),
            partial(adapter_gradients, again),
        )

        @pl.when(again == 0)
        def _():
            for i, part in enumerate(pieces):
                relay_rows(0, i, w.layer_v, layer_outs, part)

        return carry

    lax.fori_loop(0, 2, back, 0)

    @pl.when(section == 1)
    def _():
        for n, end in enumerate(ends):
            relay_rows(1, n, w.dh_v, in_grads, end)
        through_corner(w.dh_v).wait_recv()
        through_beyond().start()

    tensor_copies = over_tensor(True)
    for copy in tensor_copies:
        copy.wait()
    w.plane_down[plane] = w.from_down[0] + w.from_down[1] + w.from_down[2] + w.from_down[3]
    w.plane_up[plane] = w.grad_up[0] + w.from_up[0] + w.from_up[1] + w.from_up[2]
    base = len(tensor_copies)
    totals = (w.plane_down, w.plane_up)
    for m, device in enumerate(ring):
        for k, ref in enumerate(totals):
            summed(base + 2 * m + k, ref.at[plane], ref.at[plane], device).start()

    @pl.when(section == 0)
    def _():
        relay_rows(1, 1, w.dh_v, in_grads, ends[1])

    for m, device in enumerate(ring):
        source = lax.rem(plane + planes - m - 1, planes)
        for k, ref in enumerate(totals):
            summed(base + 2 * m + k, ref.at[source], ref.at[source], device).wait_recv()
    for m, device in enumerate(ring):
        for k, ref in enumerate(totals):
            summed(base + 2 * m + k, ref.at[plane], ref.at[plane], device).wait_send()
    down_total, up_total = w.plane_down[0], w.plane_up[0]
    for m in range(1, planes):
        down_total = down_total + w.plane_down[m]
        up_total = up_total + w.plane_up[m]
    up_out[...] = up_total
    down_out[...] = down_total

    @pl.when(section == 0)
    def _():
        through_beyond().wait_recv()
        rows_relay(1, 0, in_grads, ends[0]).start()
        relay_rows(1, 2, w.dh_v, in_grads, ends[2])
        through_corner(w.dh_v).wait_send()
        for n in (1, 2):
            rows_far(1, n, w.dh_v, in_grads, ends[n]).wait_send()
        for i, part in enumerate(pieces):
            hop(0, i, w.hop_v.at[part], w.recv_v.at[part]).wait_send()
        for k in (1, 2, 3):
            context_to(k).wait_send()
        gather.sent(0)

    @pl.when(section == 1)
    def _():
        through_beyond().wait_send()
        for n, end in enumerate(ends):
            rows_far(1, n, w.dh_v, in_grads, end).wait_send()
        for i, part in enumerate(pieces):
            hop(1, i, w.dh_v.at[part], w.back_v.at[part]).wait_send()
        gather.sent(1)

    for i, part in enumerate(pieces):
        rows_far(0, i, w.layer_v, layer_outs, part).wait_send()
        gathered(0, i, w.layer_v, layer_outs, part)
    for n, end in enumerate(ends):
        gathered(1, n, w.dh_v, in_grads, end)


def local(
    embedded,
    segment,
    query_key_value_weight,
    attention_output_weight,
    feedforward_up_weight,
    feedforward_down_weight,
    adapter_down_weight,
    adapter_up_weight,
    layer_norm_gain,
    layer_norm_bias,
    cotangent,
):
    slots, packs, planes = lax.axis_size("tensor"), segment.shape[0], lax.axis_size("dp")
    assert slots == 4 and packs == slots and planes % 2 == 0
    rows, width = segment.shape[1], embedded.shape[1]
    piece = query_key_value_weight.shape[3]
    wide = feedforward_up_weight.shape[2]
    assert wide == width
    rank = adapter_down_weight.shape[3]
    span = 256
    groups = width // span
    heads = width // HEAD_DIM

    def arr(shape, dtype):
        return jax.ShapeDtypeStruct(shape, dtype)

    low_rows = pltpu.VMEM((rows, width), BF16)
    full_rows = pltpu.VMEM((rows, width), F32)
    of_heads = pltpu.VMEM((groups, rows, span), BF16)
    of_hidden = pltpu.VMEM((slots, rows, wide), BF16)
    down_part = (2, rank, width)
    up_part = (2, rank, piece)
    sums = 2 * (slots - 1) + 2 * (planes - 1)
    scratch = dict(
        qkv_v=pltpu.VMEM((3, width, width), BF16),
        out_v=pltpu.VMEM((width, width), BF16),
        ff_v=pltpu.VMEM((2, slots, width, wide), BF16),
        adapt_v=pltpu.VMEM((width, 2 * rank), BF16),
        adapt_own=pltpu.VMEM((piece, 2 * rank), BF16),
        q_own=pltpu.VMEM((rows, piece), BF16),
        ctx_out=pltpu.VMEM((slots, rows, piece), BF16),
        ctx_in=pltpu.VMEM((slots, rows, piece), BF16),
        inv_v=pltpu.VMEM((groups, rows, span), F32),
        p_v=pltpu.VMEM((heads, rows, rows), BF16),
        s1_v=pltpu.VMEM((rows, 1), F32),
        s2_v=pltpu.VMEM((rows, 1), F32),
        bias=pltpu.VMEM((rows, rows), F32),
        mid_t=pltpu.VMEM((2 * rank, rows), BF16),
        dmid_v=pltpu.VMEM((rows, 2 * rank), BF16),
        grad_down=pltpu.VMEM(down_part, F32),
        grad_up=pltpu.VMEM((slots, *up_part), F32),
        from_down=pltpu.VMEM((slots, *down_part), F32),
        from_up=pltpu.VMEM((slots - 1, *up_part), F32),
        plane_down=pltpu.VMEM((planes, *down_part), F32),
        plane_up=pltpu.VMEM((planes, *up_part), F32),
        local=pltpu.SemaphoreType.DMA((15,)),
        packs=pltpu.SemaphoreType.DMA((packs,)),
        send=pltpu.SemaphoreType.DMA((11, Gather.items)),
        recv=pltpu.SemaphoreType.DMA((11, Gather.items)),
        ctx_send=pltpu.SemaphoreType.DMA((slots,)),
        ctx_recv=pltpu.SemaphoreType.DMA((slots,)),
        hop_send=pltpu.SemaphoreType.DMA((2, rows // 128)),
        hop_recv=pltpu.SemaphoreType.DMA((2, rows // 128)),
        row_send=pltpu.SemaphoreType.DMA((2, 3, rows // 128)),
        row_recv=pltpu.SemaphoreType.DMA((2, 3, rows // 128)),
        sum_send=pltpu.SemaphoreType.DMA((sums,)),
        sum_recv=pltpu.SemaphoreType.DMA((sums,)),
    )
    scratch |= dict.fromkeys(("h_v", "recv_v", "back_v", "cot_v", "low_v"), low_rows)
    scratch |= dict.fromkeys(("hop_v", "layer_v", "dh_v"), low_rows)
    scratch |= dict.fromkeys(("acc", "n1_v", "n2_v"), full_rows)
    scratch |= dict.fromkeys(("q_v", "k_v", "v_v", "ctx_v"), of_heads)
    scratch |= dict.fromkeys(("dq_v", "dk_v", "dv_v", "dctx_v"), of_heads)
    scratch |= dict.fromkeys(("act_v", "slope_v"), of_hidden)
    layer_outs, in_grads, grad_a, grad_b = pl.pallas_call(
        partial(whole_kernel, planes, tuple(scratch)),
        name="encoder_layers",
        out_shape=[
            pltpu.VMEM((packs * rows, width), BF16),
            pltpu.VMEM((packs * rows, width), BF16),
            arr(down_part, F32),
            arr(up_part, F32),
        ],
        in_specs=[ANY] + [VMEM] * 5 + [ANY] * 5,
        out_specs=[VMEM] * 4,
        scratch_shapes=list(scratch.values()),
        compiler_params=pltpu.CompilerParams(
            vmem_limit_bytes=VMEM_LIMIT, collective_id=0, has_side_effects=True
        ),
        cost_estimate=pl.CostEstimate(
            flops=7 * 10**10, bytes_accessed=3 * 10**7, transcendentals=0
        ),
    )(
        embedded,
        segment,
        layer_norm_gain[0],
        layer_norm_bias[0],
        jnp.swapaxes(adapter_down_weight[0], 1, 2).reshape(2 * rank, width),
        adapter_up_weight[0].reshape(2 * rank, piece),
        jnp.swapaxes(query_key_value_weight[0], 1, 2),
        attention_output_weight[0],
        feedforward_up_weight[0],
        feedforward_down_weight[0],
        cotangent,
    )
    grad_a = jnp.swapaxes(grad_a, 1, 2)
    return (layer_outs[None], in_grads[None], grad_a[None], grad_b[None])


def solution(mesh):
    in_specs = (
        P("dp", None),
        P("dp", None),
        P("section", None, None, "tensor"),
        P("section", "tensor", None),
        P("section", None, "tensor"),
        P("section", "tensor", None),
        P("section", None, None, None),
        P("section", None, None, "tensor"),
        P("section", None, None),
        P("section", None, None),
        P("dp", None),
    )
    out_specs = (
        P("section", "dp", None),
        P("section", "dp", None),
        P("section", None, None, None),
        P("section", None, None, "tensor"),
    )
    return jax.shard_map(local, mesh=mesh, in_specs=in_specs, out_specs=out_specs, check_vma=False)
```

```python
from functools import partial

import jax
import jax.numpy as jnp
from jax import lax
from jax.experimental import pallas as pl
from jax.experimental.pallas import tpu as pltpu
from jax.sharding import PartitionSpec as P

HEAD_DIM = 64
EPS = 1e-05
VMEM_LIMIT = 115 * 2**19
F32 = jnp.float32
BF16 = jnp.bfloat16
ANY = pl.BlockSpec(memory_space=pl.ANY)
VMEM = pl.BlockSpec(memory_space=pltpu.VMEM)
MESH = pl.DeviceIdType.MESH
SMEM = pl.BlockSpec(memory_space=pltpu.SMEM)


def nn(a, b):
    return jnp.dot(a, b, preferred_element_type=F32)


def nt(a, b):
    return lax.dot_general(a, b, (((1,), (1,)), ((), ())), preferred_element_type=F32)


def lane_mask(shape, low, high):
    lanes = lax.broadcasted_iota(jnp.int32, shape, len(shape) - 1)
    return (lanes >= low) & (lanes < high)


def normalize(total):
    average = jnp.mean(total, -1, keepdims=True)
    centred = total - average
    spread = jnp.mean(centred * centred, -1, keepdims=True)
    scaled = lax.rsqrt(spread + EPS)
    return centred * scaled, scaled


def normalize_back(normed, scaled, gains, incoming):
    weighted = incoming * gains
    return scaled * (
        weighted
        - jnp.mean(weighted, -1, keepdims=True)
        - normed * jnp.mean(weighted * normed, -1, keepdims=True)
    )


def neighbours():
    section, plane, tensor = (lax.axis_index(n) for n in ("section", "dp", "tensor"))
    turned = lax.rem(tensor + 2, 4)
    other = tensor + 1 - 2 * lax.rem(tensor, 2)
    paired = plane + 1 - 2 * lax.rem(plane, 2)
    return (
        (section, plane, other),
        (section, plane, turned),
        (section, paired, tensor),
        (1 - section, plane, tensor),
        (1 - section, plane, turned),
    )


def meet(devices):
    barrier = pltpu.get_barrier_semaphore()
    for device in devices:
        pl.semaphore_signal(barrier, inc=1, device_id=device, device_id_type=MESH)
    pl.semaphore_wait(barrier, len(devices))


def remote(src, dst, send, recv, device):
    return pltpu.make_async_remote_copy(
        src_ref=src,
        dst_ref=dst,
        send_sem=send,
        recv_sem=recv,
        device_id=device,
        device_id_type=MESH,
    )


def identity(n):
    rows = lax.broadcasted_iota(jnp.int32, (n, n), 0)
    return (rows == lax.broadcasted_iota(jnp.int32, (n, n), 1)).astype(BF16)


def blocks_of(rows, size):
    return [pl.ds(r, size) for r in range(0, rows, size)]


class Gather:
    items, ahead, ahead_own = 8, 2, 8
    through = 5

    def __init__(self, own, gathered, resting, partners, sems):
        self.qkv, self.outw, self.up, self.down, self.adapt = own
        self.qkv_v, self.out_v, self.ff_v, self.adapt_v = gathered
        self.resting_v = resting
        self.core, self.far, self.plane, self.beyond, self.corner = partners
        self.send, self.recv, self.local = sems
        self.parity = lax.rem(lax.axis_index("dp"), 2)
        self.n_qkv, self.n_out = self.qkv.shape[1], self.outw.shape[0]
        self.n_ff, self.n_adapt = self.up.shape[0], self.adapt.shape[0]

    def block(self, i, slot, third):
        if i == 0:
            size = self.n_out // 3
            return self.out_v.at[pl.ds(slot * self.n_out + third * size, size)]
        if i >= 5:
            size = self.n_qkv // 3
            return self.qkv_v.at[i - 5, pl.ds(slot * self.n_qkv + third * size, size)]
        which, j = divmod(i - 1, 2)
        rows = self.n_ff // 3
        size = rows // 2
        return self.ff_v.at[which, slot, pl.ds(third * rows + j * size, size)]

    def resting(self, i):
        size = self.n_out // 3 if i == 0 else self.n_ff // 6
        return self.resting_v.at[i // 4, pl.ds(i % 4 * (self.n_ff // 6), size)]

    def whole(self, i, slot):
        if i == 0:
            return self.qkv_v.at[:, pl.ds(slot * self.n_qkv, self.n_qkv)]
        if i == 1:
            return self.out_v.at[pl.ds(slot * self.n_out, self.n_out)]
        if i == 4:
            return self.adapt_v.at[pl.ds(slot * self.n_adapt, self.n_adapt)]
        return self.ff_v.at[i - 2, slot]

    def link(self, kind, i, src, dst, device):
        return remote(src, dst, self.send.at[kind, i], self.recv.at[kind, i], device)

    def over_far(self, i):
        p = self.parity
        return self.link(0, i, self.block(i, 0, p), self.block(i, 2, p), self.far)

    def to_plane(self, i, third):
        here = self.block(i, 2, third)
        return self.link(1, i, here, here, self.plane)

    def pass_on(self, i, kind):
        third = (self.parity, 1 - self.parity, 2)[kind]
        return self.link(2 + kind, i, self.block(i, 2, third), self.block(i, 3, third), self.core)

    def to_corner(self, i):
        return self.link(7, i, self.block(i, 0, 2), self.resting(i), self.corner)

    def to_beyond(self, i):
        return self.link(8, i, self.resting(i), self.block(i, 2, 2), self.beyond)

    def last_far(self, i):
        return self.link(9, i, self.block(i, 0, 2), self.block(i, 2, 2), self.far)

    def last_plane(self, i):
        here = self.block(i, 2, 2)
        return self.link(10, i, here, here, self.plane)

    def load(self, i):
        own = (self.qkv, self.outw, self.up, self.down, self.adapt)[i]
        return pltpu.make_async_copy(own, self.whole(i, 0), self.local.at[i])

    def to_core(self, i):
        return self.link(5, i, self.whole(i, 0), self.whole(i, 1), self.core)

    def adapt_far(self):
        return self.link(6, 0, self.whole(4, 0), self.whole(4, 2), self.far)

    def adapt_core(self):
        return self.link(6, 1, self.whole(4, 2), self.whole(4, 3), self.core)

    def when_last(self, i, mine):
        here = i % 2
        return pl.when(self.parity == (here if mine else 1 - here))

    def issue(self, i, through):
        self.over_far(i).start()
        if through:
            self.to_corner(i).start()
        else:

            @self.when_last(i, True)
            def _():
                self.last_far(i).start()

    def pump(self, i, through):
        self.over_far(i).wait_recv()
        self.to_plane(i, self.parity).start()
        self.pass_on(i, 0).start()
        if not through:

            @self.when_last(i, True)
            def _():
                self.last_far(i).wait_recv()
                self.last_plane(i).start()
                self.pass_on(i, 2).start()

    def relay(self, i, through):
        self.to_plane(i, 1 - self.parity).wait_recv()
        self.pass_on(i, 1).start()
        if not through:

            @self.when_last(i, False)
            def _():
                self.last_plane(i).wait_recv()
                self.pass_on(i, 2).start()

    def relay_last(self, i):
        self.to_beyond(i).wait_recv()
        self.pass_on(i, 2).start()

    def help(self, i):
        self.to_corner(i).wait_recv()
        self.to_beyond(i).start()

    def landed(self, *items):
        for i in items:
            for kind in range(3):
                self.pass_on(i, kind).wait_recv()

    def sent(self, section):
        for i in range(self.items):
            self.over_far(i).wait_send()
            self.to_plane(i, self.parity).wait_send()
            for kind in range(3):
                self.pass_on(i, kind).wait_send()
            if section == 0 and i < self.through:
                self.to_corner(i).wait_send()
            else:

                @self.when_last(i, True)
                def _():
                    self.last_far(i).wait_send()
                    self.last_plane(i).wait_send()

        for i in range(5):
            self.to_core(i).wait_send()
        self.adapt_far().wait_send()
        self.adapt_core().wait_send()


def middle(h, adapt_down):
    rank = adapt_down.shape[0] // 2
    mid = nt(h, adapt_down[...]).astype(BF16)
    is_query = lane_mask(mid.shape, 0, rank)
    double = mid * jnp.asarray(2.0, BF16)
    zero = jnp.zeros((), BF16)
    return mid, jnp.where(is_query, double, zero), jnp.where(is_query, zero, double)


def project(h_v, adapt_down, w, ready):
    for part in blocks_of(h_v.shape[0], 256):
        ready(part)
        h = h_v[part]
        mid, mid_q, mid_v = middle(h, adapt_down)
        w.mid_t[:, part] = nt(identity(mid.shape[1]), mid).astype(BF16)
        for s, (ref, low) in enumerate(((w.q_v, mid_q), (w.k_v, None), (w.v_v, mid_v))):
            value = nt(h, w.qkv_v[s])
            if low is not None:
                value = value + nt(low, w.adapt_v[...])
            value = value.astype(BF16)
            span = ref.shape[2]
            for g in range(ref.shape[0]):
                ref[g, part] = value[:, g * span : (g + 1) * span]


def attend(q_v, k, v, bias, give):
    rows, span = k.shape
    chunk = 256
    zero = jnp.zeros((), BF16)
    for part in blocks_of(rows, chunk):
        q_c = q_v[part] * jnp.asarray(HEAD_DIM**-0.5, BF16)
        ctx = jnp.zeros((chunk, span), F32)
        inverse = jnp.zeros((chunk, span), F32)
        weights = []
        for e in range(span // HEAD_DIM):
            low = e * HEAD_DIM
            of_head = lane_mask(q_c.shape, low, low + HEAD_DIM)
            v_e = jnp.where(lane_mask(v.shape, low, low + HEAD_DIM), v, zero)
            s = nt(jnp.where(of_head, q_c, zero), k) + bias[part]
            weight = jnp.exp(s - jnp.max(s, -1, keepdims=True))
            scale = 1.0 / jnp.sum(weight, -1, keepdims=True)
            weight = weight.astype(BF16)
            ctx = ctx + nn(weight, v_e) * scale
            inverse = jnp.where(of_head, scale, inverse)
            give(part, e, weight, None)
        give(part, None, ctx.astype(BF16), inverse)


def attention_out(h_v, context, gains, biases, w, keep):
    groups, rows, span = context.shape
    for part in blocks_of(rows, 256):
        total = h_v[part].astype(F32)
        for g in range(groups):
            total = total + nn(context[g, part], w.out_v[g * span : (g + 1) * span])
        normed, scaled = normalize(total)
        if keep:
            w.n1_v[part] = normed
            w.s1_v[part] = scaled
        first = normed * gains[0:1] + biases[0:1]
        w.acc[part] = first
        w.low_v[part] = first.astype(BF16)


def feedforward_up(w, keep, ready):
    rows = w.low_v.shape[0]

    def one(slot, part):
        pre = nn(w.low_v[part], w.ff_v[0, slot])
        cdf = 0.5 + 0.5 * lax.erf(pre * (0.5**0.5))
        w.act_v[slot, part] = (pre * cdf).astype(BF16)
        if keep:
            density = jnp.exp(pre * pre * -0.5) * 0.3989422804014327
            w.slope_v[slot, part] = (cdf + pre * density).astype(BF16)

    def small_step(slot, carry):
        ready(slot)

        def some(i, carry):
            one(slot, pl.ds(pl.multiple_of(i * 256, 256), 256))
            return carry

        return lax.fori_loop(0, rows // 256, some, carry)

    if keep:
        for slot in range(w.act_v.shape[0]):
            ready(jnp.int32(slot))
            for part in blocks_of(rows, 128):
                one(slot, part)
    else:
        lax.fori_loop(0, w.act_v.shape[0], small_step, 0)


def backward(w, gains, adapt_down, incoming, give, sums):
    rows = w.acc.shape[0]
    slots = w.ff_v.shape[1]
    groups, _, span = w.q_v.shape
    for part in blocks_of(rows, 256):
        back = normalize_back(w.n2_v[part], w.s2_v[part], gains[1:2], incoming(part))
        w.acc[part] = back
        w.low_v[part] = back.astype(BF16)

        def step(slot, carry):
            dact = nt(w.low_v[part], w.ff_v[1, slot])
            w.act_v[slot, part] = (dact * w.slope_v[slot, part].astype(F32)).astype(BF16)
            return carry

        for slot in range(slots):
            step(slot, 0)
        total = w.acc[part]
        for slot in range(slots):
            total = total + nt(w.act_v[slot, part], w.ff_v[0, slot])
        back = normalize_back(w.n1_v[part], w.s1_v[part], gains[0:1], total)
        w.acc[part] = back
        dctx = nt(back.astype(BF16), w.out_v[...])
        for g in range(groups):
            scaled = dctx[:, g * span : (g + 1) * span] * w.inv_v[g, part]
            w.dctx_v[g, part] = scaled.astype(BF16)
    heads = span // HEAD_DIM
    factor = HEAD_DIM**-0.5

    def group(g, carry):
        q, k, v = w.q_v[g], w.k_v[g], w.v_v[g]
        dctx, ctx = w.dctx_v[g], w.ctx_v[g].astype(F32)
        q_t, dctx_t = q.T, dctx.T
        zero = jnp.zeros((), BF16)
        dq = jnp.zeros((rows, span), F32)
        dk_t, dv_t = [], []
        for e in range(heads):
            low, high = e * HEAD_DIM, (e + 1) * HEAD_DIM
            of_head = lane_mask((rows, span), low, high)
            weight = w.p_v[g * heads + e]
            dctx_e = jnp.where(of_head, dctx, zero)
            delta = jnp.sum(dctx_e.astype(F32) * ctx, -1, keepdims=True)
            ds = (weight.astype(F32) * (nt(dctx_e, v) - delta)).astype(BF16)
            dq = dq + nn(ds, jnp.where(of_head, k, zero))
            dk_t.append(nn(q_t[low:high], ds))
            dv_t.append(nn(dctx_t[low:high], weight))
        w.dq_v[g] = (dq * factor).astype(BF16)
        w.dk_v[g] = (jnp.concatenate(dk_t, 0) * factor).astype(BF16).T
        w.dv_v[g] = jnp.concatenate(dv_t, 0).astype(BF16).T
        return carry

    lax.fori_loop(0, groups, group, 0)
    rank = adapt_down.shape[0] // 2
    for part in blocks_of(rows, 256):
        dmid_q = dmid_v = 0.0
        for g in range(groups):
            cols = slice(g * span, (g + 1) * span)
            dmid_q = dmid_q + nn(w.dq_v[g, part], w.adapt_v[cols])
            dmid_v = dmid_v + nn(w.dv_v[g, part], w.adapt_v[cols])
        dmid = 2.0 * jnp.where(lane_mask(dmid_q.shape, 0, rank), dmid_q, dmid_v)
        w.dmid_v[part] = dmid.astype(BF16)
    sums()
    for part in blocks_of(rows, 256):
        total = w.acc[part]
        for g in range(groups):
            cols = slice(g * span, (g + 1) * span)
            for s, ref in enumerate((w.dq_v, w.dk_v, w.dv_v)):
                total = total + nn(ref[g, part], w.qkv_v[s, cols])
        give(part, (total + nn(w.dmid_v[part], adapt_down[...])).astype(BF16))


class Refs:
    def __init__(self, names, refs):
        self.__dict__.update(zip(names, refs, strict=True))


def whole_kernel(planes, names, *refs):
    embedded, segment, gains, biases, adapt_down, adapt, qkv, outw, up, down, cotangent = refs[:11]
    layer_outs, in_grads, down_out, up_out = refs[11:15]
    w = Refs(names, refs[15:])
    section, plane, tensor = (lax.axis_index(n) for n in ("section", "dp", "tensor"))
    core, far, paired, beyond, corner = neighbours()
    turned = lax.rem(tensor + 2, 4)
    other = tensor + 1 - 2 * lax.rem(tensor, 2)
    across = lax.rem(other + 2, 4)
    indices = (other, turned, across)
    sides = tuple((section, plane, i) for i in indices)
    ring = [(section, lax.rem(plane + m, planes), tensor) for m in range(1, planes)]
    rows, width = w.h_v.shape
    groups = w.q_v.shape[0]

    own = pl.ds(tensor * rows, rows)
    gather = Gather(
        (qkv, outw, up, down, w.adapt_own),
        (w.qkv_v, w.out_v, w.ff_v, w.adapt_v),
        w.act_v,
        (core, far, paired, beyond, corner),
        (w.send, w.recv, w.local),
    )
    for i in (1, 0, 2, 3):
        gather.load(i).start()
    pack_copies = [
        pltpu.make_async_copy(embedded.at[pl.ds(i * rows, rows)], w.slope_v.at[i], w.packs.at[i])
        for i in range(len(indices) + 1)
    ]
    for copy in pack_copies:
        copy.start()
    h_copy = pltpu.make_async_copy(embedded.at[own], w.h_v, w.local.at[5])
    h_copy.start()
    cot_copy = pltpu.make_async_copy(cotangent.at[own], w.cot_v, w.local.at[6])
    cot_copy.start()
    adapt_t = nt(identity(adapt.shape[1]), adapt[...]).astype(BF16)
    w.adapt_own[...] = adapt_t
    w.adapt_v[: adapt.shape[1]] = adapt_t
    meet((*sides, *ring, beyond, corner))

    for i in (1, 2, 3, 0):
        gather.load(i).wait()
    gather.adapt_far().start()
    for i in (4, 1, 2, 3, 0):
        gather.to_core(i).start()
    for copy in pack_copies:
        copy.wait()
    h_copy.wait()
    square = (rows, rows)
    piece = adapt.shape[1]
    pieces = blocks_of(rows, 256)

    def mask(pack):
        diagonal = lax.broadcasted_iota(jnp.int32, square, 0) == lax.broadcasted_iota(
            jnp.int32, square, 1
        )
        ids = segment[pl.ds(pack, 1), :].astype(F32)
        column = jnp.sum(jnp.where(diagonal, ids, 0.0), -1, keepdims=True)
        w.bias[...] = jnp.where(column == ids, 0.0, -1e9)

    def index_of(k):
        high = lax.rem(tensor // 2 + k // 2, 2)
        return 2 * high + lax.rem(lax.rem(tensor, 2) + lax.rem(k, 2), 2)

    def context_to(k):
        device = (section, plane, index_of(k))
        return remote(w.ctx_out.at[k], w.ctx_in.at[k], w.ctx_send.at[k], w.ctx_recv.at[k], device)

    def attend_pack(step, carry):
        k = 3 - step
        pack = index_of(k)
        mask(pack)
        h = w.slope_v[pack]
        _, mid_q, mid_v = middle(h, adapt_down)
        w.q_own[...] = (nt(h, w.qkv_v[0, :piece]) + nt(mid_q, w.adapt_own[...])).astype(BF16)
        k_own = nt(h, w.qkv_v[1, :piece]).astype(BF16)
        v_own = (nt(h, w.qkv_v[2, :piece]) + nt(mid_v, w.adapt_own[...])).astype(BF16)

        def give(part, head, value, inverse):
            if head is None:
                w.ctx_out[k, part] = value

        attend(w.q_own, k_own, v_own, w.bias, give)

        @pl.when(step < 3)
        def _():
            context_to(k).start()

        for i in (1, 2, 3):

            @pl.when(step == i)
            def _():
                gather.pump(i - 1, True)
                ask(i - 1 + gather.ahead)
                if i > 1:
                    gather.relay(i - 2, True)
                if i > 2:
                    gather.relay_last(i - 3)

        return carry

    def hop(way, i, src, dst):
        return remote(src, dst, w.hop_send.at[way, i], w.hop_recv.at[way, i], beyond)

    def ask(i):
        if i < gather.items:
            gather.issue(i, i < gather.through)

    @pl.when(section == 0)
    def _():
        for i in range(gather.ahead):
            ask(i)
        lax.fori_loop(0, 4, attend_pack, 0)
        w.ctx_in[0] = w.ctx_out[0]
        gather.adapt_far().wait_recv()
        gather.adapt_core().start()
        for k in (1, 2, 3):
            context_to(k).wait_recv()
        gather.to_core(1).wait_recv()
        gather.landed(0)
        attention_out(w.h_v, w.ctx_in, gains, biases, w, False)
        gather.pump(3, True)
        ask(3 + gather.ahead)
        gather.relay(2, True)
        gather.relay_last(1)
        for i in (2, 3):
            gather.to_core(i).wait_recv()

        def rest_of_up(slot):
            @pl.when(slot == 2)
            def _():
                gather.relay_last(2)
                gather.landed(1, 2)

            @pl.when(slot == 3)
            def _():
                gather.pump(4, True)
                ask(4 + gather.ahead)
                gather.relay(3, True)

        feedforward_up(w, False, rest_of_up)
        gather.relay_last(3)
        for part in blocks_of(rows, 256):
            w.acc[part] += nn(w.act_v[0, part], w.ff_v[1, 0]) + nn(w.act_v[1, part], w.ff_v[1, 1])
        gather.relay(4, True)
        gather.relay_last(4)
        gather.landed(3, 4)
        for i, part in enumerate(pieces):
            total = w.acc[part]
            for slot in (2, 3):
                total = total + nn(w.act_v[slot, part], w.ff_v[1, slot])
            w.hop_v[part] = (normalize(total)[0] * gains[1:2] + biases[1:2]).astype(BF16)
            hop(0, i, w.hop_v.at[part], w.recv_v.at[part]).start()
        for i in range(5, gather.items):
            gather.pump(i, False)
            ask(i + gather.ahead)
            if i > 5:
                gather.relay(i - 1, False)
        gather.relay(gather.items - 1, False)

    order = (5, 6, 7, 0, 1, 2, 3, 4)

    def own_step(n):
        gather.pump(order[n], False)
        if n + gather.ahead_own < gather.items:
            gather.issue(order[n + gather.ahead_own], False)
        if n > 0:
            gather.relay(order[n - 1], False)

    @pl.when(section == 1)
    def _():
        mask(tensor)
        gather.adapt_far().wait_recv()
        gather.adapt_core().start()
        for n in range(gather.ahead_own):
            gather.issue(order[n], False)
        for i in range(gather.through):
            gather.help(i)
            if i > 0:
                own_step(i - 1)
        for n in (4, 5, 6):
            own_step(n)
        for i in range(gather.through):
            gather.to_beyond(i).wait_send()
        gather.to_core(1).wait_recv()
        gather.landed(0)

    for i in (0, 4):
        gather.to_core(i).wait_recv()
    gather.adapt_core().wait_recv()
    gather.landed(5, 6, 7)

    def ready(part):
        @pl.when(section == 1)
        def _():
            hop(0, part.start // 256, w.hop_v.at[part], w.recv_v.at[part]).wait_recv()
            w.h_v[part] = w.recv_v[part]

    project(w.h_v, adapt_down, w, ready)

    def attend_group(g, carry):
        def give(part, head, value, inverse):
            if head is None:
                w.ctx_v[g, part] = value
                w.inv_v[g, part] = inverse
            else:
                w.p_v[g * (w.q_v.shape[2] // HEAD_DIM) + head, part] = value

        attend(w.q_v.at[g], w.k_v[g], w.v_v[g], w.bias, give)
        @pl.when(jnp.logical_and(section == 1, g == 0))
        def _():
            own_step(7)


        return carry

    lax.fori_loop(0, groups, attend_group, 0)
    attention_out(w.h_v, w.ctx_v, gains, biases, w, True)

    @pl.when(section == 1)
    def _():
        for i in (2, 3):
            gather.to_core(i).wait_recv()
        gather.landed(1, 2)

    def rest_of_down(slot):
        @pl.when(jnp.logical_and(section == 1, slot == 3))
        def _():
            gather.relay(order[7], False)

    feedforward_up(w, True, rest_of_down)

    @pl.when(section == 1)
    def _():
        gather.landed(3, 4)

    def block(out, index, part):
        return out.at[pl.ds(index * rows + part.start, part.size)]

    def rows_to(n, way, i, src, out, part, device):
        sems = w.row_send.at[n, way, i], w.row_recv.at[n, way, i]
        return remote(src.at[part], block(out, tensor, part), *sems, device)

    def rows_far(n, i, src, out, part):
        return rows_to(n, 0, i, src, out, part, far)

    def rows_core(n, i, src, out, part):
        return rows_to(n, 1, i, src, out, part, core)

    def rows_mine(n, i, src, out, part):
        return pltpu.make_async_copy(src.at[part], block(out, tensor, part), w.local.at[7 + 4 * n + i])

    def rows_relay(n, i, out, part):
        landed = block(out, turned, part)
        return remote(landed, landed, w.row_send.at[n, 2, i], w.row_recv.at[n, 2, i], core)

    def spread(n, i, src, out, part):
        for make in (rows_far, rows_core, rows_mine):
            make(n, i, src, out, part).start()

    def relay_rows(n, i, src, out, part):
        rows_far(n, i, src, out, part).wait_recv()
        rows_relay(n, i, out, part).start()

    def gathered(n, i, src, out, part):
        rows_core(n, i, src, out, part).wait()
        rows_relay(n, i, out, part).wait()
        rows_mine(n, i, src, out, part).wait()

    ends = (pl.ds(0, 128), pl.ds(128, 128), pl.ds(256, rows - 256))

    def through_corner(src):
        sems = w.row_send.at[1, 1, 3], w.row_recv.at[1, 1, 3]
        return remote(src.at[ends[0]], w.back_v.at[ends[0]], *sems, corner)

    def through_beyond():
        sems = w.row_send.at[1, 0, 3], w.row_recv.at[1, 0, 3]
        return remote(w.back_v.at[ends[0]], block(in_grads, turned, ends[0]), *sems, beyond)

    for i, part in enumerate(pieces):
        total = w.acc[part]
        for slot in range(w.ff_v.shape[1]):
            total = total + nn(w.act_v[slot, part], w.ff_v[1, slot])
        normed, scaled = normalize(total)
        w.n2_v[part] = normed
        w.s2_v[part] = scaled
        w.layer_v[part] = (normed * gains[1:2] + biases[1:2]).astype(BF16)
        spread(0, i, w.layer_v, layer_outs, part)

    cot_copy.wait()
    rank = adapt_down.shape[0] // 2

    def incoming(again, part):
        @pl.when(jnp.logical_and(again == 1, section == 0))
        def _():
            hop(1, part.start // 256, w.dh_v.at[part], w.back_v.at[part]).wait_recv()
            w.cot_v[part] = w.back_v[part]

        return w.cot_v[part].astype(F32)

    def summed(n, src, dst, device):
        return remote(src, dst, w.sum_send.at[n], w.sum_recv.at[n], device)

    def over_tensor(landing):
        copies = []
        for i, device in enumerate(sides):
            slot = indices[i] if landing else tensor
            for src, dst in (
                (w.grad_down, w.from_down.at[slot]),
                (w.grad_up.at[i + 1], w.from_up.at[i]),
            ):
                copies.append(summed(len(copies), src, dst, device))
        return copies

    def adapter_gradients(again):
        @pl.when(again == 1)
        def _():
            dmid_t = nt(identity(2 * rank), w.dmid_v[...]).astype(BF16)
            grad_down = nn(dmid_t, w.h_v[...])
            for j in range(2):
                w.grad_down[j] = grad_down[j * rank : (j + 1) * rank]
            up_q, up_v = (
                jnp.concatenate([2.0 * nn(w.mid_t[...], ref[g]) for g in range(groups)], 1)
                for ref in (w.dq_v, w.dv_v)
            )
            for i in range(len(sides) + 1):
                cols = slice(i * piece, (i + 1) * piece)
                w.grad_up[i, 0] = up_q[:rank, cols]
                w.grad_up[i, 1] = up_v[rank:, cols]
            w.from_down[tensor] = w.grad_down[...]
            for copy in over_tensor(False):
                copy.start()

    def hand_over(again, part, value):
        here = [n for n, end in enumerate(ends) if 0 <= end.start - part.start < part.size]

        @pl.when(jnp.logical_and(again == 0, section == 1))
        def _():
            w.dh_v[part] = value
            hop(1, part.start // 256, w.dh_v.at[part], w.back_v.at[part]).start()
            for n in here:
                spread(1, n, w.dh_v, in_grads, ends[n])

        @pl.when(jnp.logical_and(again == 1, section == 0))
        def _():
            w.dh_v[part] = value
            for n in here:
                if n:
                    rows_far(1, n, w.dh_v, in_grads, ends[n]).start()
                else:
                    through_corner(w.dh_v).start()
                rows_core(1, n, w.dh_v, in_grads, ends[n]).start()
                rows_mine(1, n, w.dh_v, in_grads, ends[n]).start()

    def back(again, carry):
        backward(
            w,
            gains,
            adapt_down,
            partial(incoming, again),
            partial(hand_over, again),
            partial(adapter_gradients, again),
        )

        @pl.when(again == 0)
        def _():
            for i, part in enumerate(pieces):
                relay_rows(0, i, w.layer_v, layer_outs, part)

        return carry

    lax.fori_loop(0, 2, back, 0)

    @pl.when(section == 1)
    def _():
        for n, end in enumerate(ends):
            relay_rows(1, n, w.dh_v, in_grads, end)
        through_corner(w.dh_v).wait_recv()
        through_beyond().start()

    tensor_copies = over_tensor(True)
    for copy in tensor_copies:
        copy.wait()
    w.plane_down[plane] = w.from_down[0] + w.from_down[1] + w.from_down[2] + w.from_down[3]
    w.plane_up[plane] = w.grad_up[0] + w.from_up[0] + w.from_up[1] + w.from_up[2]
    base = len(tensor_copies)
    totals = (w.plane_down, w.plane_up)
    for m, device in enumerate(ring):
        for k, ref in enumerate(totals):
            summed(base + 2 * m + k, ref.at[plane], ref.at[plane], device).start()

    @pl.when(section == 0)
    def _():
        relay_rows(1, 1, w.dh_v, in_grads, ends[1])

    for m, device in enumerate(ring):
        source = lax.rem(plane + planes - m - 1, planes)
        for k, ref in enumerate(totals):
            summed(base + 2 * m + k, ref.at[source], ref.at[source], device).wait_recv()
    for m, device in enumerate(ring):
        for k, ref in enumerate(totals):
            summed(base + 2 * m + k, ref.at[plane], ref.at[plane], device).wait_send()
    down_total, up_total = w.plane_down[0], w.plane_up[0]
    for m in range(1, planes):
        down_total = down_total + w.plane_down[m]
        up_total = up_total + w.plane_up[m]
    up_out[...] = up_total
    down_out[...] = down_total

    @pl.when(section == 0)
    def _():
        through_beyond().wait_recv()
        rows_relay(1, 0, in_grads, ends[0]).start()
        relay_rows(1, 2, w.dh_v, in_grads, ends[2])
        through_corner(w.dh_v).wait_send()
        for n in (1, 2):
            rows_far(1, n, w.dh_v, in_grads, ends[n]).wait_send()
        for i, part in enumerate(pieces):
            hop(0, i, w.hop_v.at[part], w.recv_v.at[part]).wait_send()
        for k in (1, 2, 3):
            context_to(k).wait_send()
        gather.sent(0)

    @pl.when(section == 1)
    def _():
        through_beyond().wait_send()
        for n, end in enumerate(ends):
            rows_far(1, n, w.dh_v, in_grads, end).wait_send()
        for i, part in enumerate(pieces):
            hop(1, i, w.dh_v.at[part], w.back_v.at[part]).wait_send()
        gather.sent(1)

    for i, part in enumerate(pieces):
        rows_far(0, i, w.layer_v, layer_outs, part).wait_send()
        gathered(0, i, w.layer_v, layer_outs, part)
    for n, end in enumerate(ends):
        gathered(1, n, w.dh_v, in_grads, end)


def local(
    embedded,
    segment,
    query_key_value_weight,
    attention_output_weight,
    feedforward_up_weight,
    feedforward_down_weight,
    adapter_down_weight,
    adapter_up_weight,
    layer_norm_gain,
    layer_norm_bias,
    cotangent,
):
    slots, packs, planes = lax.axis_size("tensor"), segment.shape[0], lax.axis_size("dp")
    assert slots == 4 and packs == slots and planes % 2 == 0
    rows, width = segment.shape[1], embedded.shape[1]
    piece = query_key_value_weight.shape[3]
    wide = feedforward_up_weight.shape[2]
    assert wide == width
    rank = adapter_down_weight.shape[3]
    span = 256
    groups = width // span
    heads = width // HEAD_DIM

    def arr(shape, dtype):
        return jax.ShapeDtypeStruct(shape, dtype)

    low_rows = pltpu.VMEM((rows, width), BF16)
    full_rows = pltpu.VMEM((rows, width), F32)
    of_heads = pltpu.VMEM((groups, rows, span), BF16)
    of_hidden = pltpu.VMEM((slots, rows, wide), BF16)
    down_part = (2, rank, width)
    up_part = (2, rank, piece)
    sums = 2 * (slots - 1) + 2 * (planes - 1)
    scratch = dict(
        qkv_v=pltpu.VMEM((3, width, width), BF16),
        out_v=pltpu.VMEM((width, width), BF16),
        ff_v=pltpu.VMEM((2, slots, width, wide), BF16),
        adapt_v=pltpu.VMEM((width, 2 * rank), BF16),
        adapt_own=pltpu.VMEM((piece, 2 * rank), BF16),
        q_own=pltpu.VMEM((rows, piece), BF16),
        ctx_out=pltpu.VMEM((slots, rows, piece), BF16),
        ctx_in=pltpu.VMEM((slots, rows, piece), BF16),
        inv_v=pltpu.VMEM((groups, rows, span), F32),
        p_v=pltpu.VMEM((heads, rows, rows), BF16),
        s1_v=pltpu.VMEM((rows, 1), F32),
        s2_v=pltpu.VMEM((rows, 1), F32),
        bias=pltpu.VMEM((rows, rows), F32),
        mid_t=pltpu.VMEM((2 * rank, rows), BF16),
        dmid_v=pltpu.VMEM((rows, 2 * rank), BF16),
        grad_down=pltpu.VMEM(down_part, F32),
        grad_up=pltpu.VMEM((slots, *up_part), F32),
        from_down=pltpu.VMEM((slots, *down_part), F32),
        from_up=pltpu.VMEM((slots - 1, *up_part), F32),
        plane_down=pltpu.VMEM((planes, *down_part), F32),
        plane_up=pltpu.VMEM((planes, *up_part), F32),
        local=pltpu.SemaphoreType.DMA((15,)),
        packs=pltpu.SemaphoreType.DMA((packs,)),
        send=pltpu.SemaphoreType.DMA((11, Gather.items)),
        recv=pltpu.SemaphoreType.DMA((11, Gather.items)),
        ctx_send=pltpu.SemaphoreType.DMA((slots,)),
        ctx_recv=pltpu.SemaphoreType.DMA((slots,)),
        hop_send=pltpu.SemaphoreType.DMA((2, rows // 128)),
        hop_recv=pltpu.SemaphoreType.DMA((2, rows // 128)),
        row_send=pltpu.SemaphoreType.DMA((2, 3, rows // 128)),
        row_recv=pltpu.SemaphoreType.DMA((2, 3, rows // 128)),
        sum_send=pltpu.SemaphoreType.DMA((sums,)),
        sum_recv=pltpu.SemaphoreType.DMA((sums,)),
    )
    scratch |= dict.fromkeys(("h_v", "recv_v", "back_v", "cot_v", "low_v"), low_rows)
    scratch |= dict.fromkeys(("hop_v", "layer_v", "dh_v"), low_rows)
    scratch |= dict.fromkeys(("acc", "n1_v", "n2_v"), full_rows)
    scratch |= dict.fromkeys(("q_v", "k_v", "v_v", "ctx_v"), of_heads)
    scratch |= dict.fromkeys(("dq_v", "dk_v", "dv_v", "dctx_v"), of_heads)
    scratch |= dict.fromkeys(("act_v", "slope_v"), of_hidden)
    layer_outs, in_grads, grad_a, grad_b = pl.pallas_call(
        partial(whole_kernel, planes, tuple(scratch)),
        name="encoder_layers",
        out_shape=[
            pltpu.VMEM((packs * rows, width), BF16),
            pltpu.VMEM((packs * rows, width), BF16),
            arr(down_part, F32),
            arr(up_part, F32),
        ],
        in_specs=[ANY] + [VMEM] * 5 + [ANY] * 5,
        out_specs=[VMEM] * 4,
        scratch_shapes=list(scratch.values()),
        compiler_params=pltpu.CompilerParams(
            vmem_limit_bytes=VMEM_LIMIT, collective_id=0, has_side_effects=True
        ),
        cost_estimate=pl.CostEstimate(
            flops=7 * 10**10, bytes_accessed=3 * 10**7, transcendentals=0
        ),
    )(
        embedded,
        segment,
        layer_norm_gain[0],
        layer_norm_bias[0],
        jnp.swapaxes(adapter_down_weight[0], 1, 2).reshape(2 * rank, width),
        adapter_up_weight[0].reshape(2 * rank, piece),
        jnp.swapaxes(query_key_value_weight[0], 1, 2),
        attention_output_weight[0],
        feedforward_up_weight[0],
        feedforward_down_weight[0],
        cotangent,
    )
    grad_a = jnp.swapaxes(grad_a, 1, 2)
    return (layer_outs[None], in_grads[None], grad_a[None], grad_b[None])


def solution(mesh):
    in_specs = (
        P("dp", None),
        P("dp", None),
        P("section", None, None, "tensor"),
        P("section", "tensor", None),
        P("section", None, "tensor"),
        P("section", "tensor", None),
        P("section", None, None, None),
        P("section", None, None, "tensor"),
        P("section", None, None),
        P("section", None, None),
        P("dp", None),
    )
    out_specs = (
        P("section", "dp", None),
        P("section", "dp", None),
        P("section", None, None, None),
        P("section", None, None, "tensor"),
    )
    return jax.shard_map(local, mesh=mesh, in_specs=in_specs, out_specs=out_specs, check_vma=False)
```

```python
from functools import partial

import jax
import jax.numpy as jnp
from jax import lax
from jax.experimental import pallas as pl
from jax.experimental.pallas import tpu as pltpu
from jax.sharding import PartitionSpec as P

HEAD_DIM = 64
EPS = 1e-05
VMEM_LIMIT = 115 * 2**19
F32 = jnp.float32
BF16 = jnp.bfloat16
ANY = pl.BlockSpec(memory_space=pl.ANY)
VMEM = pl.BlockSpec(memory_space=pltpu.VMEM)
MESH = pl.DeviceIdType.MESH
SMEM = pl.BlockSpec(memory_space=pltpu.SMEM)


def nn(a, b):
    return jnp.dot(a, b, preferred_element_type=F32)


def nt(a, b):
    return lax.dot_general(a, b, (((1,), (1,)), ((), ())), preferred_element_type=F32)


def lane_mask(shape, low, high):
    lanes = lax.broadcasted_iota(jnp.int32, shape, len(shape) - 1)
    return (lanes >= low) & (lanes < high)


def normalize(total):
    average = jnp.mean(total, -1, keepdims=True)
    centred = total - average
    spread = jnp.mean(centred * centred, -1, keepdims=True)
    scaled = lax.rsqrt(spread + EPS)
    return centred * scaled, scaled


def normalize_back(normed, scaled, gains, incoming):
    weighted = incoming * gains
    return scaled * (
        weighted
        - jnp.mean(weighted, -1, keepdims=True)
        - normed * jnp.mean(weighted * normed, -1, keepdims=True)
    )


def neighbours():
    section, plane, tensor = (lax.axis_index(n) for n in ("section", "dp", "tensor"))
    turned = lax.rem(tensor + 2, 4)
    other = tensor + 1 - 2 * lax.rem(tensor, 2)
    paired = plane + 1 - 2 * lax.rem(plane, 2)
    return (
        (section, plane, other),
        (section, plane, turned),
        (section, paired, tensor),
        (1 - section, plane, tensor),
        (1 - section, plane, turned),
    )


def meet(devices):
    barrier = pltpu.get_barrier_semaphore()
    for device in devices:
        pl.semaphore_signal(barrier, inc=1, device_id=device, device_id_type=MESH)
    pl.semaphore_wait(barrier, len(devices))


def remote(src, dst, send, recv, device):
    return pltpu.make_async_remote_copy(
        src_ref=src,
        dst_ref=dst,
        send_sem=send,
        recv_sem=recv,
        device_id=device,
        device_id_type=MESH,
    )


def identity(n):
    rows = lax.broadcasted_iota(jnp.int32, (n, n), 0)
    return (rows == lax.broadcasted_iota(jnp.int32, (n, n), 1)).astype(BF16)


def blocks_of(rows, size):
    return [pl.ds(r, size) for r in range(0, rows, size)]


class Gather:
    items, ahead, ahead_own = 8, 2, 8
    through = 5

    def __init__(self, own, gathered, resting, partners, sems):
        self.qkv, self.outw, self.up, self.down, self.adapt = own
        self.qkv_v, self.out_v, self.ff_v, self.adapt_v = gathered
        self.resting_v = resting
        self.core, self.far, self.plane, self.beyond, self.corner = partners
        self.send, self.recv, self.local = sems
        self.parity = lax.rem(lax.axis_index("dp"), 2)
        self.n_qkv, self.n_out = self.qkv.shape[1], self.outw.shape[0]
        self.n_ff, self.n_adapt = self.up.shape[0], self.adapt.shape[0]

    def block(self, i, slot, third):
        if i == 0:
            size = self.n_out // 3
            return self.out_v.at[pl.ds(slot * self.n_out + third * size, size)]
        if i >= 5:
            size = self.n_qkv // 3
            return self.qkv_v.at[i - 5, pl.ds(slot * self.n_qkv + third * size, size)]
        which, j = divmod(i - 1, 2)
        rows = self.n_ff // 3
        size = rows // 2
        return self.ff_v.at[which, slot, pl.ds(third * rows + j * size, size)]

    def resting(self, i):
        size = self.n_out // 3 if i == 0 else self.n_ff // 6
        return self.resting_v.at[i // 4, pl.ds(i % 4 * (self.n_ff // 6), size)]

    def whole(self, i, slot):
        if i == 0:
            return self.qkv_v.at[:, pl.ds(slot * self.n_qkv, self.n_qkv)]
        if i == 1:
            return self.out_v.at[pl.ds(slot * self.n_out, self.n_out)]
        if i == 4:
            return self.adapt_v.at[pl.ds(slot * self.n_adapt, self.n_adapt)]
        return self.ff_v.at[i - 2, slot]

    def link(self, kind, i, src, dst, device):
        return remote(src, dst, self.send.at[kind, i], self.recv.at[kind, i], device)

    def over_far(self, i):
        p = self.parity
        return self.link(0, i, self.block(i, 0, p), self.block(i, 2, p), self.far)

    def to_plane(self, i, third):
        here = self.block(i, 2, third)
        return self.link(1, i, here, here, self.plane)

    def pass_on(self, i, kind):
        third = (self.parity, 1 - self.parity, 2)[kind]
        return self.link(2 + kind, i, self.block(i, 2, third), self.block(i, 3, third), self.core)

    def to_corner(self, i):
        return self.link(7, i, self.block(i, 0, 2), self.resting(i), self.corner)

    def to_beyond(self, i):
        return self.link(8, i, self.resting(i), self.block(i, 2, 2), self.beyond)

    def last_far(self, i):
        return self.link(9, i, self.block(i, 0, 2), self.block(i, 2, 2), self.far)

    def last_plane(self, i):
        here = self.block(i, 2, 2)
        return self.link(10, i, here, here, self.plane)

    def load(self, i):
        own = (self.qkv, self.outw, self.up, self.down, self.adapt)[i]
        return pltpu.make_async_copy(own, self.whole(i, 0), self.local.at[i])

    def to_core(self, i):
        return self.link(5, i, self.whole(i, 0), self.whole(i, 1), self.core)

    def adapt_far(self):
        return self.link(6, 0, self.whole(4, 0), self.whole(4, 2), self.far)

    def adapt_core(self):
        return self.link(6, 1, self.whole(4, 2), self.whole(4, 3), self.core)

    def when_last(self, i, mine):
        here = i % 2
        return pl.when(self.parity == (here if mine else 1 - here))

    def issue(self, i, through):
        self.over_far(i).start()
        if through:
            self.to_corner(i).start()
        else:

            @self.when_last(i, True)
            def _():
                self.last_far(i).start()

    def pump(self, i, through):
        self.over_far(i).wait_recv()
        self.to_plane(i, self.parity).start()
        self.pass_on(i, 0).start()
        if not through:

            @self.when_last(i, True)
            def _():
                self.last_far(i).wait_recv()
                self.last_plane(i).start()
                self.pass_on(i, 2).start()

    def relay(self, i, through):
        self.to_plane(i, 1 - self.parity).wait_recv()
        self.pass_on(i, 1).start()
        if not through:

            @self.when_last(i, False)
            def _():
                self.last_plane(i).wait_recv()
                self.pass_on(i, 2).start()

    def relay_last(self, i):
        self.to_beyond(i).wait_recv()
        self.pass_on(i, 2).start()

    def help(self, i):
        self.to_corner(i).wait_recv()
        self.to_beyond(i).start()

    def landed(self, *items):
        for i in items:
            for kind in range(3):
                self.pass_on(i, kind).wait_recv()

    def sent(self, section):
        for i in range(self.items):
            self.over_far(i).wait_send()
            self.to_plane(i, self.parity).wait_send()
            for kind in range(3):
                self.pass_on(i, kind).wait_send()
            if section == 0 and i < self.through:
                self.to_corner(i).wait_send()
            else:

                @self.when_last(i, True)
                def _():
                    self.last_far(i).wait_send()
                    self.last_plane(i).wait_send()

        for i in range(5):
            self.to_core(i).wait_send()
        self.adapt_far().wait_send()
        self.adapt_core().wait_send()


def middle(h, adapt_down):
    rank = adapt_down.shape[0] // 2
    mid = nt(h, adapt_down[...]).astype(BF16)
    is_query = lane_mask(mid.shape, 0, rank)
    double = mid * jnp.asarray(2.0, BF16)
    zero = jnp.zeros((), BF16)
    return mid, jnp.where(is_query, double, zero), jnp.where(is_query, zero, double)


def project(h_v, adapt_down, w, ready):
    for part in blocks_of(h_v.shape[0], 256):
        ready(part)
        h = h_v[part]
        mid, mid_q, mid_v = middle(h, adapt_down)
        w.mid_t[:, part] = nt(identity(mid.shape[1]), mid).astype(BF16)
        for s, (ref, low) in enumerate(((w.q_v, mid_q), (w.k_v, None), (w.v_v, mid_v))):
            value = nt(h, w.qkv_v[s])
            if low is not None:
                value = value + nt(low, w.adapt_v[...])
            value = value.astype(BF16)
            span = ref.shape[2]
            for g in range(ref.shape[0]):
                ref[g, part] = value[:, g * span : (g + 1) * span]


def attend(q_v, k, v, bias, give, small=False):
    rows, span = k.shape
    chunk = 256
    zero = jnp.zeros((), BF16)
    def some(part):
        q_c = q_v[part] * jnp.asarray(HEAD_DIM**-0.5, BF16)
        ctx = jnp.zeros((chunk, span), F32)
        inverse = jnp.zeros((chunk, span), F32)
        weights = []
        for e in range(span // HEAD_DIM):
            low = e * HEAD_DIM
            of_head = lane_mask(q_c.shape, low, low + HEAD_DIM)
            v_e = jnp.where(lane_mask(v.shape, low, low + HEAD_DIM), v, zero)
            s = nt(jnp.where(of_head, q_c, zero), k) + bias[part]
            weight = jnp.exp(s - jnp.max(s, -1, keepdims=True))
            scale = 1.0 / jnp.sum(weight, -1, keepdims=True)
            weight = weight.astype(BF16)
            ctx = ctx + nn(weight, v_e) * scale
            inverse = jnp.where(of_head, scale, inverse)
            give(part, e, weight, None)
        give(part, None, ctx.astype(BF16), inverse)

    if small:

        def step(i, carry):
            some(pl.ds(pl.multiple_of(i * chunk, chunk), chunk))
            return carry

        lax.fori_loop(0, rows // chunk, step, 0)
    else:
        for part in blocks_of(rows, chunk):
            some(part)


def attention_out(h_v, context, gains, biases, w, keep):
    groups, rows, span = context.shape
    for part in blocks_of(rows, 256):
        total = h_v[part].astype(F32)
        for g in range(groups):
            total = total + nn(context[g, part], w.out_v[g * span : (g + 1) * span])
        normed, scaled = normalize(total)
        if keep:
            w.n1_v[part] = normed
            w.s1_v[part] = scaled
        first = normed * gains[0:1] + biases[0:1]
        w.acc[part] = first
        w.low_v[part] = first.astype(BF16)


def feedforward_up(w, keep, ready):
    rows = w.low_v.shape[0]

    def one(slot, part):
        pre = nn(w.low_v[part], w.ff_v[0, slot])
        cdf = 0.5 + 0.5 * lax.erf(pre * (0.5**0.5))
        w.act_v[slot, part] = (pre * cdf).astype(BF16)
        if keep:
            density = jnp.exp(pre * pre * -0.5) * 0.3989422804014327
            w.slope_v[slot, part] = (cdf + pre * density).astype(BF16)

    def small_step(slot, carry):
        ready(slot)

        def some(i, carry):
            one(slot, pl.ds(pl.multiple_of(i * 256, 256), 256))
            return carry

        return lax.fori_loop(0, rows // 256, some, carry)

    if keep:
        for slot in range(w.act_v.shape[0]):
            ready(jnp.int32(slot))
            for part in blocks_of(rows, 128):
                one(slot, part)
    else:
        lax.fori_loop(0, w.act_v.shape[0], small_step, 0)


def backward(w, gains, adapt_down, incoming, give, sums):
    rows = w.acc.shape[0]
    slots = w.ff_v.shape[1]
    groups, _, span = w.q_v.shape
    for part in blocks_of(rows, 256):
        back = normalize_back(w.n2_v[part], w.s2_v[part], gains[1:2], incoming(part))
        w.acc[part] = back
        w.low_v[part] = back.astype(BF16)

        def step(slot, carry):
            dact = nt(w.low_v[part], w.ff_v[1, slot])
            w.act_v[slot, part] = (dact * w.slope_v[slot, part].astype(F32)).astype(BF16)
            return carry

        for slot in range(slots):
            step(slot, 0)
        total = w.acc[part]
        for slot in range(slots):
            total = total + nt(w.act_v[slot, part], w.ff_v[0, slot])
        back = normalize_back(w.n1_v[part], w.s1_v[part], gains[0:1], total)
        w.acc[part] = back
        dctx = nt(back.astype(BF16), w.out_v[...])
        for g in range(groups):
            scaled = dctx[:, g * span : (g + 1) * span] * w.inv_v[g, part]
            w.dctx_v[g, part] = scaled.astype(BF16)
    heads = span // HEAD_DIM
    factor = HEAD_DIM**-0.5

    def group(g, carry):
        q, k, v = w.q_v[g], w.k_v[g], w.v_v[g]
        dctx, ctx = w.dctx_v[g], w.ctx_v[g].astype(F32)
        q_t, dctx_t = q.T, dctx.T
        zero = jnp.zeros((), BF16)
        dq = jnp.zeros((rows, span), F32)
        dk_t, dv_t = [], []
        for e in range(heads):
            low, high = e * HEAD_DIM, (e + 1) * HEAD_DIM
            of_head = lane_mask((rows, span), low, high)
            weight = w.p_v[g * heads + e]
            dctx_e = jnp.where(of_head, dctx, zero)
            delta = jnp.sum(dctx_e.astype(F32) * ctx, -1, keepdims=True)
            ds = (weight.astype(F32) * (nt(dctx_e, v) - delta)).astype(BF16)
            dq = dq + nn(ds, jnp.where(of_head, k, zero))
            dk_t.append(nn(q_t[low:high], ds))
            dv_t.append(nn(dctx_t[low:high], weight))
        w.dq_v[g] = (dq * factor).astype(BF16)
        w.dk_v[g] = (jnp.concatenate(dk_t, 0) * factor).astype(BF16).T
        w.dv_v[g] = jnp.concatenate(dv_t, 0).astype(BF16).T
        return carry

    for g in range(groups):
        group(g, 0)
    rank = adapt_down.shape[0] // 2
    for part in blocks_of(rows, 256):
        dmid_q = dmid_v = 0.0
        for g in range(groups):
            cols = slice(g * span, (g + 1) * span)
            dmid_q = dmid_q + nn(w.dq_v[g, part], w.adapt_v[cols])
            dmid_v = dmid_v + nn(w.dv_v[g, part], w.adapt_v[cols])
        dmid = 2.0 * jnp.where(lane_mask(dmid_q.shape, 0, rank), dmid_q, dmid_v)
        w.dmid_v[part] = dmid.astype(BF16)
    sums()
    for part in blocks_of(rows, 256):
        total = w.acc[part]
        for g in range(groups):
            cols = slice(g * span, (g + 1) * span)
            for s, ref in enumerate((w.dq_v, w.dk_v, w.dv_v)):
                total = total + nn(ref[g, part], w.qkv_v[s, cols])
        give(part, (total + nn(w.dmid_v[part], adapt_down[...])).astype(BF16))


class Refs:
    def __init__(self, names, refs):
        self.__dict__.update(zip(names, refs, strict=True))


def whole_kernel(planes, names, *refs):
    embedded, segment, gains, biases, adapt_down, adapt, qkv, outw, up, down, cotangent = refs[:11]
    layer_outs, in_grads, down_out, up_out = refs[11:15]
    w = Refs(names, refs[15:])
    section, plane, tensor = (lax.axis_index(n) for n in ("section", "dp", "tensor"))
    core, far, paired, beyond, corner = neighbours()
    turned = lax.rem(tensor + 2, 4)
    other = tensor + 1 - 2 * lax.rem(tensor, 2)
    across = lax.rem(other + 2, 4)
    indices = (other, turned, across)
    sides = tuple((section, plane, i) for i in indices)
    ring = [(section, lax.rem(plane + m, planes), tensor) for m in range(1, planes)]
    rows, width = w.h_v.shape
    groups = w.q_v.shape[0]

    own = pl.ds(tensor * rows, rows)
    gather = Gather(
        (qkv, outw, up, down, w.adapt_own),
        (w.qkv_v, w.out_v, w.ff_v, w.adapt_v),
        w.act_v,
        (core, far, paired, beyond, corner),
        (w.send, w.recv, w.local),
    )
    for i in (1, 0, 2, 3):
        gather.load(i).start()
    pack_copies = [
        pltpu.make_async_copy(embedded.at[pl.ds(i * rows, rows)], w.slope_v.at[i], w.packs.at[i])
        for i in range(len(indices) + 1)
    ]
    for copy in pack_copies:
        copy.start()
    h_copy = pltpu.make_async_copy(embedded.at[own], w.h_v, w.local.at[5])
    h_copy.start()
    cot_copy = pltpu.make_async_copy(cotangent.at[own], w.cot_v, w.local.at[6])
    cot_copy.start()
    adapt_t = nt(identity(adapt.shape[1]), adapt[...]).astype(BF16)
    w.adapt_own[...] = adapt_t
    w.adapt_v[: adapt.shape[1]] = adapt_t
    meet((*sides, *ring, beyond, corner))

    for i in (1, 2, 3, 0):
        gather.load(i).wait()
    gather.adapt_far().start()
    for i in (4, 1, 2, 3, 0):
        gather.to_core(i).start()
    for copy in pack_copies:
        copy.wait()
    h_copy.wait()
    square = (rows, rows)
    piece = adapt.shape[1]
    pieces = blocks_of(rows, 256)

    def mask(pack):
        diagonal = lax.broadcasted_iota(jnp.int32, square, 0) == lax.broadcasted_iota(
            jnp.int32, square, 1
        )
        ids = segment[pl.ds(pack, 1), :].astype(F32)
        column = jnp.sum(jnp.where(diagonal, ids, 0.0), -1, keepdims=True)
        w.bias[...] = jnp.where(column == ids, 0.0, -1e9)

    def index_of(k):
        high = lax.rem(tensor // 2 + k // 2, 2)
        return 2 * high + lax.rem(lax.rem(tensor, 2) + lax.rem(k, 2), 2)

    def context_to(k):
        device = (section, plane, index_of(k))
        return remote(w.ctx_out.at[k], w.ctx_in.at[k], w.ctx_send.at[k], w.ctx_recv.at[k], device)

    def attend_pack(step, carry):
        k = 3 - step
        pack = index_of(k)
        mask(pack)
        h = w.slope_v[pack]
        _, mid_q, mid_v = middle(h, adapt_down)
        w.q_own[...] = (nt(h, w.qkv_v[0, :piece]) + nt(mid_q, w.adapt_own[...])).astype(BF16)
        k_own = nt(h, w.qkv_v[1, :piece]).astype(BF16)
        v_own = (nt(h, w.qkv_v[2, :piece]) + nt(mid_v, w.adapt_own[...])).astype(BF16)

        def give(part, head, value, inverse):
            if head is None:
                w.ctx_out[k, part] = value

        attend(w.q_own, k_own, v_own, w.bias, give, True)

        @pl.when(step < 3)
        def _():
            context_to(k).start()

        for i in (1, 2, 3):

            @pl.when(step == i)
            def _():
                gather.pump(i - 1, True)
                ask(i - 1 + gather.ahead)
                if i > 1:
                    gather.relay(i - 2, True)
                if i > 2:
                    gather.relay_last(i - 3)

        return carry

    def hop(way, i, src, dst):
        return remote(src, dst, w.hop_send.at[way, i], w.hop_recv.at[way, i], beyond)

    def ask(i):
        if i < gather.items:
            gather.issue(i, i < gather.through)

    @pl.when(section == 0)
    def _():
        for i in range(gather.ahead):
            ask(i)
        lax.fori_loop(0, 4, attend_pack, 0)
        w.ctx_in[0] = w.ctx_out[0]
        gather.adapt_far().wait_recv()
        gather.adapt_core().start()
        for k in (1, 2, 3):
            context_to(k).wait_recv()
        gather.to_core(1).wait_recv()
        gather.landed(0)
        attention_out(w.h_v, w.ctx_in, gains, biases, w, False)
        gather.pump(3, True)
        ask(3 + gather.ahead)
        gather.relay(2, True)
        gather.relay_last(1)
        for i in (2, 3):
            gather.to_core(i).wait_recv()

        def rest_of_up(slot):
            @pl.when(slot == 2)
            def _():
                gather.relay_last(2)
                gather.landed(1, 2)

            @pl.when(slot == 3)
            def _():
                gather.pump(4, True)
                ask(4 + gather.ahead)
                gather.relay(3, True)

        feedforward_up(w, False, rest_of_up)
        gather.relay_last(3)
        for part in blocks_of(rows, 256):
            w.acc[part] += nn(w.act_v[0, part], w.ff_v[1, 0]) + nn(w.act_v[1, part], w.ff_v[1, 1])
        gather.relay(4, True)
        gather.relay_last(4)
        gather.landed(3, 4)
        for i, part in enumerate(pieces):
            total = w.acc[part]
            for slot in (2, 3):
                total = total + nn(w.act_v[slot, part], w.ff_v[1, slot])
            w.hop_v[part] = (normalize(total)[0] * gains[1:2] + biases[1:2]).astype(BF16)
            hop(0, i, w.hop_v.at[part], w.recv_v.at[part]).start()
        for i in range(5, gather.items):
            gather.pump(i, False)
            ask(i + gather.ahead)
            if i > 5:
                gather.relay(i - 1, False)
        gather.relay(gather.items - 1, False)

    order = (5, 6, 7, 0, 1, 2, 3, 4)

    def own_step(n):
        gather.pump(order[n], False)
        if n + gather.ahead_own < gather.items:
            gather.issue(order[n + gather.ahead_own], False)
        if n > 0:
            gather.relay(order[n - 1], False)

    @pl.when(section == 1)
    def _():
        mask(tensor)
        gather.adapt_far().wait_recv()
        gather.adapt_core().start()
        for n in range(gather.ahead_own):
            gather.issue(order[n], False)
        for i in range(gather.through):
            gather.help(i)
            if i > 0:
                own_step(i - 1)
        for n in (4, 5, 6):
            own_step(n)
        for i in range(gather.through):
            gather.to_beyond(i).wait_send()
        gather.to_core(1).wait_recv()
        gather.landed(0)

    for i in (0, 4):
        gather.to_core(i).wait_recv()
    gather.adapt_core().wait_recv()
    gather.landed(5, 6, 7)

    def ready(part):
        @pl.when(section == 1)
        def _():
            hop(0, part.start // 256, w.hop_v.at[part], w.recv_v.at[part]).wait_recv()
            w.h_v[part] = w.recv_v[part]

    project(w.h_v, adapt_down, w, ready)

    def attend_group(g, carry):
        def give(part, head, value, inverse):
            if head is None:
                w.ctx_v[g, part] = value
                w.inv_v[g, part] = inverse
            else:
                w.p_v[g * (w.q_v.shape[2] // HEAD_DIM) + head, part] = value

        attend(w.q_v.at[g], w.k_v[g], w.v_v[g], w.bias, give)
        @pl.when(jnp.logical_and(section == 1, g == 0))
        def _():
            own_step(7)


        return carry

    lax.fori_loop(0, groups, attend_group, 0)
    attention_out(w.h_v, w.ctx_v, gains, biases, w, True)

    @pl.when(section == 1)
    def _():
        for i in (2, 3):
            gather.to_core(i).wait_recv()
        gather.landed(1, 2)

    def rest_of_down(slot):
        @pl.when(jnp.logical_and(section == 1, slot == 3))
        def _():
            gather.relay(order[7], False)

    feedforward_up(w, True, rest_of_down)

    @pl.when(section == 1)
    def _():
        gather.landed(3, 4)

    def block(out, index, part):
        return out.at[pl.ds(index * rows + part.start, part.size)]

    def rows_to(n, way, i, src, out, part, device):
        sems = w.row_send.at[n, way, i], w.row_recv.at[n, way, i]
        return remote(src.at[part], block(out, tensor, part), *sems, device)

    def rows_far(n, i, src, out, part):
        return rows_to(n, 0, i, src, out, part, far)

    def rows_core(n, i, src, out, part):
        return rows_to(n, 1, i, src, out, part, core)

    def rows_mine(n, i, src, out, part):
        return pltpu.make_async_copy(src.at[part], block(out, tensor, part), w.local.at[7 + 4 * n + i])

    def rows_relay(n, i, out, part):
        landed = block(out, turned, part)
        return remote(landed, landed, w.row_send.at[n, 2, i], w.row_recv.at[n, 2, i], core)

    def spread(n, i, src, out, part):
        for make in (rows_far, rows_core, rows_mine):
            make(n, i, src, out, part).start()

    def relay_rows(n, i, src, out, part):
        rows_far(n, i, src, out, part).wait_recv()
        rows_relay(n, i, out, part).start()

    def gathered(n, i, src, out, part):
        rows_core(n, i, src, out, part).wait()
        rows_relay(n, i, out, part).wait()
        rows_mine(n, i, src, out, part).wait()

    ends = (pl.ds(0, 128), pl.ds(128, 128), pl.ds(256, rows - 256))

    def through_corner(src):
        sems = w.row_send.at[1, 1, 3], w.row_recv.at[1, 1, 3]
        return remote(src.at[ends[0]], w.back_v.at[ends[0]], *sems, corner)

    def through_beyond():
        sems = w.row_send.at[1, 0, 3], w.row_recv.at[1, 0, 3]
        return remote(w.back_v.at[ends[0]], block(in_grads, turned, ends[0]), *sems, beyond)

    for i, part in enumerate(pieces):
        total = w.acc[part]
        for slot in range(w.ff_v.shape[1]):
            total = total + nn(w.act_v[slot, part], w.ff_v[1, slot])
        normed, scaled = normalize(total)
        w.n2_v[part] = normed
        w.s2_v[part] = scaled
        w.layer_v[part] = (normed * gains[1:2] + biases[1:2]).astype(BF16)
        spread(0, i, w.layer_v, layer_outs, part)

    cot_copy.wait()
    rank = adapt_down.shape[0] // 2

    def incoming(again, part):
        @pl.when(jnp.logical_and(again == 1, section == 0))
        def _():
            hop(1, part.start // 256, w.dh_v.at[part], w.back_v.at[part]).wait_recv()
            w.cot_v[part] = w.back_v[part]

        return w.cot_v[part].astype(F32)

    def summed(n, src, dst, device):
        return remote(src, dst, w.sum_send.at[n], w.sum_recv.at[n], device)

    def over_tensor(landing):
        copies = []
        for i, device in enumerate(sides):
            slot = indices[i] if landing else tensor
            for src, dst in (
                (w.grad_down, w.from_down.at[slot]),
                (w.grad_up.at[i + 1], w.from_up.at[i]),
            ):
                copies.append(summed(len(copies), src, dst, device))
        return copies

    def adapter_gradients(again):
        @pl.when(again == 1)
        def _():
            dmid_t = nt(identity(2 * rank), w.dmid_v[...]).astype(BF16)
            grad_down = nn(dmid_t, w.h_v[...])
            for j in range(2):
                w.grad_down[j] = grad_down[j * rank : (j + 1) * rank]
            up_q, up_v = (
                jnp.concatenate([2.0 * nn(w.mid_t[...], ref[g]) for g in range(groups)], 1)
                for ref in (w.dq_v, w.dv_v)
            )
            for i in range(len(sides) + 1):
                cols = slice(i * piece, (i + 1) * piece)
                w.grad_up[i, 0] = up_q[:rank, cols]
                w.grad_up[i, 1] = up_v[rank:, cols]
            w.from_down[tensor] = w.grad_down[...]
            for copy in over_tensor(False):
                copy.start()

    def hand_over(again, part, value):
        here = [n for n, end in enumerate(ends) if 0 <= end.start - part.start < part.size]

        @pl.when(jnp.logical_and(again == 0, section == 1))
        def _():
            w.dh_v[part] = value
            hop(1, part.start // 256, w.dh_v.at[part], w.back_v.at[part]).start()
            for n in here:
                spread(1, n, w.dh_v, in_grads, ends[n])

        @pl.when(jnp.logical_and(again == 1, section == 0))
        def _():
            w.dh_v[part] = value
            for n in here:
                if n:
                    rows_far(1, n, w.dh_v, in_grads, ends[n]).start()
                else:
                    through_corner(w.dh_v).start()
                rows_core(1, n, w.dh_v, in_grads, ends[n]).start()
                rows_mine(1, n, w.dh_v, in_grads, ends[n]).start()

    def back(again, carry):
        backward(
            w,
            gains,
            adapt_down,
            partial(incoming, again),
            partial(hand_over, again),
            partial(adapter_gradients, again),
        )

        @pl.when(again == 0)
        def _():
            for i, part in enumerate(pieces):
                relay_rows(0, i, w.layer_v, layer_outs, part)

        return carry

    lax.fori_loop(0, 2, back, 0)

    @pl.when(section == 1)
    def _():
        for n, end in enumerate(ends):
            relay_rows(1, n, w.dh_v, in_grads, end)
        through_corner(w.dh_v).wait_recv()
        through_beyond().start()

    tensor_copies = over_tensor(True)
    for copy in tensor_copies:
        copy.wait()
    w.plane_down[plane] = w.from_down[0] + w.from_down[1] + w.from_down[2] + w.from_down[3]
    w.plane_up[plane] = w.grad_up[0] + w.from_up[0] + w.from_up[1] + w.from_up[2]
    base = len(tensor_copies)
    totals = (w.plane_down, w.plane_up)
    for m, device in enumerate(ring):
        for k, ref in enumerate(totals):
            summed(base + 2 * m + k, ref.at[plane], ref.at[plane], device).start()

    @pl.when(section == 0)
    def _():
        relay_rows(1, 1, w.dh_v, in_grads, ends[1])

    for m, device in enumerate(ring):
        source = lax.rem(plane + planes - m - 1, planes)
        for k, ref in enumerate(totals):
            summed(base + 2 * m + k, ref.at[source], ref.at[source], device).wait_recv()
    for m, device in enumerate(ring):
        for k, ref in enumerate(totals):
            summed(base + 2 * m + k, ref.at[plane], ref.at[plane], device).wait_send()
    down_total, up_total = w.plane_down[0], w.plane_up[0]
    for m in range(1, planes):
        down_total = down_total + w.plane_down[m]
        up_total = up_total + w.plane_up[m]
    up_out[...] = up_total
    down_out[...] = down_total

    @pl.when(section == 0)
    def _():
        through_beyond().wait_recv()
        rows_relay(1, 0, in_grads, ends[0]).start()
        relay_rows(1, 2, w.dh_v, in_grads, ends[2])
        through_corner(w.dh_v).wait_send()
        for n in (1, 2):
            rows_far(1, n, w.dh_v, in_grads, ends[n]).wait_send()
        for i, part in enumerate(pieces):
            hop(0, i, w.hop_v.at[part], w.recv_v.at[part]).wait_send()
        for k in (1, 2, 3):
            context_to(k).wait_send()
        gather.sent(0)

    @pl.when(section == 1)
    def _():
        through_beyond().wait_send()
        for n, end in enumerate(ends):
            rows_far(1, n, w.dh_v, in_grads, end).wait_send()
        for i, part in enumerate(pieces):
            hop(1, i, w.dh_v.at[part], w.back_v.at[part]).wait_send()
        gather.sent(1)

    for i, part in enumerate(pieces):
        rows_far(0, i, w.layer_v, layer_outs, part).wait_send()
        gathered(0, i, w.layer_v, layer_outs, part)
    for n, end in enumerate(ends):
        gathered(1, n, w.dh_v, in_grads, end)


def local(
    embedded,
    segment,
    query_key_value_weight,
    attention_output_weight,
    feedforward_up_weight,
    feedforward_down_weight,
    adapter_down_weight,
    adapter_up_weight,
    layer_norm_gain,
    layer_norm_bias,
    cotangent,
):
    slots, packs, planes = lax.axis_size("tensor"), segment.shape[0], lax.axis_size("dp")
    assert slots == 4 and packs == slots and planes % 2 == 0
    rows, width = segment.shape[1], embedded.shape[1]
    piece = query_key_value_weight.shape[3]
    wide = feedforward_up_weight.shape[2]
    assert wide == width
    rank = adapter_down_weight.shape[3]
    span = 256
    groups = width // span
    heads = width // HEAD_DIM

    def arr(shape, dtype):
        return jax.ShapeDtypeStruct(shape, dtype)

    low_rows = pltpu.VMEM((rows, width), BF16)
    full_rows = pltpu.VMEM((rows, width), F32)
    of_heads = pltpu.VMEM((groups, rows, span), BF16)
    of_hidden = pltpu.VMEM((slots, rows, wide), BF16)
    down_part = (2, rank, width)
    up_part = (2, rank, piece)
    sums = 2 * (slots - 1) + 2 * (planes - 1)
    scratch = dict(
        qkv_v=pltpu.VMEM((3, width, width), BF16),
        out_v=pltpu.VMEM((width, width), BF16),
        ff_v=pltpu.VMEM((2, slots, width, wide), BF16),
        adapt_v=pltpu.VMEM((width, 2 * rank), BF16),
        adapt_own=pltpu.VMEM((piece, 2 * rank), BF16),
        q_own=pltpu.VMEM((rows, piece), BF16),
        ctx_out=pltpu.VMEM((slots, rows, piece), BF16),
        ctx_in=pltpu.VMEM((slots, rows, piece), BF16),
        inv_v=pltpu.VMEM((groups, rows, span), F32),
        p_v=pltpu.VMEM((heads, rows, rows), BF16),
        s1_v=pltpu.VMEM((rows, 1), F32),
        s2_v=pltpu.VMEM((rows, 1), F32),
        bias=pltpu.VMEM((rows, rows), F32),
        mid_t=pltpu.VMEM((2 * rank, rows), BF16),
        dmid_v=pltpu.VMEM((rows, 2 * rank), BF16),
        grad_down=pltpu.VMEM(down_part, F32),
        grad_up=pltpu.VMEM((slots, *up_part), F32),
        from_down=pltpu.VMEM((slots, *down_part), F32),
        from_up=pltpu.VMEM((slots - 1, *up_part), F32),
        plane_down=pltpu.VMEM((planes, *down_part), F32),
        plane_up=pltpu.VMEM((planes, *up_part), F32),
        local=pltpu.SemaphoreType.DMA((15,)),
        packs=pltpu.SemaphoreType.DMA((packs,)),
        send=pltpu.SemaphoreType.DMA((11, Gather.items)),
        recv=pltpu.SemaphoreType.DMA((11, Gather.items)),
        ctx_send=pltpu.SemaphoreType.DMA((slots,)),
        ctx_recv=pltpu.SemaphoreType.DMA((slots,)),
        hop_send=pltpu.SemaphoreType.DMA((2, rows // 128)),
        hop_recv=pltpu.SemaphoreType.DMA((2, rows // 128)),
        row_send=pltpu.SemaphoreType.DMA((2, 3, rows // 128)),
        row_recv=pltpu.SemaphoreType.DMA((2, 3, rows // 128)),
        sum_send=pltpu.SemaphoreType.DMA((sums,)),
        sum_recv=pltpu.SemaphoreType.DMA((sums,)),
    )
    scratch |= dict.fromkeys(("h_v", "recv_v", "back_v", "cot_v", "low_v"), low_rows)
    scratch |= dict.fromkeys(("hop_v", "layer_v", "dh_v"), low_rows)
    scratch |= dict.fromkeys(("acc", "n1_v", "n2_v"), full_rows)
    scratch |= dict.fromkeys(("q_v", "k_v", "v_v", "ctx_v"), of_heads)
    scratch |= dict.fromkeys(("dq_v", "dk_v", "dv_v", "dctx_v"), of_heads)
    scratch |= dict.fromkeys(("act_v", "slope_v"), of_hidden)
    layer_outs, in_grads, grad_a, grad_b = pl.pallas_call(
        partial(whole_kernel, planes, tuple(scratch)),
        name="encoder_layers",
        out_shape=[
            pltpu.VMEM((packs * rows, width), BF16),
            pltpu.VMEM((packs * rows, width), BF16),
            arr(down_part, F32),
            arr(up_part, F32),
        ],
        in_specs=[ANY] + [VMEM] * 5 + [ANY] * 5,
        out_specs=[VMEM] * 4,
        scratch_shapes=list(scratch.values()),
        compiler_params=pltpu.CompilerParams(
            vmem_limit_bytes=VMEM_LIMIT, collective_id=0, has_side_effects=True
        ),
        cost_estimate=pl.CostEstimate(
            flops=7 * 10**10, bytes_accessed=3 * 10**7, transcendentals=0
        ),
    )(
        embedded,
        segment,
        layer_norm_gain[0],
        layer_norm_bias[0],
        jnp.swapaxes(adapter_down_weight[0], 1, 2).reshape(2 * rank, width),
        adapter_up_weight[0].reshape(2 * rank, piece),
        jnp.swapaxes(query_key_value_weight[0], 1, 2),
        attention_output_weight[0],
        feedforward_up_weight[0],
        feedforward_down_weight[0],
        cotangent,
    )
    grad_a = jnp.swapaxes(grad_a, 1, 2)
    return (layer_outs[None], in_grads[None], grad_a[None], grad_b[None])


def solution(mesh):
    in_specs = (
        P("dp", None),
        P("dp", None),
        P("section", None, None, "tensor"),
        P("section", "tensor", None),
        P("section", None, "tensor"),
        P("section", "tensor", None),
        P("section", None, None, None),
        P("section", None, None, "tensor"),
        P("section", None, None),
        P("section", None, None),
        P("dp", None),
    )
    out_specs = (
        P("section", "dp", None),
        P("section", "dp", None),
        P("section", None, None, None),
        P("section", None, None, "tensor"),
    )
    return jax.shard_map(local, mesh=mesh, in_specs=in_specs, out_specs=out_specs, check_vma=False)
```
